128 devices in a mesh: dp: 32 (over y, z, core), section: 4 (over x).
Axes of the slice: x: 4, y: 4, z: 4, core: 2. Of those that a mesh axis runs over, the one named last changes fastest.
Arguments:
- latents_in: bfloat16 [96, 128, 768], P('dp', 'section'), may hold values from -6 to 6
- raw_inputs: bfloat16 [96, 512, 768], P('dp', 'section'), may hold values from -6 to 6
- cotangent: bfloat16 [96, 128, 768], P('dp', 'section'), may hold values from -6 to 6
- clip_lengths: int32 [96, 4], P('dp'), may hold values from 1 to 448, 512 in all within a row
- latent_clip: int32 [96, 128], P('dp'), may hold values from 0 to 3, never falling along the last dimension, each value on 1 to 64 neighbouring positions
- entry_w: bfloat16 [4, 768, 3072], P('section'), may hold values from -4 to 4
- down_halves: bfloat16 [4, 1536, 768], P('section'), may hold values from -0.109375 to 0.109375
- section_norm: bfloat16 [4, 2, 768], P('section'), may hold values from -1 to 1
- input_norm: bfloat16 [2, 768], P(None, 'section'), may hold values from -1 to 1
Outputs:
- out_latents: bfloat16 [96, 128, 768], P('dp', 'section')
- latent_grad: float32 [96, 128, 768], P('dp', 'section')
- input_grad: float32 [96, 512, 768], P('dp', 'section')
- entry_grad: float32 [4, 768, 3072], P('section')
- down_grad: float32 [4, 1536, 768], P('section')
- norm_grad: float32 [4, 2, 768], P('section')
- input_norm_grad: float32 [2, 768], P(None, 'section')
The draws below stay inside these ranges and needn't reach their ends.
Inputs may be any that keep to these rules, and one draw needn't show every extreme that they name: `clip_lengths`: each item's 4 clip lengths sum to 512; the longest clip of every item has exactly 448 tokens. `latent_clip`: within an item the clip numbers of the latents never fall; every clip has 1 to 64 latents and one clip exactly 64.
All inputs are finite; a program needn't handle non-finite values.
Results may differ from the reference program's by a relative error of at most 0.025.
Values may be sent and summed in bfloat16 or wider, within the bound.
A program may use at most 448 MiB of HBM per device.

```python
import math
import jax
import jax.numpy as jnp
import numpy as np
from jax import lax

D = 768
FF = 3072
HEADS = 12
HEAD_DIM = 64
LAT = 128
CLIPS = 4
SEQ_DEV = 128
SEQ = 512
ITEMS = 96
N_SECTION = 4


def draw_entry_w(key, part):
    key = jax.random.fold_in(key, 17)
    standard = jax.random.truncated_normal(key, -4.0, 4.0, (4, D, FF), jnp.float32)
    section_ids = lax.broadcasted_iota(jnp.int32, (4, 1, FF), 0)
    columns = lax.broadcasted_iota(jnp.int32, (4, 1, FF), 2)
    enlarge = jnp.where(section_ids == 0, 8.0, 4.0)
    factor = jnp.where((columns >= 3 * D) & (section_ids % 2 == 0), enlarge, 1.0)
    return (standard * factor * D ** (-0.5)).astype(jnp.bfloat16)


def shard_levels(rng, extent, shards, low, high):
    level, own = 1.0, jax.random.fold_in(rng, 6)
    for axis_at, parts in shards:
        draws = jnp.exp(jax.random.uniform(jax.random.fold_in(own, axis_at), (parts,), jnp.float32, low / len(shards), high / len(shards)))
        level = level * jnp.repeat(draws, extent[axis_at] // parts).reshape([-1 if axis == axis_at else 1 for axis in range(len(extent))])
    return level


def profile(count, total, most, lean):
    portions = [(1 << 20) // math.isqrt(rank ** lean) + 1 for rank in range(2, count + 1)]
    rest, holding = total - most - (count - 1), [1] * (count - 1)
    while rest > 0:
        free = [i for i in range(count - 1) if holding[i] < most]
        pool, budget = sum([portions[i] for i in free]), rest
        for i in free:
            more = min(most - holding[i], max(1, budget * portions[i] // pool), rest)
            holding[i] = holding[i] + more
            rest = rest - more
    return np.array([most] + holding)


def uneven_parts(own_key, amount, total, reach, lean):
    if amount == 2:
        one = jax.random.randint(own_key, (), max(1, total - reach), min(reach, total - 1) + 1)
        return jnp.stack([one, total - one])
    tallies = jnp.asarray(profile(amount, total, reach, lean), jnp.int32)
    pairs = (amount - 1) // 2
    source_of, sink = tallies[1:1 + 2 * pairs:2], tallies[2:2 + 2 * pairs:2]
    room = jnp.minimum(source_of - 1, reach - sink)
    passed = jax.random.randint(jax.random.fold_in(own_key, 1), (pairs,), 0, 1 << 20) % (room + 1)
    tallies = tallies.at[1:1 + 2 * pairs:2].set(source_of - passed).at[2:2 + 2 * pairs:2].set(sink + passed)
    return tallies[jax.random.permutation(jax.random.fold_in(own_key, 2), amount)]


def noise(key, shape, deviation, bound, split=(), kind=jnp.bfloat16):
    gain = shard_levels(key, shape, split, -0.22, 0.18) if split else 1.0
    drawn = jax.random.normal(key, shape, jnp.float32) * deviation * gain
    return jnp.minimum(jnp.maximum(drawn, -bound), bound).astype(kind)


def setup_inputs(seed: int = 0) -> dict:
    splits = jax.random.split(jax.random.key(seed), 10)
    return {
        "latents_in": noise(splits[0], (ITEMS, LAT, D), 1.0, 6.0, ((0, 32), (1, 4))),
        "raw_inputs": noise(splits[1], (ITEMS, SEQ, D), 1.0, 6.0, ((0, 32), (1, 4))),
        "cotangent": noise(splits[2], (ITEMS, LAT, D), 1.0, 6.0, ((0, 32), (1, 4))),
        "clip_lengths": jax.vmap(lambda own: uneven_parts(own, CLIPS, SEQ, SEQ - SEQ_DEV // 2, 1))(jax.random.split(splits[3], ITEMS)).reshape((ITEMS, CLIPS)).astype(jnp.int32),
        "latent_clip": jax.vmap(lambda own: jnp.searchsorted(jnp.cumsum(uneven_parts(own, CLIPS, LAT, LAT // 2, 1)), jnp.arange(LAT), side="right"))(jax.random.split(splits[4], ITEMS)).reshape((ITEMS, LAT)).astype(jnp.int32),
        "entry_w": draw_entry_w(jax.random.fold_in(splits[9], 71), 0),
        "down_halves": noise(splits[6], (N_SECTION, FF // 2, D), FF ** -0.5, 0.109375, ((0, 4),)),
        "section_norm": noise(splits[7], (N_SECTION, 2, D), 0.2, 1.0, ((0, 4),)),
        "input_norm": noise(splits[8], (2, D), 0.2, 1.0, ((1, 4),)),
    }


@jax.custom_vjp
def low(v):
    return lax.optimization_barrier(v.astype(jnp.bfloat16)).astype(jnp.float32)

@jax.custom_vjp
def low_back(v):
    return v

def low_keep(v):
    return (low(v), None)

def low_pass(kept, grad):
    return (grad,)

def back_keep(v):
    return (v, None)

def back_low(kept, grad):
    return (low(grad),)
low.defvjp(low_keep, low_pass)
low_back.defvjp(back_keep, back_low)
NORM_EPS = 1e-05
NEG_FILL = -1000000000.0
exact_mode = lax.Precision.HIGHEST

def product(first_operand, second_operand):
    return jnp.dot(first_operand, second_operand, precision=exact_mode)

def normed(values, affine):
    center = lax.optimization_barrier(jnp.mean(values, -1, keepdims=True))
    centred = values - center
    variance = lax.optimization_barrier(jnp.mean(centred * centred, -1, keepdims=True))
    return centred * lax.rsqrt(variance + NORM_EPS) * (1.0 + affine[0]) + affine[1]

def split_heads(values):
    return values.reshape(values.shape[0], HEADS, HEAD_DIM)

def attend(query_rows, key_rows, value_rows, key_mask):
    scores = jnp.einsum('qhd,khd->hqk', split_heads(query_rows), split_heads(key_rows), precision=exact_mode) * HEAD_DIM ** (-0.5)
    scores = low_back(jnp.where(key_mask[None], scores, NEG_FILL))
    exponent = jnp.exp(scores - lax.optimization_barrier(jnp.max(scores, -1, keepdims=True)))
    soft_probs = low(exponent / lax.optimization_barrier(jnp.sum(exponent, -1, keepdims=True)))
    mixed = jnp.einsum('hqk,khd->qhd', soft_probs, split_heads(value_rows), precision=exact_mode)
    return low_back(low(mixed.reshape(query_rows.shape[0], HEADS * HEAD_DIM)))

def cross_block(latent_state, raw_rows, weights, affine, input_affine, key_mask):
    normed_low = low(normed(latent_state, affine))
    input_low = low(normed(raw_rows, input_affine))
    query_rows = low_back(low(product(normed_low, weights[:, :D])))
    pair_rows = low_back(low(product(input_low, weights[:, D:3 * D])))
    mixed = attend(query_rows, pair_rows[:, :D], pair_rows[:, D:], key_mask)
    return latent_state + product(mixed, weights[:, 3 * D:])

def self_block(latent_state, weights, affine, key_mask):
    normed_low = low(normed(latent_state, affine))
    triple_rows = low_back(low(product(normed_low, weights[:, :3 * D])))
    mixed = attend(triple_rows[:, :D], triple_rows[:, D:2 * D], triple_rows[:, 2 * D:], key_mask)
    return latent_state + product(mixed, weights[:, 3 * D:])

def ffn_block(latent_state, weights, down_matrix, affine):
    normed_low = low(normed(latent_state, affine))
    hidden = low_back(product(normed_low, weights))
    activated = low(jax.nn.gelu(hidden, approximate=False))
    return latent_state + product(activated, down_matrix)

def two_layers(latents, raw_rows, entry, halves, norms, input_affine, cross_mask, self_mask):
    latent_state = cross_block(latents, raw_rows, entry[0], norms[0], input_affine, cross_mask)
    latent_state = low_back(low(latent_state))
    latent_state = ffn_block(latent_state, entry[1], jnp.concatenate([halves[0], halves[1]], 0), norms[1])
    latent_state = low_back(low(latent_state))
    latent_state = self_block(latent_state, entry[2], norms[2], self_mask)
    latent_state = low_back(low(latent_state))
    return ffn_block(latent_state, entry[3], jnp.concatenate([halves[2], halves[3]], 0), norms[3])

def reference(latents_in, raw_inputs, cotangent, clip_lengths, latent_clip, entry_w, down_halves, section_norm, input_norm):
    entry = entry_w.astype(jnp.float32)
    halves = down_halves.astype(jnp.float32)
    norms = section_norm.astype(jnp.float32)
    input_affine = input_norm.astype(jnp.float32)
    positions = jnp.arange(SEQ, dtype=jnp.int32)

    def per_item(totals, item_slices):
        latents, raw_rows, grad_rows, lengths, clip_ids = item_slices
        clip_ends = jnp.cumsum(lengths).astype(jnp.int32)
        token_clip = lax.optimization_barrier(jnp.sum((positions[:, None] >= clip_ends[None, :]).astype(jnp.int32), axis=1)).astype(jnp.int32)
        cross_mask = clip_ids[:, None] == token_clip[None, :]
        self_mask = clip_ids[:, None] == clip_ids[None, :]

        def forward(latent_arg, raw_arg, entry_arg, halves_arg, norms_arg, input_arg):
            return two_layers(latent_arg, raw_arg, entry_arg, halves_arg, norms_arg, input_arg, cross_mask, self_mask)
        result, pullback = jax.vjp(forward, latents.astype(jnp.float32), raw_rows.astype(jnp.float32), entry, halves, norms, input_affine)
        gradients = pullback(grad_rows.astype(jnp.float32))
        totals = (totals[0] + gradients[2], totals[1] + gradients[3], totals[2] + gradients[4], totals[3] + gradients[5])
        return (totals, (result.astype(jnp.bfloat16), gradients[0], gradients[1]))
    start = (jnp.zeros_like(entry), jnp.zeros_like(halves), jnp.zeros_like(norms), jnp.zeros_like(input_affine))
    totals, stacked = lax.scan(per_item, start, (latents_in, raw_inputs, cotangent, clip_lengths, latent_clip))
    return (stacked[0], stacked[1], stacked[2], totals[0], totals[1], totals[2], totals[3])
```

```python
import functools
import math

import jax
import jax.numpy as jnp
from jax import lax
from jax.experimental import pallas as pl
from jax.experimental.pallas import tpu as pltpu
from jax.sharding import PartitionSpec as P


D = 768
LAT = 128
SEQ = 512
EPS = 1e-5
NEG = -1e9
F32 = jnp.float32
BF = jnp.bfloat16


def nn(a, b):
    return jnp.dot(a, b, preferred_element_type=F32)


def nt(a, b):
    return lax.dot_general(a, b, (((1,), (1,)), ((), ())), preferred_element_type=F32)


def tn(a, b):
    return lax.dot_general(a, b, (((0,), (0,)), ((), ())), preferred_element_type=F32)


def unit(x):
    mean = jnp.mean(x, -1, keepdims=True)
    cen = x - mean
    var = jnp.mean(cen * cen, -1, keepdims=True)
    rstd = lax.rsqrt(var + EPS)
    return cen * rstd, rstd


def ln_back(x, da, gain):
    xhat, rstd = unit(x)
    dx = da * gain
    m1 = jnp.mean(dx, -1, keepdims=True)
    m2 = jnp.mean(dx * xhat, -1, keepdims=True)
    grad = rstd * (dx - m1 - xhat * m2)
    return grad, jnp.sum(da * xhat, 0, keepdims=True), jnp.sum(da, 0, keepdims=True)


def gelu_pair(z):
    a = jnp.abs(z)
    t = 1.0 / (1.0 + (0.3275911 * 0.7071067811865476) * a)
    e = jnp.exp(-0.5 * (z * z))
    p = t * (0.254829592 + t * (-0.284496736 + t * (1.421413741 + t * (-1.453152027 + t * 1.061405429))))
    half = (0.5 * p) * e
    cdf = jnp.where(z >= 0, 1.0 - half, half)
    return z * cdf, cdf + z * (0.3989422804014327 * e)


def rows(i, n):
    return pl.ds(pl.multiple_of(i * n, n), n)


def ffn_fwd(i, xin, gain, shift, W, Fd, A, X):
    x = xin[i].astype(F32)
    xhat, _ = unit(x)
    a = (xhat * gain + shift).astype(BF)
    A[rows(i, LAT)] = a
    total = x
    for c in range(4):
        gate, slope = gelu_pair(nn(a, W[:, c * D:(c + 1) * D]))
        gate = gate.astype(BF)
        where_ = pl.ds(pl.multiple_of(c * 384 + i * LAT, LAT), LAT)
        X[0, where_] = gate
        X[2, where_] = slope.astype(BF)
        total = total + nn(gate, Fd[c // 2, (c % 2) * D:(c % 2 + 1) * D])
    return total


def ffn_bwd(i, db, W, Fd, X):
    da = None
    for c in range(4):
        dg = nt(db, Fd[c // 2, (c % 2) * D:(c % 2 + 1) * D])
        where_ = pl.ds(pl.multiple_of(c * 384 + i * LAT, LAT), LAT)
        dz = (X[2, where_].astype(F32) * dg).astype(BF)
        X[1, where_] = dz
        part = nt(dz, W[:, c * D:(c + 1) * D])
        da = part if da is None else da + part
    return da


def halves(m):
    lane = lax.broadcasted_iota(jnp.int32, m.shape, 1)
    zero = jnp.zeros_like(m)
    return jnp.concatenate([jnp.where(lane < 64, m, zero), jnp.where(lane >= 64, m, zero)], 0)


def unhalves(mt):
    q = mt.shape[1] // 2
    return jnp.concatenate([mt[0:64, 0:q], mt[64:128, q:2 * q]], 0).T


def attn_fwd(q, k, v, maskf, PT, O):
    for p in range(6):
        cols = slice(p * 128, (p + 1) * 128)
        qs = halves(q[:, cols])
        s = nt(k[:, cols], qs) * 0.125
        s = jnp.where(maskf, s, NEG)
        m = jnp.max(s, 0, keepdims=True)
        e = jnp.exp(s - m)
        l = jnp.sum(e, 0, keepdims=True)
        pt = (e * (1.0 / l)).astype(BF)
        PT[p] = pt
        ot = tn(v[:, cols], pt)
        O[:, cols] = unhalves(ot).astype(BF)


def attn_bwd(q, k, v, PT, do, dq, dk, dv):
    for p in range(6):
        cols = slice(p * 128, (p + 1) * 128)
        dos = halves(do[:, cols])
        qs = halves(q[:, cols])
        pt = PT[p]
        dp = nt(v[:, cols], dos)
        ptf = pt.astype(F32)
        w = dp * ptf
        delta = jnp.sum(w, 0, keepdims=True)
        ds = (w - ptf * delta).astype(BF)
        dk[:, cols] = (nn(ds, qs) * 0.125).astype(BF)
        dv[:, cols] = nn(pt, dos).astype(BF)
        dqt = tn(k[:, cols], ds)
        dq[:, cols] = (unhalves(dqt) * 0.125).astype(BF)


HALF = 768
MESH = pl.DeviceIdType.MESH


def kernel(
    n,
    lat_ref, raw_ref, cot_ref, len_ref, clip_ref, w_ref, f_ref, snorm_ref, inorm_ref,
    out_ref, lgrad_ref, igrad_ref, g_out, tiny_ref,
    W, Fd, g, X, PT, rA, rB, rC, q, xin, dBin, sendB, sendD, A, Q, O, dQ, dO, rawv, usend, dUb, outb, lgb,
    inb, inr, nacc, tsrc, tX, tC, t1, t2,
    loc, in_s, in_r, lat_s, lat_r, cot_s, cot_r, u_s, u_r, fx_s, fx_r, b_s, b_r, d_s, d_r,
    o_s, o_r, lg_s, lg_r, du_s, du_r, gx_s, gx_r,
    a_s, a_r, bb_s, bb_r, c_s, c_r, gd_s, gd_r, ge_s, ge_r, gf_s, gf_r,
    fd_s, fd_r, fe_s, fe_r, ff_s, ff_r, tx_s, tx_r, tc_s, tc_r, t1_s, t1_r, t2_s, t2_r, g_sem, free_a, free_b,
):
    quarter = HALF // n
    piece = quarter // n
    s = lax.axis_index("section")
    dp = lax.axis_index("dp")
    c = lax.rem(dp, 2)
    z = lax.rem(dp // 2, n)
    y = dp // (2 * n)
    odd = lax.rem(s, 2) == 1
    r1 = y * (1 - c) + z * c
    r2 = z * (1 - c) + y * c
    mate = dp + 1 - 2 * c

    def sec_of(k):
        return lax.rem(s + k, 4)

    def peer1(k):
        other = lax.rem(r1 + k, n)
        return ((other * (1 - c) + y * c) * n + z * (1 - c) + other * c) * 2 + c

    def peer2(k):
        other = lax.rem(r2 + k, n)
        return ((y * (1 - c) + other * c) * n + other * (1 - c) + z * c) * 2 + c

    def at(start, size, unit_size):
        return pl.ds(pl.multiple_of(start, unit_size), size)

    def remote(src, dst, send_sem, recv_sem, dp_to, sec_to):
        return pltpu.make_async_remote_copy(
            src_ref=src, dst_ref=dst, send_sem=send_sem, recv_sem=recv_sem,
            device_id=(dp_to, sec_to), device_id_type=MESH,
        )

    def local_w():
        return pltpu.make_async_copy(w_ref.at[0], W, loc.at[0])

    def local_f():
        return pltpu.make_async_copy(f_ref.at[0], Fd.at[1], loc.at[1])

    def local_raw():
        return pltpu.make_async_copy(raw_ref, rawv, loc.at[2])

    def local_lat():
        return pltpu.make_async_copy(lat_ref, xin.at[:, at(s * 32, 32, 32)], loc.at[3])

    def local_cot():
        return pltpu.make_async_copy(cot_ref, dBin.at[:, at(s * 32, 32, 32)], loc.at[4])

    def cp_in(k):
        return remote(inb, inr.at[k - 1], in_s.at[k - 1], in_r.at[k - 1], dp, sec_of(k))

    def cp_lat(src):
        return remote(lat_ref, xin.at[:, at(src * 32, 32, 32)], lat_s, lat_r.at[src - 1], dp, 0)

    def cp_cot(src):
        return remote(cot_ref, dBin.at[:, at(src * 32, 32, 32)], cot_s, cot_r.at[src], dp, 3)

    def cp_u(i, src):
        return remote(
            usend.at[i], X.at[0, at(i * SEQ + src * 128, 128, 128)],
            u_s.at[i], u_r.at[i, src - 1], dp, 0,
        )

    own_piece = c * HALF + r1 * quarter + r2 * piece

    def cp_fx():
        return remote(
            f_ref.at[0, at(own_piece, piece, piece)], Fd.at[0, at(own_piece, piece, piece)],
            fx_s, fx_r, dp, jnp.minimum(s + 1, 3),
        )

    def cp_b(i):
        return remote(sendB.at[i], xin.at[i], b_s.at[i], b_r.at[i], dp, jnp.minimum(s + 1, 3))

    def cp_d(i):
        return remote(sendD.at[i], dBin.at[i], d_s.at[i], d_r.at[i], dp, jnp.maximum(s - 1, 0))

    def cp_o(i, t):
        return remote(sendB.at[i, t * 32:(t + 1) * 32], outb.at[i], o_s.at[i, t], o_r.at[i], dp, t)

    def cp_lg(i, t):
        return remote(sendD.at[i, t * 32:(t + 1) * 32], lgb.at[i], lg_s.at[i, t - 1], lg_r.at[i], dp, t)

    def cp_du(i, t):
        return remote(
            X.at[5, at(i * SEQ + t * 128, 128, 128)], dUb.at[i],
            du_s.at[i, t - 1], du_r.at[i], dp, t,
        )

    def cp_gx():
        return remote(
            q.at[3, at(r2 * piece, piece, piece)], q.at[2, at(r2 * piece, piece, piece)],
            gx_s, gx_r, dp, jnp.maximum(s - 1, 0),
        )

    def cp_a(b):
        return remote(g.at[b, at((1 - c) * HALF, HALF, HALF)], rA.at[b], a_s.at[b], a_r.at[b], mate, s)

    def cp_rb(b, k):
        start = c * HALF + lax.rem(r1 + k, n) * quarter
        return remote(
            g.at[b, at(start, quarter, quarter)], rB.at[b, k - 1],
            bb_s.at[b, k - 1], bb_r.at[b, k - 1], peer1(k), s,
        )

    def cp_rc(b, k):
        start = c * HALF + r1 * quarter + lax.rem(r2 + k, n) * piece
        return remote(
            g.at[b, at(start, piece, piece)], rC.at[b, k - 1],
            c_s.at[b, k - 1], c_r.at[b, k - 1], peer2(k), s,
        )

    def ag_d(ref, start, ss, rs, k):
        where_ = at(start + r2 * piece, piece, piece)
        return remote(ref.at[where_], ref.at[where_], ss.at[k - 1], rs.at[k - 1], peer2(k), s)

    def ag_d_in(ref, start, ss, rs, k):
        where_ = at(start + lax.rem(r2 + n - k, n) * piece, piece, piece)
        return remote(ref.at[where_], ref.at[where_], ss.at[k - 1], rs.at[k - 1], peer2(k), s)

    own_quarter = c * HALF + r1 * quarter

    def ag_e(src, ref, ss, rs, k):
        where_ = at(own_quarter, quarter, quarter)
        return remote(src, ref.at[where_], ss.at[k - 1], rs.at[k - 1], peer1(k), s)

    def ag_e_in(src, ref, ss, rs, k):
        where_ = at(c * HALF + lax.rem(r1 + n - k, n) * quarter, quarter, quarter)
        return remote(src, ref.at[where_], ss.at[k - 1], rs.at[k - 1], peer1(k), s)

    def ag_f(ref, ss, rs):
        where_ = at(c * HALF, HALF, HALF)
        return remote(ref.at[where_], ref.at[where_], ss, rs, mate, s)

    def ag_f_in(ref, ss, rs):
        where_ = at((1 - c) * HALF, HALF, HALF)
        return remote(ref.at[where_], ref.at[where_], ss, rs, mate, s)

    ring = range(1, n)

    local_raw().start()
    local_w().start()
    local_f().start()

    barrier = pltpu.get_barrier_semaphore()
    partners = [(dp, sec_of(k)) for k in (1, 2, 3)] + [(mate, s)]
    partners += [(peer1(k), s) for k in ring] + [(peer2(k), s) for k in ring]
    for partner in partners:
        pl.semaphore_signal(barrier, inc=1, device_id=partner, device_id_type=MESH)
    select = lax.broadcasted_iota(jnp.int32, (192, D), 1) == lax.broadcasted_iota(jnp.int32, (192, D), 0) + s * 192
    inb[...] = jnp.zeros_like(inb)
    inb[0:2] = nn(inorm_ref[...], select.astype(F32).astype(BF))
    nacc[...] = jnp.zeros_like(nacc)
    pl.semaphore_wait(barrier, len(partners))

    for k in (1, 2, 3):
        cp_in(k).start()

    @pl.when(s == 0)
    def _():
        local_lat().start()

    @pl.when(s != 0)
    def _():
        cp_lat(s).start()

    @pl.when(jnp.logical_not(odd))
    def _():
        cp_fx().start()

    for k in (1, 2, 3):
        cp_in(k).wait_recv()
    inb_all = inb[...] + inr[0] + inr[1] + inr[2]
    in_gain = 1.0 + inb_all[0:1]
    in_shift = inb_all[1:2]
    local_raw().wait()

    @pl.loop(0, 3)
    def _(i):
        xhat, _ = unit(rawv[i].astype(F32))
        u = (xhat * in_gain + in_shift).astype(BF)

        @pl.when(s == 0)
        def _():
            X[0, at(i * SEQ, 128, 128)] = u

        @pl.when(s != 0)
        def _():
            usend[i] = u
            cp_u(i, s).start()

    @pl.when(s == 3)
    def _():
        local_cot().start()

    @pl.when(s != 3)
    def _():
        cp_cot(s).start()

    snorm = snorm_ref[0].astype(F32)
    gain = 1.0 + snorm[0:1]
    shift = snorm[1:2]

    def project(a, lo, hi):
        return nn(a, W[:, lo:hi])

    def latent_back(i, da, db):
        dx, dg, dbias = ln_back(xin[i].astype(F32), da, gain)
        nacc[0:1] = nacc[0:1] + dg
        nacc[1:2] = nacc[1:2] + dbias
        return db.astype(F32) + dx

    local_w().wait()

    @pl.when(s == 0)
    def _():
        local_lat().wait()
        for src in (1, 2, 3):
            cp_lat(src).wait_recv()

        @pl.loop(0, 3)
        def _(i):
            xhat, _ = unit(xin[i].astype(F32))
            A[rows(i, LAT)] = (xhat * gain + shift).astype(BF)
        Q[...] = project(A[...], 0, D).astype(BF)

        @pl.loop(0, 3)
        def _(i):
            for src in (1, 2, 3):
                cp_u(i, src).wait_recv()
            u = X[0, rows(i, SEQ)]
            kv = [X.at[j, rows(i, SEQ)] for j in (1, 2)]
            kv[0][...] = project(u, D, 2 * D).astype(BF)
            kv[1][...] = project(u, 2 * D, 3 * D).astype(BF)
            where_ = lax.broadcasted_iota(jnp.int32, (SEQ, 256), 0)
            clip = jnp.zeros((SEQ, 256), jnp.int32)
            end = jnp.int32(0)
            for j in range(4):
                end = end + len_ref[i, j]
                clip = clip + (where_ >= end).astype(jnp.int32)
            ids = jnp.concatenate([clip_ref[i], clip_ref[i]], 1)
            attn_fwd(Q.at[rows(i, LAT)], kv[0], kv[1], clip == ids, PT.at[i], O.at[rows(i, LAT)])
            b = xin[i].astype(F32) + project(O[rows(i, LAT)], 3 * D, 4 * D)
            sendB[i] = b.astype(BF)
            cp_b(i).start()

        @pl.loop(0, 3)
        def _(i):
            cp_d(i).wait_recv()
            db = dBin[i]
            dO[...] = nt(db, W[:, 3 * D:]).astype(BF)
            kv = [X.at[j, rows(i, SEQ)] for j in (1, 2, 3, 4)]
            lat_rows = rows(i, LAT)
            attn_bwd(Q.at[lat_rows], kv[0], kv[1], PT.at[i], dO, dQ.at[lat_rows], kv[2], kv[3])
            grad = latent_back(i, nt(dQ[lat_rows], W[:, :D]), db).astype(BF)
            sendD[i] = grad
            lgb[i] = grad[0:32]
            for t in (1, 2, 3):
                cp_lg(i, t).start()

        everything = [X.at[j] for j in range(5)]
        g[0, 0:D] = tn(A[...], dQ[...]).astype(BF)
        g[0, D:] = tn(everything[0][...], everything[3][...]).astype(BF)
        cp_a(0).start()
        g[1, 0:D] = tn(everything[0][...], everything[4][...]).astype(BF)
        g[1, D:] = tn(O[...], dBin[...].reshape(3 * LAT, D)).astype(BF)
        cp_a(1).start()

        @pl.loop(0, 3)
        def _(i):
            at_rows = rows(i, SEQ)
            du = nt(X[3, at_rows], W[:, D:2 * D]) + nt(X[4, at_rows], W[:, 2 * D:3 * D])
            X[5, at_rows] = du.astype(BF)
            dUb[i] = X[5, at(i * SEQ, 128, 128)]
            for t in (1, 2, 3):
                cp_du(i, t).start()

    @pl.when(s == 2)
    def _():
        @pl.loop(0, 3)
        def _(i):
            lat_rows = rows(i, LAT)
            cp_b(i).wait_recv()
            x = xin[i].astype(F32)
            xhat, _ = unit(x)
            a = (xhat * gain + shift).astype(BF)
            A[lat_rows] = a
            Q[lat_rows] = project(a, 0, D).astype(BF)
            X[1, lat_rows] = project(a, D, 2 * D).astype(BF)
            X[2, lat_rows] = project(a, 2 * D, 3 * D).astype(BF)
            ids = jnp.broadcast_to(clip_ref[i].astype(F32), (LAT, LAT))
            mask = jnp.concatenate([ids, ids], 1) == jnp.concatenate([ids.T, ids.T], 1)
            attn_fwd(
                Q.at[lat_rows], X.at[1, lat_rows], X.at[2, lat_rows], mask,
                PT.at[i, :, 0:LAT], O.at[lat_rows],
            )
            b = x + project(O[lat_rows], 3 * D, 4 * D)
            sendB[i] = b.astype(BF)
            cp_b(i).start()

        @pl.loop(0, 3)
        def _(i):
            lat_rows = rows(i, LAT)
            cp_d(i).wait_recv()
            db = dBin[i]
            dO[...] = nt(db, W[:, 3 * D:]).astype(BF)
            attn_bwd(
                Q.at[lat_rows], X.at[1, lat_rows], X.at[2, lat_rows], PT.at[i, :, 0:LAT],
                dO, dQ.at[lat_rows], X.at[3, lat_rows], X.at[4, lat_rows],
            )
            da = nt(dQ[lat_rows], W[:, :D]) + nt(X[3, lat_rows], W[:, D:2 * D])
            da = da + nt(X[4, lat_rows], W[:, 2 * D:3 * D])
            sendD[i] = latent_back(i, da, db).astype(BF)
            cp_d(i).start()

        a = A[...]
        g[0, 0:D] = tn(a, dQ[...]).astype(BF)
        g[0, D:] = tn(a, X[3, 0:3 * LAT]).astype(BF)
        cp_a(0).start()
        g[1, 0:D] = tn(a, X[4, 0:3 * LAT]).astype(BF)
        g[1, D:] = tn(O[...], dBin[...].reshape(3 * LAT, D)).astype(BF)
        cp_a(1).start()

    @pl.when(odd)
    def _():
        prior = Fd.at[0]
        mine = prior.at[at(own_quarter, quarter, quarter)]
        cp_fx().wait_recv()
        for k in ring:
            ag_d(prior, own_quarter, fd_s, fd_r, k).start()
        for k in ring:
            ag_d_in(prior, own_quarter, fd_s, fd_r, k).wait_recv()
        for k in ring:
            ag_e(mine, prior, fe_s, fe_r, k).start()
        for k in ring:
            ag_e_in(mine, prior, fe_s, fe_r, k).wait_recv()
        ag_f(prior, ff_s, ff_r).start()
        local_f().wait()
        ag_f_in(prior, ff_s, ff_r).wait_recv()

        @pl.when(s == 3)
        def _():
            local_cot().wait()
            for src in (0, 1, 2):
                cp_cot(src).wait_recv()

        @pl.loop(0, 6)
        def _(step):
            last = s == 3
            forward = jnp.where(last, lax.rem(step, 2) == 0, step < 3)
            i = jnp.where(last, step // 2, lax.rem(step, 3))

            @pl.when(forward)
            def _():
                cp_b(i).wait_recv()
                b = ffn_fwd(i, xin, gain, shift, W, Fd, A, X).astype(BF)
                sendB[i] = b

                @pl.when(s == 1)
                def _():
                    cp_b(i).start()

                @pl.when(last)
                def _():
                    outb[i] = b[96:128]
                    for t in (0, 1, 2):
                        cp_o(i, t).start()

            @pl.when(jnp.logical_not(forward))
            def _():
                @pl.when(s == 1)
                def _():
                    cp_d(i).wait_recv()
                db = dBin[i]
                sendD[i] = latent_back(i, ffn_bwd(i, db, W, Fd, X), db).astype(BF)
                cp_d(i).start()

        a = A[...]
        db = dBin[...].reshape(3 * LAT, D)
        for b in (3, 2, 0, 1):
            for j in range(2):
                blk = {3: 0, 2: 2, 0: 0, 1: 2}[b] + j
                here = slice(blk * 384, (blk + 1) * 384)
                grad = tn(X[0, here], db) if b > 1 else tn(a, X[1, here])
                g[b, j * D:(j + 1) * D] = grad.astype(BF)
            cp_a(b).start()

    count = jnp.where(odd, 4, 2)

    def block(t):
        return jnp.where(odd, jnp.where(t < 2, 3 - t, t - 2), t)

    @pl.loop(0, count)
    def _(t):
        b = block(t)
        cp_a(b).wait_recv()
        for j in range(n):
            part = at(c * HALF + j * quarter, quarter, quarter)
            g[b, part] = (g[b, part].astype(F32) + rA[b, j * quarter:(j + 1) * quarter].astype(F32)).astype(BF)
        for k in ring:
            cp_rb(b, k).start()

    @pl.loop(0, count)
    def _(t):
        b = block(t)
        for k in ring:
            cp_rb(b, k).wait_recv()
        part = at(c * HALF + r1 * quarter, quarter, quarter)
        total = g[b, part].astype(F32)
        for k in ring:
            total = total + rB[b, k - 1].astype(F32)
        g[b, part] = total.astype(BF)
        for k in ring:
            cp_rc(b, k).start()

    @pl.loop(0, count)
    def _(t):
        b = block(t)
        cp_a(b).wait_send()
        pl.semaphore_signal(free_a, inc=1, device_id=(mate, s), device_id_type=MESH)
        for k in ring:
            cp_rb(b, k).wait_send()
            pl.semaphore_signal(free_b, inc=1, device_id=(peer1(k), s), device_id_type=MESH)
        for k in ring:
            cp_rc(b, k).wait_recv()
        total = g[b, at(own_piece, piece, piece)].astype(F32)
        for k in ring:
            total = total + rC[b, k - 1].astype(F32)
        q[b, at(r2 * piece, piece, piece)] = total.astype(BF)

        @pl.when(b == 3)
        def _():
            cp_gx().start()

        @pl.when(b < 3)
        def _():
            for k in ring:
                ag_d(q.at[b], 0, gd_s.at[b], gd_r.at[b], k).start()

    @pl.when(jnp.logical_not(odd))
    def _():
        cp_gx().wait_recv()
        for k in ring:
            ag_d(q.at[2], 0, gd_s.at[2], gd_r.at[2], k).start()

    @pl.loop(0, 3)
    def _(i):
        @pl.when(s != 3)
        def _():
            cp_o(i, 0).wait_recv()

        @pl.when(s != 0)
        def _():
            cp_lg(i, 1).wait_recv()
            cp_du(i, 1).wait_recv()
        dx, dg, dbias = ln_back(rawv[i].astype(F32), dUb[i].astype(F32), in_gain)
        igrad_ref[i] = dx
        nacc[2:3] = nacc[2:3] + dg
        nacc[3:4] = nacc[3:4] + dbias
        out_ref[i] = outb[i]
        lgrad_ref[i] = lgb[i].astype(F32)

    def small(step, buf, ss, rs, k, dp_to, sec_to):
        return remote(tsrc.at[step], buf.at[k], ss.at[k], rs.at[k], dp_to, sec_to)

    row = lax.broadcasted_iota(jnp.int32, (8, D), 0)
    own = jnp.where(row < 4, nacc[...], 0.0)
    tsrc[0] = own
    for k in (1, 2, 3):
        small(0, tX, tx_s, tx_r, k - 1, dp, sec_of(k)).start()

    @pl.loop(0, count)
    def _(t):
        for k in ring:
            cp_rc(block(t), k).wait_send()
    pl.semaphore_wait(free_b, count * len(ring))
    for b in range(3):
        for k in ring:
            ag_d_in(q.at[b], 0, gd_s.at[b], gd_r.at[b], k).wait_recv()
        for k in ring:
            ag_e(q.at[b], g.at[b], ge_s.at[b], ge_r.at[b], k).start()
        g[b, at(own_quarter, quarter, quarter)] = q[b]
    pl.semaphore_wait(free_a, count)

    for k in (1, 2, 3):
        small(0, tX, tx_s, tx_r, k - 1, dp, sec_of(k)).wait_recv()
    own = jnp.where(row < 2, own, own + tX[0] + tX[1] + tX[2])
    tsrc[1] = own
    small(1, tC, tc_s, tc_r, 0, mate, s).start()

    for b in range(3):
        for k in ring:
            ag_e_in(q.at[b], g.at[b], ge_s.at[b], ge_r.at[b], k).wait_recv()
        ag_f(g.at[b], gf_s.at[b], gf_r.at[b]).start()
        if b == 0:
            small(1, tC, tc_s, tc_r, 0, mate, s).wait_recv()
            own = own + tC[0]
            tsrc[2] = own
            for k in ring:
                small(2, t1, t1_s, t1_r, k - 1, peer1(k), s).start()
        if b == 1:
            for k in ring:
                small(2, t1, t1_s, t1_r, k - 1, peer1(k), s).wait_recv()
                own = own + t1[k - 1]
            tsrc[3] = own
            for k in ring:
                small(3, t2, t2_s, t2_r, k - 1, peer2(k), s).start()
    for k in ring:
        small(3, t2, t2_s, t2_r, k - 1, peer2(k), s).wait_recv()
        own = own + t2[k - 1]
    tiny_ref[...] = own

    for b in range(3):
        ag_f_in(g.at[b], gf_s.at[b], gf_r.at[b]).wait_recv()
        pltpu.make_async_copy(g.at[b], g_out.at[b], g_sem.at[b]).start()
    for b in range(3):
        pltpu.make_async_copy(g.at[b], g_out.at[b], g_sem.at[b]).wait()

    for k in (1, 2, 3):
        cp_in(k).wait_send()
        small(0, tX, tx_s, tx_r, k - 1, dp, sec_of(k)).wait_send()
    small(1, tC, tc_s, tc_r, 0, mate, s).wait_send()
    for k in ring:
        small(2, t1, t1_s, t1_r, k - 1, peer1(k), s).wait_send()
        small(3, t2, t2_s, t2_r, k - 1, peer2(k), s).wait_send()

    @pl.when(s == 0)
    def _():
        @pl.loop(0, 3)
        def _(i):
            for t in (1, 2, 3):
                cp_lg(i, t).wait_send()
                cp_du(i, t).wait_send()

    @pl.when(s != 0)
    def _():
        cp_lat(s).wait_send()

        @pl.loop(0, 3)
        def _(i):
            cp_u(i, s).wait_send()
            cp_d(i).wait_send()

    @pl.when(s == 3)
    def _():
        @pl.loop(0, 3)
        def _(i):
            for t in (0, 1, 2):
                cp_o(i, t).wait_send()

    @pl.when(s != 3)
    def _():
        cp_cot(s).wait_send()

        @pl.loop(0, 3)
        def _(i):
            cp_b(i).wait_send()

    @pl.when(odd)
    def _():
        for k in ring:
            mine = Fd.at[0, at(own_quarter, quarter, quarter)]
            ag_d(Fd.at[0], own_quarter, fd_s, fd_r, k).wait_send()
            ag_e(mine, Fd.at[0], fe_s, fe_r, k).wait_send()
        ag_f(Fd.at[0], ff_s, ff_r).wait_send()
        cp_gx().wait_send()

    @pl.when(jnp.logical_not(odd))
    def _():
        cp_fx().wait_send()
        local_f().wait()

    for b in range(3):
        for k in ring:
            ag_d(q.at[b], 0, gd_s.at[b], gd_r.at[b], k).wait_send()
            ag_e(q.at[b], g.at[b], ge_s.at[b], ge_r.at[b], k).wait_send()
        ag_f(g.at[b], gf_s.at[b], gf_r.at[b]).wait_send()


def on_device(lat, raw, cot, lengths, clip, w, f, snorm, inorm):
    n = math.isqrt(lax.axis_size("dp") // 2)
    quarter = HALF // n
    piece = quarter // n
    ring = max(n - 1, 1)

    def low(*shape):
        return pltpu.VMEM(shape, BF)

    def full(*shape):
        return pltpu.VMEM(shape, F32)

    def sem(*shape):
        return pltpu.SemaphoreType.DMA(shape)

    one = pltpu.SemaphoreType.DMA
    scratch = [
        low(D, 4 * D), low(2, 2 * D, D), low(4, 2 * D, D), low(6, 2 * D, D), low(3, 6, SEQ, 256),
        low(4, HALF, D), low(4, ring, quarter, D), low(4, ring, piece, D), low(4, quarter, D),
        low(3, LAT, D), low(3, LAT, D), low(3, LAT, D), low(3, LAT, D),
        low(3 * LAT, D), low(3 * LAT, D), low(3 * LAT, D), low(3 * LAT, D), low(LAT, D),
        low(3, LAT, D), low(3, LAT, D), low(3, LAT, D), low(3, 32, D), low(3, 32, D),
        full(8, D), full(3, 8, D), full(8, D), full(4, 8, D),
        full(3, 8, D), full(1, 8, D), full(ring, 8, D), full(ring, 8, D),
        sem(5), sem(3), sem(3), one, sem(3), one, sem(3), sem(3), sem(3, 3), one, one,
        sem(3), sem(3), sem(3), sem(3),
        sem(3, 3), sem(3), sem(3, 3), sem(3), sem(3, 3), sem(3), one, one,
        sem(4), sem(4), sem(4, ring), sem(4, ring), sem(4, ring), sem(4, ring),
        sem(3, ring), sem(3, ring), sem(3, ring), sem(3, ring), sem(3), sem(3),
        sem(ring), sem(ring), sem(ring), sem(ring), one, one,
        sem(3), sem(3), sem(1), sem(1), sem(ring), sem(ring), sem(ring), sem(ring), sem(3),
        pltpu.SemaphoreType.REGULAR, pltpu.SemaphoreType.REGULAR,
    ]
    hbm = pl.BlockSpec(memory_space=pl.ANY)
    vmem = pl.BlockSpec(memory_space=pltpu.VMEM)
    out, lgrad, igrad, grads, tiny = pl.pallas_call(
        functools.partial(kernel, n),
        name="layers",
        out_shape=(
            jax.ShapeDtypeStruct(lat.shape, BF),
            jax.ShapeDtypeStruct(lat.shape, F32),
            jax.ShapeDtypeStruct(raw.shape, F32),
            jax.ShapeDtypeStruct((3, 2 * D, D), BF),
            jax.ShapeDtypeStruct((8, D), F32),
        ),
        in_specs=[hbm, hbm, hbm, pl.BlockSpec(memory_space=pltpu.SMEM), vmem, hbm, hbm, vmem, vmem],
        out_specs=(vmem, vmem, vmem, hbm, vmem),
        scratch_shapes=scratch,
        compiler_params=pltpu.CompilerParams(
            collective_id=0, has_side_effects=True, vmem_limit_bytes=60 * 2**20
        ),
    )(lat, raw, cot, lengths, clip.reshape(3, 1, LAT), w, f, snorm, inorm)
    entry = grads[0:2].reshape(4, D, D).transpose(1, 0, 2).reshape(1, D, 4 * D).astype(F32)
    down = grads[2].reshape(1, 2 * D, D).astype(F32)
    column = lax.axis_index("section") * 192
    return (
        out, lgrad, igrad, entry, down, tiny[0:2][None],
        lax.dynamic_slice(tiny, (2, column), (2, 192)),
    )


def solution(mesh):
    rows_split = P("dp", "section", None)
    weight = P("section", None, None)
    return jax.shard_map(
        on_device,
        mesh=mesh,
        in_specs=(
            rows_split, rows_split, rows_split, P("dp", None), P("dp", None),
            weight, weight, weight, P(None, "section"),
        ),
        out_specs=(rows_split, rows_split, rows_split, weight, weight, weight, P(None, "section")),
        check_vma=False,
    )
```

```python
import jax
import jax.numpy as jnp
from jax import lax
from jax.experimental import pallas as pl
from jax.experimental.pallas import tpu as pltpu
from jax.sharding import PartitionSpec as P


D = 768
LAT = 128
SEQ = 512
EPS = 1e-5
NEG = -1e9
F32 = jnp.float32
BF = jnp.bfloat16


def nn(a, b):
    return jnp.dot(a, b, preferred_element_type=F32)


def nt(a, b):
    return lax.dot_general(a, b, (((1,), (1,)), ((), ())), preferred_element_type=F32)


def tn(a, b):
    return lax.dot_general(a, b, (((0,), (0,)), ((), ())), preferred_element_type=F32)


def unit(x):
    mean = jnp.mean(x, -1, keepdims=True)
    cen = x - mean
    var = jnp.mean(cen * cen, -1, keepdims=True)
    rstd = lax.rsqrt(var + EPS)
    return cen * rstd, rstd


def ln_back(x, da, gain):
    xhat, rstd = unit(x)
    dx = da * gain
    m1 = jnp.mean(dx, -1, keepdims=True)
    m2 = jnp.mean(dx * xhat, -1, keepdims=True)
    grad = rstd * (dx - m1 - xhat * m2)
    return grad, jnp.sum(da * xhat, 0, keepdims=True), jnp.sum(da, 0, keepdims=True)


def gelu_pair(z):
    a = jnp.abs(z)
    t = 1.0 / (1.0 + (0.3275911 * 0.7071067811865476) * a)
    e = jnp.exp(-0.5 * (z * z))
    p = t * (0.254829592 + t * (-0.284496736 + t * (1.421413741 + t * (-1.453152027 + t * 1.061405429))))
    half = (0.5 * p) * e
    cdf = jnp.where(z >= 0, 1.0 - half, half)
    return z * cdf, cdf + z * (0.3989422804014327 * e)


def rows(i, n):
    return pl.ds(pl.multiple_of(i * n, n), n)


def ffn_fwd(i, xin, gain, shift, W, Fd, A, X):
    x = xin[i].astype(F32)
    xhat, _ = unit(x)
    a = (xhat * gain + shift).astype(BF)
    A[rows(i, LAT)] = a
    total = x
    for c in range(4):
        gate, slope = gelu_pair(nn(a, W[:, c * D:(c + 1) * D]))
        gate = gate.astype(BF)
        where_ = pl.ds(pl.multiple_of(c * 384 + i * LAT, LAT), LAT)
        X[0, where_] = gate
        X[2, where_] = slope.astype(BF)
        total = total + nn(gate, Fd[c // 2, (c % 2) * D:(c % 2 + 1) * D])
    return total


def ffn_bwd(i, db, W, Fd, X):
    da = None
    for c in range(4):
        dg = nt(db, Fd[c // 2, (c % 2) * D:(c % 2 + 1) * D])
        where_ = pl.ds(pl.multiple_of(c * 384 + i * LAT, LAT), LAT)
        dz = (X[2, where_].astype(F32) * dg).astype(BF)
        X[1, where_] = dz
        part = nt(dz, W[:, c * D:(c + 1) * D])
        da = part if da is None else da + part
    return da


def halves(m):
    lane = lax.broadcasted_iota(jnp.int32, m.shape, 1)
    zero = jnp.zeros_like(m)
    return jnp.concatenate([jnp.where(lane < 64, m, zero), jnp.where(lane >= 64, m, zero)], 0)


def unhalves(mt):
    q = mt.shape[1] // 2
    return jnp.concatenate([mt[0:64, 0:q], mt[64:128, q:2 * q]], 0).T


def attn_fwd(q, k, v, maskf, PT, O):
    for p in range(6):
        cols = slice(p * 128, (p + 1) * 128)
        qs = halves(q[:, cols])
        s = nt(k[:, cols], qs) * 0.125
        s = jnp.where(maskf, s, NEG)
        m = jnp.max(s, 0, keepdims=True)
        e = jnp.exp(s - m)
        l = jnp.sum(e, 0, keepdims=True)
        pt = (e * (1.0 / l)).astype(BF)
        PT[p] = pt
        ot = tn(v[:, cols], pt)
        O[:, cols] = unhalves(ot).astype(BF)


def attn_bwd(q, k, v, PT, do, dq, dk, dv):
    for p in range(6):
        cols = slice(p * 128, (p + 1) * 128)
        dos = halves(do[:, cols])
        qs = halves(q[:, cols])
        pt = PT[p]
        dp = nt(v[:, cols], dos)
        ptf = pt.astype(F32)
        w = dp * ptf
        delta = jnp.sum(w, 0, keepdims=True)
        ds = (w - ptf * delta).astype(BF)
        dk[:, cols] = (nn(ds, qs) * 0.125).astype(BF)
        dv[:, cols] = nn(pt, dos).astype(BF)
        dqt = tn(k[:, cols], ds)
        dq[:, cols] = (unhalves(dqt) * 0.125).astype(BF)


HALF = 768
QUARTER = 192
PIECE = 48
SIDE = 96
VIA = 80
N = 4
MESH = pl.DeviceIdType.MESH


def kernel(
    lat_ref, raw_ref, cot_ref, len_ref, clip_ref, w_ref, f_ref, snorm_ref, inorm_ref,
    out_ref, lgrad_ref, igrad_ref, entry_ref, down_ref, tiny_ref,
    W, Fd, g, X, PT, rA, rB, rC, q, xin, dBin, sendB, sendD, A, Q, O, dQ, dO, rawv, relay, dUb, outb, lgb,
    inb, inr, nacc, tsrc, tX, tC, t1, t2,
    loc, in_s, in_r, lat_s, lat_r, cot_s, cot_r, u_s, u_r, via_s, via_r, fx_s, fx_r, b_s, b_r, d_s, d_r,
    o_s, o_r, lg_s, lg_r, du_s, du_r, gx_s, gx_r,
    a_s, a_r, bb_s, bb_r, c_s, c_r, gd_s, gd_r, ge_s, ge_r, gf_s, gf_r,
    fd_s, fd_r, fe_s, fe_r, ff_s, ff_r, tx_s, tx_r, tc_s, tc_r, t1_s, t1_r, t2_s, t2_r, g_sem, free_a, free_b,
):
    s = lax.axis_index("section")
    dp = lax.axis_index("dp")
    c = lax.rem(dp, 2)
    z = lax.rem(dp // 2, N)
    y = dp // (2 * N)
    odd = lax.rem(s, 2) == 1
    r1 = y * (1 - c) + z * c
    r2 = z * (1 - c) + y * c
    mate = dp + 1 - 2 * c

    def sec_of(k):
        return lax.rem(s + k, 4)

    def peer1(k):
        other = lax.rem(r1 + k, N)
        return ((other * (1 - c) + y * c) * N + z * (1 - c) + other * c) * 2 + c

    def peer2(k):
        other = lax.rem(r2 + k, N)
        return ((y * (1 - c) + other * c) * N + other * (1 - c) + z * c) * 2 + c

    def at(start, size, unit_size):
        return pl.ds(pl.multiple_of(start, unit_size), size)

    def remote(src, dst, send_sem, recv_sem, dp_to, sec_to):
        return pltpu.make_async_remote_copy(
            src_ref=src, dst_ref=dst, send_sem=send_sem, recv_sem=recv_sem,
            device_id=(dp_to, sec_to), device_id_type=MESH,
        )

    def local_w():
        return pltpu.make_async_copy(w_ref.at[0], W, loc.at[0])

    def local_f():
        return pltpu.make_async_copy(f_ref.at[0], Fd.at[1], loc.at[1])

    def local_raw():
        return pltpu.make_async_copy(raw_ref, rawv, loc.at[2])

    def local_lat():
        return pltpu.make_async_copy(lat_ref, xin.at[:, at(s * 32, 32, 32)], loc.at[3])

    def local_tokens(i):
        return pltpu.make_async_copy(raw_ref.at[i], X.at[0, at(i * SEQ, LAT, LAT)], loc.at[5 + i])

    def local_cot():
        return pltpu.make_async_copy(cot_ref, dBin.at[:, at(s * 32, 32, 32)], loc.at[4])

    def cp_in(k):
        return remote(inb, inr.at[k - 1], in_s.at[k - 1], in_r.at[k - 1], dp, sec_of(k))

    def cp_lat(i, src):
        return remote(
            lat_ref.at[i], xin.at[i, at(src * 32, 32, 32)],
            lat_s.at[i], lat_r.at[i, src - 1], dp, 0,
        )

    def cp_cot(src):
        return remote(cot_ref, dBin.at[:, at(src * 32, 32, 32)], cot_s, cot_r.at[src], dp, 3)

    def cp_u(i, src):
        count = LAT - VIA if src == 2 else LAT
        return remote(
            raw_ref.at[i, 0:count], X.at[0, at(i * SEQ + src * LAT, count, 16)],
            u_s.at[i], u_r.at[i, src - 1], dp, 0,
        )

    def cp_via(i):
        return remote(raw_ref.at[i, LAT - VIA:LAT], relay.at[i], via_s.at[i], via_r.at[i], dp, 1)

    def cp_on(i):
        return remote(
            relay.at[i], X.at[0, at(i * SEQ + 3 * LAT - VIA, VIA, 16)],
            via_s.at[i], u_r.at[i, 3], dp, 0,
        )

    own_piece = c * HALF + r1 * QUARTER + r2 * PIECE

    def cp_fx():
        return remote(
            f_ref.at[0, at(own_piece, PIECE, PIECE)], Fd.at[0, at(own_piece, PIECE, PIECE)],
            fx_s, fx_r, dp, jnp.minimum(s + 1, 3),
        )

    def cp_b(i):
        return remote(sendB.at[i], xin.at[i], b_s.at[i], b_r.at[i], dp, jnp.minimum(s + 1, 3))

    def cp_d(i):
        return remote(sendD.at[i], dBin.at[i], d_s.at[i], d_r.at[i], dp, jnp.maximum(s - 1, 0))

    def cp_o(i, t):
        return remote(sendB.at[i, t * 32:(t + 1) * 32], outb.at[i], o_s.at[i, t], o_r.at[i], dp, t)

    def cp_lg(i, t):
        return remote(sendD.at[i, t * 32:(t + 1) * 32], lgb.at[i], lg_s.at[i, t - 1], lg_r.at[i], dp, t)

    def cp_du(i, t):
        return remote(
            X.at[5, at(i * SEQ + t * 128, 128, 128)], dUb.at[i],
            du_s.at[i, t - 1], du_r.at[i], dp, t,
        )

    def cp_gx():
        return remote(
            q.at[3, at(r2 * PIECE, PIECE, PIECE)], q.at[2, at(r2 * PIECE, PIECE, PIECE)],
            gx_s, gx_r, dp, jnp.maximum(s - 1, 0),
        )

    def cp_a(b):
        return remote(g.at[b, at((1 - c) * HALF, HALF, HALF)], rA.at[b], a_s.at[b], a_r.at[b], mate, s)

    def half_of(j, h):
        return at(c * HALF + lax.rem(r1 + j, N) * QUARTER + h * SIDE, SIDE, SIDE)

    def cp_rb(b, j):
        source, slot, lo, to = (
            (half_of(2, 0), 2, 0, 1), (half_of(2, 1), 2, 1, 3),
            (half_of(1, 1), 0, 1, 1), (half_of(3, 0), 1, 0, 3),
            (half_of(1, 0), 0, 0, 1), (half_of(3, 1), 1, 1, 3),
        )[j]
        return remote(
            g.at[b, source], rB.at[b, slot, lo * SIDE:(lo + 1) * SIDE],
            bb_s.at[b, j], bb_r.at[b, j], peer1(to), s,
        )

    def cp_rc(b, k):
        start = c * HALF + r1 * QUARTER + lax.rem(r2 + k, N) * PIECE
        return remote(
            g.at[b, at(start, PIECE, PIECE)], rC.at[b, k - 1],
            c_s.at[b, k - 1], c_r.at[b, k - 1], peer2(k), s,
        )

    def ag_d(ref, start, ss, rs, k):
        where_ = at(start + r2 * PIECE, PIECE, PIECE)
        return remote(ref.at[where_], ref.at[where_], ss.at[k - 1], rs.at[k - 1], peer2(k), s)

    def ag_d_in(ref, start, ss, rs, k):
        where_ = at(start + lax.rem(r2 + N - k, N) * PIECE, PIECE, PIECE)
        return remote(ref.at[where_], ref.at[where_], ss.at[k - 1], rs.at[k - 1], peer2(k), s)

    own_quarter = c * HALF + r1 * QUARTER

    def ag_e(src, ref, ss, rs, j):
        if j < 2:
            where_ = at(own_quarter, QUARTER, QUARTER)
            return remote(src, ref.at[where_], ss.at[j], rs.at[j], peer1(1 + 2 * j), s)
        where_ = half_of(3, 0) if j == 2 else half_of(1, 1)
        return remote(ref.at[where_], ref.at[where_], ss.at[j], rs.at[j], peer1(1 if j == 2 else 3), s)

    def ag_e_in(src, ref, ss, rs, j):
        if j < 2:
            where_ = at(c * HALF + lax.rem(r1 + 3 - 2 * j, N) * QUARTER, QUARTER, QUARTER)
            return remote(src, ref.at[where_], ss.at[j], rs.at[j], peer1(1 + 2 * j), s)
        where_ = half_of(2, j - 2)
        return remote(ref.at[where_], ref.at[where_], ss.at[j], rs.at[j], peer1(1), s)

    def ag_f(ref, ss, rs):
        where_ = at(c * HALF, HALF, HALF)
        return remote(ref.at[where_], ref.at[where_], ss, rs, mate, s)

    def ag_f_in(ref, ss, rs):
        where_ = at((1 - c) * HALF, HALF, HALF)
        return remote(ref.at[where_], ref.at[where_], ss, rs, mate, s)

    ring = range(1, N)

    def gather_e(src, ref, ss, rs):
        for j in (0, 1):
            ag_e(src, ref, ss, rs, j).start()
        for j in (0, 1):
            ag_e_in(src, ref, ss, rs, j).wait_recv()
            ag_e(src, ref, ss, rs, j + 2).start()
        for j in (2, 3):
            ag_e_in(src, ref, ss, rs, j).wait_recv()

    def stage_b(b):
        cp_a(b).wait_recv()
        for j in (2, 1, 3, 0):
            part = at(c * HALF + lax.rem(r1 + j, N) * QUARTER, QUARTER, QUARTER)
            other = at(lax.rem(r1 + j, N) * QUARTER, QUARTER, QUARTER)
            g[b, part] = (g[b, part].astype(F32) + rA[b, other].astype(F32)).astype(BF)
            if j == 2:
                cp_rb(b, 0).start()
                cp_rb(b, 1).start()
            elif j == 1:
                cp_rb(b, 2).start()
            elif j == 3:
                cp_rb(b, 3).start()

    local_raw().start()
    local_w().start()
    local_f().start()

    barrier = pltpu.get_barrier_semaphore()
    partners = [(dp, sec_of(k)) for k in (1, 2, 3)] + [(mate, s)]
    partners += [(peer1(k), s) for k in ring] + [(peer2(k), s) for k in ring]
    for partner in partners:
        pl.semaphore_signal(barrier, inc=1, device_id=partner, device_id_type=MESH)
    select = lax.broadcasted_iota(jnp.int32, (192, D), 1) == lax.broadcasted_iota(jnp.int32, (192, D), 0) + s * 192
    inb[...] = jnp.zeros_like(inb)
    inb[0:2] = nn(inorm_ref[...], select.astype(F32).astype(BF))
    nacc[...] = jnp.zeros_like(nacc)
    pl.semaphore_wait(barrier, len(partners))

    for k in (1, 2, 3):
        cp_in(k).start()

    @pl.when(s == 0)
    def _():
        local_lat().start()
        for i in range(3):
            local_tokens(i).start()

    for sec in (1, 2, 3):
        @pl.when(s == sec)
        def _():
            for i in range(3):
                cp_lat(i, sec).start()
                if sec == 2:
                    cp_via(i).start()
                cp_u(i, sec).start()

    @pl.when(jnp.logical_not(odd))
    def _():
        cp_fx().start()

    @pl.when(s == 3)
    def _():
        local_cot().start()

    @pl.when(s != 3)
    def _():
        cp_cot(s).start()

    @pl.when(s == 1)
    def _():
        @pl.loop(0, 3)
        def _(i):
            cp_via(i).wait_recv()
            cp_on(i).start()

    snorm = snorm_ref[0].astype(F32)
    gain = 1.0 + snorm[0:1]
    shift = snorm[1:2]

    def project(a, lo, hi):
        return nn(a, W[:, lo:hi])

    def latent_back(i, da, db):
        dx, dg, dbias = ln_back(xin[i].astype(F32), da, gain)
        nacc[0:1] = nacc[0:1] + dg
        nacc[1:2] = nacc[1:2] + dbias
        return db.astype(F32) + dx

    local_w().wait()

    @pl.when(s == 0)
    def _():
        local_lat().wait()
        for k in (1, 2, 3):
            cp_in(k).wait_recv()
        in_all = inb[...] + inr[0] + inr[1] + inr[2]

        @pl.loop(0, 3)
        def _(i):
            for src in (1, 2, 3):
                cp_lat(i, src).wait_recv()
            x = xin[i].astype(F32)
            xhat, _ = unit(x)
            a = (xhat * gain + shift).astype(BF)
            lat_rows = rows(i, LAT)
            A[lat_rows] = a
            Q[lat_rows] = project(a, 0, D).astype(BF)
            for src in (1, 2, 3):
                cp_u(i, src).wait_recv()
            cp_on(i).wait_recv()
            local_tokens(i).wait()

            @pl.loop(0, 4)
            def _(j):
                part = at(i * SEQ + j * LAT, LAT, LAT)
                xhat, _ = unit(X[0, part].astype(F32))
                X[0, part] = (xhat * (1.0 + in_all[0:1]) + in_all[1:2]).astype(BF)
            u = X[0, rows(i, SEQ)]
            kv = [X.at[j, rows(i, SEQ)] for j in (1, 2)]
            kv[0][...] = project(u, D, 2 * D).astype(BF)
            kv[1][...] = project(u, 2 * D, 3 * D).astype(BF)
            where_ = lax.broadcasted_iota(jnp.int32, (SEQ, 256), 0)
            clip = jnp.zeros((SEQ, 256), jnp.int32)
            end = jnp.int32(0)
            for j in range(4):
                end = end + len_ref[i, j]
                clip = clip + (where_ >= end).astype(jnp.int32)
            ids = jnp.concatenate([clip_ref[i], clip_ref[i]], 1)
            attn_fwd(Q.at[lat_rows], kv[0], kv[1], clip == ids, PT.at[i], O.at[lat_rows])
            b = x + project(O[lat_rows], 3 * D, 4 * D)
            sendB[i] = b.astype(BF)
            cp_b(i).start()

        def send_du(i):
            at_rows = rows(i, SEQ)
            du = nt(X[3, at_rows], W[:, D:2 * D]) + nt(X[4, at_rows], W[:, 2 * D:3 * D])
            X[5, at_rows] = du.astype(BF)
            dUb[i] = X[5, at(i * SEQ, LAT, LAT)]
            for t in (1, 2, 3):
                cp_du(i, t).start()

        def latent_out(i):
            db = dBin[i]
            grad = latent_back(i, nt(dQ[rows(i, LAT)], W[:, :D]), db).astype(BF)
            sendD[i] = grad
            lgb[i] = grad[0:32]
            for t in (1, 2, 3):
                cp_lg(i, t).start()

        def block_grad(b, tokens, latents):
            count = (latents.stop - latents.start)
            db = dBin[latents.start // LAT:latents.stop // LAT].reshape(count, D)
            if b == 0:
                return tn(A[latents], dQ[latents]), tn(X[0, tokens], X[3, tokens])
            return tn(X[0, tokens], X[4, tokens]), tn(O[latents], db)

        @pl.loop(0, 3)
        def _(i):
            cp_d(i).wait_recv()
            dO[...] = nt(dBin[i], W[:, 3 * D:]).astype(BF)
            kv = [X.at[j, rows(i, SEQ)] for j in (1, 2, 3, 4)]
            lat_rows = rows(i, LAT)
            attn_bwd(Q.at[lat_rows], kv[0], kv[1], PT.at[i], dO, dQ.at[lat_rows], kv[2], kv[3])

            @pl.when(i < 2)
            def _():
                latent_out(i)

            @pl.when(i == 0)
            def _():
                send_du(0)

            @pl.when(i == 1)
            def _():
                for b in range(2):
                    upper, lower = block_grad(b, slice(0, 2 * SEQ), slice(0, 2 * LAT))
                    g[b, 0:D] = upper.astype(BF)
                    g[b, D:] = lower.astype(BF)

        for b in range(2):
            upper, lower = block_grad(b, slice(2 * SEQ, 3 * SEQ), slice(2 * LAT, 3 * LAT))
            g[b, 0:D] = (g[b, 0:D].astype(F32) + upper).astype(BF)
            g[b, D:] = (g[b, D:].astype(F32) + lower).astype(BF)
            cp_a(b).start()
        latent_out(2)
        stage_b(0)
        send_du(1)
        stage_b(1)
        send_du(2)

    @pl.when(s == 2)
    def _():
        @pl.loop(0, 3)
        def _(i):
            lat_rows = rows(i, LAT)
            cp_b(i).wait_recv()
            x = xin[i].astype(F32)
            xhat, _ = unit(x)
            a = (xhat * gain + shift).astype(BF)
            A[lat_rows] = a
            Q[lat_rows] = project(a, 0, D).astype(BF)
            X[1, lat_rows] = project(a, D, 2 * D).astype(BF)
            X[2, lat_rows] = project(a, 2 * D, 3 * D).astype(BF)
            ids = jnp.broadcast_to(clip_ref[i].astype(F32), (LAT, LAT))
            mask = jnp.concatenate([ids, ids], 1) == jnp.concatenate([ids.T, ids.T], 1)
            attn_fwd(
                Q.at[lat_rows], X.at[1, lat_rows], X.at[2, lat_rows], mask,
                PT.at[i, :, 0:LAT], O.at[lat_rows],
            )
            b = x + project(O[lat_rows], 3 * D, 4 * D)
            sendB[i] = b.astype(BF)
            cp_b(i).start()

        @pl.loop(0, 3)
        def _(i):
            lat_rows = rows(i, LAT)
            cp_d(i).wait_recv()
            db = dBin[i]
            dO[...] = nt(db, W[:, 3 * D:]).astype(BF)
            attn_bwd(
                Q.at[lat_rows], X.at[1, lat_rows], X.at[2, lat_rows], PT.at[i, :, 0:LAT],
                dO, dQ.at[lat_rows], X.at[3, lat_rows], X.at[4, lat_rows],
            )
            da = nt(dQ[lat_rows], W[:, :D]) + nt(X[3, lat_rows], W[:, D:2 * D])
            da = da + nt(X[4, lat_rows], W[:, 2 * D:3 * D])
            sendD[i] = latent_back(i, da, db).astype(BF)
            cp_d(i).start()

        a = A[...]
        g[0, 0:D] = tn(a, dQ[...]).astype(BF)
        g[0, D:] = tn(a, X[3, 0:3 * LAT]).astype(BF)
        cp_a(0).start()
        g[1, 0:D] = tn(a, X[4, 0:3 * LAT]).astype(BF)
        g[1, D:] = tn(O[...], dBin[...].reshape(3 * LAT, D)).astype(BF)
        cp_a(1).start()
        stage_b(0)
        stage_b(1)

    @pl.when(odd)
    def _():
        prior = Fd.at[0]
        mine = prior.at[at(own_quarter, QUARTER, QUARTER)]
        cp_fx().wait_recv()
        for k in ring:
            ag_d(prior, own_quarter, fd_s, fd_r, k).start()
        for k in ring:
            ag_d_in(prior, own_quarter, fd_s, fd_r, k).wait_recv()
        gather_e(mine, prior, fe_s, fe_r)
        ag_f(prior, ff_s, ff_r).start()
        local_f().wait()
        ag_f_in(prior, ff_s, ff_r).wait_recv()

        @pl.when(s == 3)
        def _():
            local_cot().wait()
            for src in (0, 1, 2):
                cp_cot(src).wait_recv()

        def block_grad(b, j, first, count):
            start = (2 * (b % 2) + j) * 384 if b < 2 else (2 * (1 - b % 2) + j) * 384
            here = slice(start + first * LAT, start + (first + count) * LAT)
            own = slice(first * LAT, (first + count) * LAT)
            if b > 1:
                return tn(X[0, here], dBin[first:first + count].reshape(count * LAT, D))
            return tn(A[own], X[1, here])

        def store_grads(b, first, count, add):
            for j in range(2):
                here = slice(j * D, (j + 1) * D)
                grad = block_grad(b, j, first, count)
                g[b, here] = ((g[b, here].astype(F32) + grad) if add else grad).astype(BF)

        @pl.loop(0, 6)
        def _(step):
            last = s == 3
            forward = jnp.where(last, lax.rem(step, 2) == 0, step < 3)
            i = jnp.where(last, step // 2, lax.rem(step, 3))

            @pl.when(forward)
            def _():
                cp_b(i).wait_recv()
                b = ffn_fwd(i, xin, gain, shift, W, Fd, A, X).astype(BF)
                sendB[i] = b

                @pl.when(s == 1)
                def _():
                    cp_b(i).start()

                @pl.when(last)
                def _():
                    outb[i] = b[96:128]
                    for t in (0, 1, 2):
                        cp_o(i, t).start()

            @pl.when(jnp.logical_not(forward))
            def _():
                @pl.when(s == 1)
                def _():
                    cp_d(i).wait_recv()
                db = dBin[i]
                sendD[i] = latent_back(i, ffn_bwd(i, db, W, Fd, X), db).astype(BF)
                cp_d(i).start()

                @pl.when((s == 1) & (i == 1))
                def _():
                    for b in range(4):
                        store_grads(b, 0, 2, False)

        for t, b in enumerate((3, 2, 0, 1)):
            @pl.when(s == 1)
            def _():
                store_grads(b, 2, 1, True)

            @pl.when(s == 3)
            def _():
                store_grads(b, 0, 3, False)
            cp_a(b).start()
            if t > 0:
                stage_b((3, 2, 0, 1)[t - 1])
        stage_b(1)

    count = jnp.where(odd, 4, 2)

    def block(t):
        return jnp.where(odd, jnp.where(t < 2, 3 - t, t - 2), t)

    @pl.loop(0, count)
    def _(t):
        b = block(t)
        for j in (0, 1):
            cp_rb(b, j).wait_recv()
            mine = half_of(1 + 2 * j, j)
            arrived = rB[b, 2, j * SIDE:(j + 1) * SIDE].astype(F32)
            g[b, mine] = (g[b, mine].astype(F32) + arrived).astype(BF)
            cp_rb(b, 4 + j).start()

    @pl.loop(0, count)
    def _(t):
        b = block(t)
        for j in (2, 3, 4, 5):
            cp_rb(b, j).wait_recv()
        part = at(own_quarter, QUARTER, QUARTER)
        total = g[b, part].astype(F32) + rB[b, 0].astype(F32) + rB[b, 1].astype(F32)
        g[b, part] = total.astype(BF)
        for k in ring:
            cp_rc(b, k).start()

    @pl.loop(0, count)
    def _(t):
        b = block(t)
        cp_a(b).wait_send()
        pl.semaphore_signal(free_a, inc=1, device_id=(mate, s), device_id_type=MESH)
        for j in range(6):
            cp_rb(b, j).wait_send()
        for k in (1, 3):
            pl.semaphore_signal(free_b, inc=1, device_id=(peer1(k), s), device_id_type=MESH)
        for k in ring:
            cp_rc(b, k).wait_recv()
        total = g[b, at(own_piece, PIECE, PIECE)].astype(F32)
        for k in ring:
            total = total + rC[b, k - 1].astype(F32)
        q[b, at(r2 * PIECE, PIECE, PIECE)] = total.astype(BF)

        @pl.when(b == 3)
        def _():
            cp_gx().start()

        @pl.when(b < 3)
        def _():
            for k in ring:
                ag_d(q.at[b], 0, gd_s.at[b], gd_r.at[b], k).start()

    @pl.when(jnp.logical_not(odd))
    def _():
        cp_gx().wait_recv()
        for k in ring:
            ag_d(q.at[2], 0, gd_s.at[2], gd_r.at[2], k).start()

    @pl.when(s != 0)
    def _():
        for k in (1, 2, 3):
            cp_in(k).wait_recv()
    local_raw().wait()
    in_gain = 1.0 + inb[0:1] + inr[0, 0:1] + inr[1, 0:1] + inr[2, 0:1]

    @pl.loop(0, 3)
    def _(i):
        @pl.when(s != 3)
        def _():
            cp_o(i, 0).wait_recv()

        @pl.when(s != 0)
        def _():
            cp_lg(i, 1).wait_recv()
            cp_du(i, 1).wait_recv()
        dx, dg, dbias = ln_back(rawv[i].astype(F32), dUb[i].astype(F32), in_gain)
        igrad_ref[i] = dx
        nacc[2:3] = nacc[2:3] + dg
        nacc[3:4] = nacc[3:4] + dbias
        out_ref[i] = outb[i]
        lgrad_ref[i] = lgb[i].astype(F32)

    def small(step, buf, ss, rs, k, dp_to, sec_to):
        return remote(tsrc.at[step], buf.at[k], ss.at[k], rs.at[k], dp_to, sec_to)

    row = lax.broadcasted_iota(jnp.int32, (8, D), 0)
    own = jnp.where(row < 4, nacc[...], 0.0)
    tsrc[0] = own
    for k in (1, 2, 3):
        small(0, tX, tx_s, tx_r, k - 1, dp, sec_of(k)).start()

    @pl.loop(0, count)
    def _(t):
        for k in ring:
            cp_rc(block(t), k).wait_send()
    pl.semaphore_wait(free_b, count * 2)
    for b in range(3):
        for k in ring:
            ag_d_in(q.at[b], 0, gd_s.at[b], gd_r.at[b], k).wait_recv()
        for j in (0, 1):
            ag_e(q.at[b], g.at[b], ge_s.at[b], ge_r.at[b], j).start()
        g[b, at(own_quarter, QUARTER, QUARTER)] = q[b]
    pl.semaphore_wait(free_a, count)

    for k in (1, 2, 3):
        small(0, tX, tx_s, tx_r, k - 1, dp, sec_of(k)).wait_recv()
    own = jnp.where(row < 2, own, own + tX[0] + tX[1] + tX[2])
    tsrc[1] = own
    small(1, tC, tc_s, tc_r, 0, mate, s).start()

    for b in range(3):
        for j in (0, 1):
            ag_e_in(q.at[b], g.at[b], ge_s.at[b], ge_r.at[b], j).wait_recv()
            ag_e(q.at[b], g.at[b], ge_s.at[b], ge_r.at[b], j + 2).start()
    for b in range(3):
        for j in (2, 3):
            ag_e_in(q.at[b], g.at[b], ge_s.at[b], ge_r.at[b], j).wait_recv()
        ag_f(g.at[b], gf_s.at[b], gf_r.at[b]).start()
        if b == 0:
            small(1, tC, tc_s, tc_r, 0, mate, s).wait_recv()
            own = own + tC[0]
            tsrc[2] = own
            for k in ring:
                small(2, t1, t1_s, t1_r, k - 1, peer1(k), s).start()
        if b == 1:
            for k in ring:
                small(2, t1, t1_s, t1_r, k - 1, peer1(k), s).wait_recv()
                own = own + t1[k - 1]
            tsrc[3] = own
            for k in ring:
                small(3, t2, t2_s, t2_r, k - 1, peer2(k), s).start()
    for k in ring:
        small(3, t2, t2_s, t2_r, k - 1, peer2(k), s).wait_recv()
        own = own + t2[k - 1]
    tiny_ref[...] = own

    def leave(b, j):
        src = g.at[b, j * D:(j + 1) * D]
        if b == 2:
            return pltpu.make_async_copy(src, down_ref.at[0, j * D:(j + 1) * D], g_sem.at[b, j])
        blk = 2 * b + j
        return pltpu.make_async_copy(src, entry_ref.at[0, :, blk * D:(blk + 1) * D], g_sem.at[b, j])

    for b in range(3):
        ag_f_in(g.at[b], gf_s.at[b], gf_r.at[b]).wait_recv()
        for j in range(2):
            leave(b, j).start()
    for b in range(3):
        for j in range(2):
            leave(b, j).wait()

    for k in (1, 2, 3):
        cp_in(k).wait_send()
        small(0, tX, tx_s, tx_r, k - 1, dp, sec_of(k)).wait_send()
    small(1, tC, tc_s, tc_r, 0, mate, s).wait_send()
    for k in ring:
        small(2, t1, t1_s, t1_r, k - 1, peer1(k), s).wait_send()
        small(3, t2, t2_s, t2_r, k - 1, peer2(k), s).wait_send()

    @pl.when(s == 0)
    def _():
        @pl.loop(0, 3)
        def _(i):
            for t in (1, 2, 3):
                cp_lg(i, t).wait_send()
                cp_du(i, t).wait_send()

    for sec in (1, 2, 3):
        @pl.when(s == sec)
        def _():
            for i in range(3):
                cp_lat(i, sec).wait_send()
                cp_u(i, sec).wait_send()
                if sec == 2:
                    cp_via(i).wait_send()
                if sec == 1:
                    cp_on(i).wait_send()
                cp_d(i).wait_send()

    @pl.when(s == 3)
    def _():
        @pl.loop(0, 3)
        def _(i):
            for t in (0, 1, 2):
                cp_o(i, t).wait_send()

    @pl.when(s != 3)
    def _():
        cp_cot(s).wait_send()

        @pl.loop(0, 3)
        def _(i):
            cp_b(i).wait_send()

    @pl.when(odd)
    def _():
        for k in ring:
            mine = Fd.at[0, at(own_quarter, QUARTER, QUARTER)]
            ag_d(Fd.at[0], own_quarter, fd_s, fd_r, k).wait_send()
        for j in range(4):
            ag_e(mine, Fd.at[0], fe_s, fe_r, j).wait_send()
        ag_f(Fd.at[0], ff_s, ff_r).wait_send()
        cp_gx().wait_send()

    @pl.when(jnp.logical_not(odd))
    def _():
        cp_fx().wait_send()
        local_f().wait()

    for b in range(3):
        for k in ring:
            ag_d(q.at[b], 0, gd_s.at[b], gd_r.at[b], k).wait_send()
        for j in range(4):
            ag_e(q.at[b], g.at[b], ge_s.at[b], ge_r.at[b], j).wait_send()
        ag_f(g.at[b], gf_s.at[b], gf_r.at[b]).wait_send()


def on_device(lat, raw, cot, lengths, clip, w, f, snorm, inorm):
    ring = N - 1

    def low(*shape):
        return pltpu.VMEM(shape, BF)

    def full(*shape):
        return pltpu.VMEM(shape, F32)

    def sem(*shape):
        return pltpu.SemaphoreType.DMA(shape)

    one = pltpu.SemaphoreType.DMA
    scratch = [
        low(D, 4 * D), low(2, 2 * D, D), low(4, 2 * D, D), low(6, 2 * D, D), low(3, 6, SEQ, 256),
        low(4, HALF, D), low(4, 3, QUARTER, D), low(4, 3, PIECE, D), low(4, QUARTER, D),
        low(3, LAT, D), low(3, LAT, D), low(3, LAT, D), low(3, LAT, D),
        low(3 * LAT, D), low(3 * LAT, D), low(3 * LAT, D), low(3 * LAT, D), low(LAT, D),
        low(3, LAT, D), low(3, VIA, D), low(3, LAT, D), low(3, 32, D), low(3, 32, D),
        full(8, D), full(3, 8, D), full(8, D), full(4, 8, D),
        full(3, 8, D), full(1, 8, D), full(ring, 8, D), full(ring, 8, D),
        sem(8), sem(3), sem(3), sem(3), sem(3, 3), one, sem(3), sem(3), sem(3, 4), sem(3), sem(3), one, one,
        sem(3), sem(3), sem(3), sem(3),
        sem(3, 3), sem(3), sem(3, 3), sem(3), sem(3, 3), sem(3), one, one,
        sem(4), sem(4), sem(4, 6), sem(4, 6), sem(4, ring), sem(4, ring),
        sem(3, ring), sem(3, ring), sem(3, 4), sem(3, 4), sem(3), sem(3),
        sem(ring), sem(ring), sem(4), sem(4), one, one,
        sem(3), sem(3), sem(1), sem(1), sem(ring), sem(ring), sem(ring), sem(ring), sem(3, 2),
        pltpu.SemaphoreType.REGULAR, pltpu.SemaphoreType.REGULAR,
    ]
    hbm = pl.BlockSpec(memory_space=pl.ANY)
    vmem = pl.BlockSpec(memory_space=pltpu.VMEM)
    out, lgrad, igrad, entry, down, tiny = pl.pallas_call(
        kernel,
        name="layers",
        out_shape=(
            jax.ShapeDtypeStruct(lat.shape, BF),
            jax.ShapeDtypeStruct(lat.shape, F32),
            jax.ShapeDtypeStruct(raw.shape, F32),
            jax.ShapeDtypeStruct(w.shape, BF),
            jax.ShapeDtypeStruct(f.shape, BF),
            jax.ShapeDtypeStruct((8, D), F32),
        ),
        in_specs=[hbm, hbm, hbm, pl.BlockSpec(memory_space=pltpu.SMEM), vmem, hbm, hbm, vmem, vmem],
        out_specs=(vmem, vmem, vmem, hbm, hbm, vmem),
        scratch_shapes=scratch,
        compiler_params=pltpu.CompilerParams(
            collective_id=0, has_side_effects=True, vmem_limit_bytes=60 * 2**20
        ),
    )(lat, raw, cot, lengths, clip.reshape(3, 1, LAT), w, f, snorm, inorm)
    column = lax.axis_index("section") * 192
    return (
        out, lgrad, igrad, entry.astype(F32), down.astype(F32), tiny[0:2][None],
        lax.dynamic_slice(tiny, (2, column), (2, 192)),
    )


def solution(mesh):
    rows_split = P("dp", "section", None)
    weight = P("section", None, None)
    return jax.shard_map(
        on_device,
        mesh=mesh,
        in_specs=(
            rows_split, rows_split, rows_split, P("dp", None), P("dp", None),
            weight, weight, weight, P(None, "section"),
        ),
        out_specs=(rows_split, rows_split, rows_split, weight, weight, weight, P(None, "section")),
        check_vma=False,
    )
```

```python
import jax
import jax.numpy as jnp
from jax import lax
from jax.experimental import pallas as pl
from jax.experimental.pallas import tpu as pltpu
from jax.sharding import PartitionSpec as P


D = 768
LAT = 128
SEQ = 512
EPS = 1e-5
NEG = -1e9
F32 = jnp.float32
BF = jnp.bfloat16


def nn(a, b):
    return jnp.dot(a, b, preferred_element_type=F32)


def nt(a, b):
    return lax.dot_general(a, b, (((1,), (1,)), ((), ())), preferred_element_type=F32)


def tn(a, b):
    return lax.dot_general(a, b, (((0,), (0,)), ((), ())), preferred_element_type=F32)


def unit(x):
    mean = jnp.mean(x, -1, keepdims=True)
    cen = x - mean
    var = jnp.mean(cen * cen, -1, keepdims=True)
    rstd = lax.rsqrt(var + EPS)
    return cen * rstd, rstd


def ln_back(x, da, gain):
    xhat, rstd = unit(x)
    dx = da * gain
    m1 = jnp.mean(dx, -1, keepdims=True)
    m2 = jnp.mean(dx * xhat, -1, keepdims=True)
    grad = rstd * (dx - m1 - xhat * m2)
    return grad, jnp.sum(da * xhat, 0, keepdims=True), jnp.sum(da, 0, keepdims=True)


def gelu_pair(z):
    a = jnp.abs(z)
    t = 1.0 / (1.0 + (0.3275911 * 0.7071067811865476) * a)
    e = jnp.exp(-0.5 * (z * z))
    p = t * (0.254829592 + t * (-0.284496736 + t * (1.421413741 + t * (-1.453152027 + t * 1.061405429))))
    half = (0.5 * p) * e
    cdf = jnp.where(z >= 0, 1.0 - half, half)
    return z * cdf, cdf + z * (0.3989422804014327 * e)


def rows(i, n):
    return pl.ds(pl.multiple_of(i * n, n), n)


def ffn_fwd(i, x, a, W, Fd, X, kept):
    total = x
    for c in range(4):
        gate, slope = gelu_pair(nn(a, W[:, c * D:(c + 1) * D]))
        gate = gate.astype(BF)
        where_ = pl.ds(pl.multiple_of(c * 384 + i * LAT, LAT), LAT)
        if c < kept:
            X[0, where_] = gate
        X[5, where_] = slope.astype(BF)
        total = total + nn(gate, Fd[c // 2, (c % 2) * D:(c % 2 + 1) * D])
    return total


def ffn_bwd(i, db, W, Fd, X, kept):
    da = None
    for c in range(4):
        dg = nt(db, Fd[c // 2, (c % 2) * D:(c % 2 + 1) * D])
        where_ = pl.ds(pl.multiple_of(c * 384 + i * LAT, LAT), LAT)
        dz = (X[5, where_].astype(F32) * dg).astype(BF)
        if kept:
            X[1, where_] = dz
        part = nt(dz, W[:, c * D:(c + 1) * D])
        da = part if da is None else da + part
    return da


def halves(m):
    lane = lax.broadcasted_iota(jnp.int32, m.shape, 1)
    zero = jnp.zeros_like(m)
    return jnp.concatenate([jnp.where(lane < 64, m, zero), jnp.where(lane >= 64, m, zero)], 0)


def unhalves(mt):
    q = mt.shape[1] // 2
    return jnp.concatenate([mt[0:64, 0:q], mt[64:128, q:2 * q]], 0).T


def attn_fwd(q, k, v, maskf, PT, O):
    for p in range(6):
        cols = slice(p * 128, (p + 1) * 128)
        qs = halves(q[:, cols])
        s = nt(k[:, cols], qs) * 0.125
        s = jnp.where(maskf, s, NEG)
        m = jnp.max(s, 0, keepdims=True)
        e = jnp.exp(s - m)
        l = jnp.sum(e, 0, keepdims=True)
        pt = (e * (1.0 / l)).astype(BF)
        PT[p] = pt
        ot = tn(v[:, cols], pt)
        O[:, cols] = unhalves(ot).astype(BF)


def attn_bwd(q, k, v, PT, do, dq, dk, dv):
    for p in range(6):
        cols = slice(p * 128, (p + 1) * 128)
        dos = halves(do[:, cols])
        qs = halves(q[:, cols])
        pt = PT[p]
        dp = nt(v[:, cols], dos)
        ptf = pt.astype(F32)
        w = dp * ptf
        delta = jnp.sum(w, 0, keepdims=True)
        ds = (w - ptf * delta).astype(BF)
        dk[:, cols] = (nn(ds, qs) * 0.125).astype(BF)
        dv[:, cols] = nn(pt, dos).astype(BF)
        dqt = tn(k[:, cols], ds)
        dq[:, cols] = (unhalves(dqt) * 0.125).astype(BF)


HALF = 768
QUARTER = 192
PIECE = 48
SIDE = 96
VIA = 80
N = 4
MESH = pl.DeviceIdType.MESH


ORDER = (2, 0, 1)


def kernel(
    lat_ref, raw_ref, cot_ref, len_ref, clip_ref, w_ref, f_ref, snorm_ref, inorm_ref,
    out_ref, lgrad_ref, igrad_ref, entry_ref, down_ref, tiny_ref,
    W, Wb, Fd, g, X, PT, rA, rB, rC, q, xin, yin, dBin, dBm, sendB, sendD,
    A, Q, O, dQ, dO, rawv, relay, dUb, outb, lgb, inb, inr, nacc, tsrc, tX, tC, t1, t2,
    loc, in_s, in_r, lat_s, lat_r, cot_s, cot_r, u_s, u_r, via_s, via_r, fx_s, fx_r, wx_s, wx_r,
    b_s, b_r, d_s, d_r, e_s, e_r, gu_s, gu_r, o_s, o_r, lg_s, lg_r, du_s, du_r,
    a_s, a_r, bb_s, bb_r, c_s, c_r, gd_s, gd_r, ge_s, ge_r, gf_s, gf_r,
    fd_s, fd_r, fe_s, fe_r, ff_s, ff_r, wd_s, wd_r, we_s, we_r, wf_s, wf_r,
    tx_s, tx_r, tc_s, tc_r, t1_s, t1_r, t2_s, t2_r, g_sem, free_a, free_b,
):
    s = lax.axis_index("section")
    dp = lax.axis_index("dp")
    c = lax.rem(dp, 2)
    z = lax.rem(dp // 2, N)
    y = dp // (2 * N)
    odd = lax.rem(s, 2) == 1
    r1 = y * (1 - c) + z * c
    r2 = z * (1 - c) + y * c
    mate = dp + 1 - 2 * c
    ring = range(1, N)
    once = jnp.minimum(s + 1, 1)

    def apart(work, *args):
        @pl.loop(0, once)
        def _(_):
            work(*args)

    def sec_of(k):
        return lax.rem(s + k, 4)

    def peer1(k):
        other = lax.rem(r1 + k, N)
        return ((other * (1 - c) + y * c) * N + z * (1 - c) + other * c) * 2 + c

    def peer2(k):
        other = lax.rem(r2 + k, N)
        return ((y * (1 - c) + other * c) * N + other * (1 - c) + z * c) * 2 + c

    def at(start, size, unit_size):
        return pl.ds(pl.multiple_of(start, unit_size), size)

    def remote(src, dst, send_sem, recv_sem, dp_to, sec_to):
        return pltpu.make_async_remote_copy(
            src_ref=src, dst_ref=dst, send_sem=send_sem, recv_sem=recv_sem,
            device_id=(dp_to, sec_to), device_id_type=MESH,
        )

    def local_w():
        return pltpu.make_async_copy(w_ref.at[0], W, loc.at[0])

    def local_f():
        return pltpu.make_async_copy(f_ref.at[0], Fd.at[jnp.where(odd, 1, 0)], loc.at[1])

    def local_raw():
        return pltpu.make_async_copy(raw_ref, rawv, loc.at[2])

    def local_lat():
        return pltpu.make_async_copy(lat_ref, xin.at[:, at(s * 32, 32, 32)], loc.at[3])

    def local_cot():
        return pltpu.make_async_copy(cot_ref, dBin.at[:, at(s * 32, 32, 32)], loc.at[4])

    def local_tokens(i):
        return pltpu.make_async_copy(raw_ref.at[i], X.at[0, at(i * SEQ, LAT, LAT)], loc.at[5 + i])

    def cp_in(k):
        return remote(inb, inr.at[k - 1], in_s.at[k - 1], in_r.at[k - 1], dp, sec_of(k))

    def cp_lat(i, src):
        return remote(
            lat_ref.at[i], xin.at[i, at(src * 32, 32, 32)],
            lat_s.at[i], lat_r.at[i, src - 1], dp, 0,
        )

    def cp_cot(src, to):
        return remote(
            cot_ref, dBin.at[:, at(src * 32, 32, 32)], cot_s.at[to - 2], cot_r.at[src], dp, to
        )

    def cp_u(i, src):
        count = LAT - VIA if src == 2 else LAT
        return remote(
            raw_ref.at[i, 0:count], X.at[0, at(i * SEQ + src * LAT, count, 16)],
            u_s.at[i], u_r.at[i, src - 1], dp, 0,
        )

    def cp_via(i):
        return remote(raw_ref.at[i, LAT - VIA:LAT], relay.at[i], via_s.at[i], via_r.at[i], dp, 1)

    def cp_on(i):
        return remote(
            relay.at[i], X.at[0, at(i * SEQ + 3 * LAT - VIA, VIA, 16)],
            via_s.at[i], u_r.at[i, 3], dp, 0,
        )

    own_quarter = c * HALF + r1 * QUARTER
    own_piece = own_quarter + r2 * PIECE

    def cp_fx():
        where_ = at(own_piece, PIECE, PIECE)
        to = jnp.where(s == 3, 2, jnp.minimum(s + 1, 3))
        return remote(
            f_ref.at[0, where_], Fd.at[jnp.where(s == 3, 1, 0), where_], fx_s, fx_r, dp, to
        )

    def cp_wx():
        rows_ = at(r1 * QUARTER + r2 * PIECE, PIECE, PIECE)
        cols = at(c * 2 * D, 2 * D, 2 * D)
        return remote(w_ref.at[0, rows_, cols], Wb.at[rows_, cols], wx_s, wx_r, dp, 2)

    def cp_b(i, src):
        return remote(src.at[i], xin.at[i], b_s.at[i], b_r.at[i], dp, jnp.minimum(s + 1, 3))

    def cp_d(i):
        return remote(sendD.at[i], dBin.at[i], d_s.at[i], d_r.at[i], dp, jnp.maximum(s - 1, 0))

    def cp_e(i):
        return remote(sendD.at[i], Fd.at[1, at(i * LAT, LAT, LAT)], e_s.at[i], e_r.at[i], dp, 0)

    def cp_gu(i, blk):
        where_ = at(blk * 384 + i * LAT, LAT, LAT)
        return remote(X.at[0, where_], Fd.at[0, where_], gu_s.at[i, blk], gu_r.at[i, blk], dp, 0)

    def cp_o(i, t):
        return remote(sendB.at[i, t * 32:(t + 1) * 32], outb.at[i], o_s.at[i, t], o_r.at[i], dp, t)

    def cp_lg(i, t):
        return remote(sendD.at[i, t * 32:(t + 1) * 32], lgb.at[i], lg_s.at[i, t - 1], lg_r.at[i], dp, t)

    def cp_du(i, t):
        return remote(
            X.at[5, at(i * SEQ + t * LAT, LAT, LAT)], dUb.at[i],
            du_s.at[i, t - 1], du_r.at[i], dp, t,
        )

    def cp_a(b):
        return remote(g.at[b, at((1 - c) * HALF, HALF, HALF)], rA.at[b], a_s.at[b], a_r.at[b], mate, s)

    def half_of(j, h):
        return at(c * HALF + lax.rem(r1 + j, N) * QUARTER + h * SIDE, SIDE, SIDE)

    def cp_rb(b, j):
        source, slot, lo, to = (
            (half_of(2, 0), 2, 0, 1), (half_of(2, 1), 2, 1, 3),
            (half_of(1, 1), 0, 1, 1), (half_of(3, 0), 1, 0, 3),
            (half_of(1, 0), 0, 0, 1), (half_of(3, 1), 1, 1, 3),
        )[j]
        return remote(
            g.at[b, source], rB.at[b, slot, lo * SIDE:(lo + 1) * SIDE],
            bb_s.at[b, j], bb_r.at[b, j], peer1(to), s,
        )

    def cp_rc(b, k):
        start = own_quarter + lax.rem(r2 + k, N) * PIECE
        return remote(
            g.at[b, at(start, PIECE, PIECE)], rC.at[b, k - 1],
            c_s.at[b, k - 1], c_r.at[b, k - 1], peer2(k), s,
        )

    class Gather:
        def __init__(self, view, own, sems):
            self.view, self.own, self.sems = view, own, sems

        def d(self, k):
            piece = self.own(r2 * PIECE, PIECE)
            return remote(piece, piece, self.sems[0].at[k - 1], self.sems[1].at[k - 1], peer2(k), s)

        def d_in(self, k):
            piece = self.own(lax.rem(r2 + N - k, N) * PIECE, PIECE)
            return remote(piece, piece, self.sems[0].at[k - 1], self.sems[1].at[k - 1], peer2(k), s)

        def e(self, j):
            if j < 2:
                src, dst = self.own(0, QUARTER), self.view(c, r1 * QUARTER, QUARTER)
            else:
                far = lax.rem(r1 + (3 if j == 2 else 1), N) * QUARTER + (j - 2) * SIDE
                src = dst = self.view(c, far, SIDE)
            return remote(
                src, dst, self.sems[2].at[j], self.sems[3].at[j], peer1(1 if j % 2 == 0 else 3), s
            )

        def e_in(self, j):
            if j < 2:
                dst = self.view(c, lax.rem(r1 + 3 - 2 * j, N) * QUARTER, QUARTER)
            else:
                dst = self.view(c, lax.rem(r1 + 2, N) * QUARTER + (j - 2) * SIDE, SIDE)
            return remote(dst, dst, self.sems[2].at[j], self.sems[3].at[j], peer1(1), s)

        def f(self):
            half = self.view(c, 0, HALF)
            return remote(half, half, self.sems[4], self.sems[5], mate, s)

        def f_in(self):
            half = self.view(1 - c, 0, HALF)
            return remote(half, half, self.sems[4], self.sems[5], mate, s)

        def e1(self):
            for j in (0, 1):
                self.e(j).start()

        def e2(self):
            for j in (0, 1):
                self.e_in(j).wait_recv()
                self.e(j + 2).start()

        def e_done(self):
            for j in (2, 3):
                self.e_in(j).wait_recv()

        def drain(self):
            for k in ring:
                self.d(k).wait_send()
            for j in range(4):
                self.e(j).wait_send()
            self.f().wait_send()

    def gather_f(half):
        def view(core, start, size):
            return Fd.at[half, at(core * HALF + start, size, 16)]
        return Gather(
            view, lambda start, size: view(c, r1 * QUARTER + start, size),
            (fd_s, fd_r, fe_s, fe_r, ff_s, ff_r),
        )

    def gather_w():
        def view(core, start, size):
            return Wb.at[at(start, size, 16), at(core * 2 * D, 2 * D, 2 * D)]
        return Gather(
            view, lambda start, size: view(c, r1 * QUARTER + start, size),
            (wd_s, wd_r, we_s, we_r, wf_s, wf_r),
        )

    def gather_g(b):
        def view(core, start, size):
            return g.at[b, at(core * HALF + start, size, 16)]
        return Gather(
            view, lambda start, size: q.at[b, at(start, size, 16)],
            (gd_s.at[b], gd_r.at[b], ge_s.at[b], ge_r.at[b], gf_s.at[b], gf_r.at[b]),
        )

    def stage_b(b):
        cp_a(b).wait_recv()
        for j in (2, 1, 3, 0):
            part = at(c * HALF + lax.rem(r1 + j, N) * QUARTER, QUARTER, QUARTER)
            other = at(lax.rem(r1 + j, N) * QUARTER, QUARTER, QUARTER)
            g[b, part] = (g[b, part].astype(F32) + rA[b, other].astype(F32)).astype(BF)
            if j == 2:
                cp_rb(b, 0).start()
                cp_rb(b, 1).start()
            elif j == 1:
                cp_rb(b, 2).start()
            elif j == 3:
                cp_rb(b, 3).start()

    local_raw().start()
    local_w().start()

    @pl.when(s != 0)
    def _():
        local_f().start()

    barrier = pltpu.get_barrier_semaphore()
    partners = [(dp, sec_of(k)) for k in (1, 2, 3)] + [(mate, s)]
    partners += [(peer1(k), s) for k in ring] + [(peer2(k), s) for k in ring]
    for partner in partners:
        pl.semaphore_signal(barrier, inc=1, device_id=partner, device_id_type=MESH)
    select = lax.broadcasted_iota(jnp.int32, (192, D), 1) == lax.broadcasted_iota(jnp.int32, (192, D), 0) + s * 192
    snorm = snorm_ref[0].astype(F32)
    gain = 1.0 + snorm[0:1]
    shift = snorm[1:2]
    inb[...] = jnp.zeros_like(inb)
    inb[0:2] = nn(inorm_ref[...], select.astype(F32).astype(BF))
    inb[2:4] = snorm
    nacc[...] = jnp.zeros_like(nacc)
    pl.semaphore_wait(barrier, len(partners))

    for k in (1, 2, 3):
        cp_in(k).start()

    @pl.when(s == 0)
    def _():
        local_lat().start()
        for i in range(3):
            local_tokens(i).start()

    @pl.when(s != 1)
    def _():
        cp_fx().start()

    @pl.when(s == 3)
    def _():
        cp_wx().start()

    for sec in (1, 2, 3):
        @pl.when(s == sec)
        def _():
            for i in range(3):
                cp_lat(i, sec).start()
                if sec == 2:
                    cp_via(i).start()
                cp_u(i, sec).start()

    @pl.when(s >= 2)
    def _():
        local_cot().start()

    for to in (2, 3):
        @pl.when(s != to)
        def _():
            cp_cot(s, to).start()

    def project(a, lo, hi):
        return nn(a, W[:, lo:hi])

    def latent_back(x_ref, i, da, db):
        dx, dg, dbias = ln_back(x_ref[i].astype(F32), da, gain)
        nacc[0:1] = nacc[0:1] + dg
        nacc[1:2] = nacc[1:2] + dbias
        return db.astype(F32) + dx

    local_w().wait()

    @pl.when(s == 0)
    def _():
        local_lat().wait()
        for k in (1, 2, 3):
            cp_in(k).wait_recv()
        in_all = inb[...] + inr[0] + inr[1] + inr[2]

        @pl.loop(0, 3)
        def _(i):
            for src in (1, 2, 3):
                cp_lat(i, src).wait_recv()
            x = xin[i].astype(F32)
            xhat, _ = unit(x)
            a = (xhat * gain + shift).astype(BF)
            lat_rows = rows(i, LAT)
            A[lat_rows] = a
            Q[lat_rows] = project(a, 0, D).astype(BF)
            for src in (1, 2, 3):
                cp_u(i, src).wait_recv()
            cp_on(i).wait_recv()
            local_tokens(i).wait()

            @pl.loop(0, 4)
            def _(j):
                part = at(i * SEQ + j * LAT, LAT, LAT)
                xhat, _ = unit(X[0, part].astype(F32))
                X[0, part] = (xhat * (1.0 + in_all[0:1]) + in_all[1:2]).astype(BF)
            u = X[0, rows(i, SEQ)]
            kv = [X.at[j, rows(i, SEQ)] for j in (1, 2)]
            kv[0][...] = project(u, D, 2 * D).astype(BF)
            kv[1][...] = project(u, 2 * D, 3 * D).astype(BF)
            where_ = lax.broadcasted_iota(jnp.int32, (SEQ, 256), 0)
            clip = jnp.zeros((SEQ, 256), jnp.int32)
            end = jnp.int32(0)
            for j in range(4):
                end = end + len_ref[i, j]
                clip = clip + (where_ >= end).astype(jnp.int32)
            ids = clip_ref[pl.ds(i, 1)]
            ids = jnp.concatenate([ids, ids], 1)
            attn_fwd(Q.at[lat_rows], kv[0], kv[1], clip == ids, PT.at[i], O.at[lat_rows])
            b = x + project(O[lat_rows], 3 * D, 4 * D)
            sendB[i] = b.astype(BF)
            cp_b(i, sendB).start()

        def send_du(i):
            at_rows = rows(i, SEQ)
            du = nt(X[3, at_rows], W[:, D:2 * D]) + nt(X[4, at_rows], W[:, 2 * D:3 * D])
            X[5, at_rows] = du.astype(BF)
            dUb[i] = X[5, at(i * SEQ, LAT, LAT)]
            for t in (1, 2, 3):
                cp_du(i, t).start()

        def latent_out(i):
            db = dBin[i]
            grad = latent_back(xin, i, nt(dQ[rows(i, LAT)], W[:, :D]), db).astype(BF)
            sendD[i] = grad
            lgb[i] = grad[0:32]
            for t in (1, 2, 3):
                cp_lg(i, t).start()

        def block_grad(b, tokens, latents):
            count = latents.stop - latents.start
            db = dBin[latents.start // LAT:latents.stop // LAT].reshape(count, D)
            if b == 0:
                return tn(A[latents], dQ[latents]), tn(X[0, tokens], X[3, tokens])
            return tn(X[0, tokens], X[4, tokens]), tn(O[latents], db)

        def item_back(i):
            cp_d(i).wait_recv()
            dO[...] = nt(dBin[i], W[:, 3 * D:]).astype(BF)
            kv = [X.at[j, rows(i, SEQ)] for j in (1, 2, 3, 4)]
            lat_rows = rows(i, LAT)
            attn_bwd(Q.at[lat_rows], kv[0], kv[1], PT.at[i], dO, dQ.at[lat_rows], kv[2], kv[3])

        @pl.loop(0, 2)
        def _(i):
            item_back(i)
            latent_out(i)

            @pl.when(i == 0)
            def _():
                send_du(0)

        def first_grads(b):
            upper, lower = block_grad(b, slice(0, 2 * SEQ), slice(0, 2 * LAT))
            g[b, 0:D] = upper.astype(BF)
            g[b, D:] = lower.astype(BF)

        def last_grads(b):
            upper, lower = block_grad(b, slice(2 * SEQ, 3 * SEQ), slice(2 * LAT, 3 * LAT))
            g[b, 0:D] = (g[b, 0:D].astype(F32) + upper).astype(BF)
            g[b, D:] = (g[b, D:].astype(F32) + lower).astype(BF)

        def down_grads():
            for blk in range(2):
                g[2, blk * D:(blk + 1) * D] = tn(
                    Fd[0, blk * 384:(blk + 1) * 384], Fd[1, 0:384]
                ).astype(BF)

        apart(first_grads, 0)
        apart(first_grads, 1)
        for t in range(3):
            cp_e(t).wait_recv()
            for blk in range(2):
                cp_gu(t, blk).wait_recv()
        apart(down_grads)
        cp_a(2).start()
        pl.loop(2, 2 + once)(item_back)
        apart(last_grads, 0)
        cp_a(0).start()
        apart(stage_b, 2)
        apart(last_grads, 1)
        cp_a(1).start()
        apart(stage_b, 0)
        pl.loop(2, 2 + once)(latent_out)
        pl.loop(1, 1 + once)(send_du)
        apart(stage_b, 1)
        pl.loop(2, 2 + once)(send_du)

    @pl.when(s == 2)
    def _():
        for k in (1, 2, 3):
            cp_in(k).wait_recv()
        far_gain = 1.0 + inr[2, 2:3]
        far_shift = inr[2, 3:4]
        w3, f3 = gather_w(), gather_f(1)
        cp_fx().wait_recv()
        cp_wx().wait_recv()
        for k in ring:
            w3.d(k).start()
            f3.d(k).start()
        for one in (w3, f3):
            for k in ring:
                one.d_in(k).wait_recv()
            one.e1()
        for one in (w3, f3):
            one.e2()
        for one in (w3, f3):
            one.e_done()
            one.f().start()
        local_f().wait()
        local_cot().wait()
        for src in (0, 1, 3):
            cp_cot(src, 2).wait_recv()
        for one in (w3, f3):
            one.f_in().wait_recv()

        @pl.loop(0, 3)
        def _(i):
            lat_rows = rows(i, LAT)
            cp_b(i, yin).wait_recv()
            x = xin[i].astype(F32)
            xhat, _ = unit(x)
            a = (xhat * gain + shift).astype(BF)
            A[lat_rows] = a
            Q[lat_rows] = project(a, 0, D).astype(BF)
            X[1, lat_rows] = project(a, D, 2 * D).astype(BF)
            X[2, lat_rows] = project(a, 2 * D, 3 * D).astype(BF)
            ids = jnp.broadcast_to(clip_ref[pl.ds(i, 1)].astype(F32), (LAT, LAT))
            mask = jnp.concatenate([ids, ids], 1) == jnp.concatenate([ids.T, ids.T], 1)
            attn_fwd(
                Q.at[lat_rows], X.at[1, lat_rows], X.at[2, lat_rows], mask,
                PT.at[i, :, 0:LAT], O.at[lat_rows],
            )
            middle = (x + project(O[lat_rows], 3 * D, 4 * D)).astype(BF)
            yin[i] = middle
            cp_b(i, yin).start()
            x = middle.astype(F32)
            xhat, _ = unit(x)
            a = (xhat * far_gain + far_shift).astype(BF)
            b = ffn_fwd(i, x, a, Wb, Fd, X, 2).astype(BF)
            sendB[i] = b
            outb[i] = b[64:96]
            for t in (0, 1, 3):
                cp_o(i, t).start()
            db = dBin[i]
            dx, _, _ = ln_back(x, ffn_bwd(i, db, Wb, Fd, X, False), far_gain)
            db = (db.astype(F32) + dx).astype(BF)
            dBm[i] = db
            dO[...] = nt(db, W[:, 3 * D:]).astype(BF)
            attn_bwd(
                Q.at[lat_rows], X.at[1, lat_rows], X.at[2, lat_rows], PT.at[i, :, 0:LAT],
                dO, dQ.at[lat_rows], X.at[3, lat_rows], X.at[4, lat_rows],
            )
            da = nt(dQ[lat_rows], W[:, :D]) + nt(X[3, lat_rows], W[:, D:2 * D])
            da = da + nt(X[4, lat_rows], W[:, 2 * D:3 * D])
            sendD[i] = latent_back(xin, i, da, db).astype(BF)
            cp_d(i).start()
            cp_e(i).start()

        def all_grads(b):
            if b == 2:
                db = dBin[...].reshape(3 * LAT, D)
                pair = tn(X[0, 0:384], db), tn(X[0, 384:768], db)
            elif b == 0:
                pair = tn(A[...], dQ[...]), tn(A[...], X[3, 0:3 * LAT])
            else:
                pair = tn(A[...], X[4, 0:3 * LAT]), tn(O[...], dBm[...].reshape(3 * LAT, D))
            g[b, 0:D] = pair[0].astype(BF)
            g[b, D:] = pair[1].astype(BF)

        for t, b in enumerate(ORDER):
            apart(all_grads, b)
            cp_a(b).start()
            if t > 0:
                apart(stage_b, ORDER[t - 1])
        apart(stage_b, ORDER[2])

    @pl.when(odd)
    def _():
        def relay_on(i):
            @pl.when(s == 1)
            def _():
                cp_via(i).wait_recv()
                cp_on(i).start()

        prior = gather_f(0)
        relay_on(0)
        cp_fx().wait_recv()
        for k in ring:
            prior.d(k).start()
        relay_on(1)
        for k in ring:
            prior.d_in(k).wait_recv()
        prior.e1()
        relay_on(2)
        prior.e2()
        prior.e_done()
        prior.f().start()
        local_f().wait()
        prior.f_in().wait_recv()

        @pl.when(s == 3)
        def _():
            local_cot().wait()
            for src in (0, 1, 2):
                cp_cot(src, 3).wait_recv()

        def block_grad(b, j, first, count):
            start = (2 + j if b == 2 else 2 * b + j) * 384
            here = slice(start + first * LAT, start + (first + count) * LAT)
            own = slice(first * LAT, (first + count) * LAT)
            if b == 2:
                return tn(X[0, here], dBin[first:first + count].reshape(count * LAT, D))
            return tn(A[own], X[1, here])

        def store_grads(b, first, count, add):
            for j in range(2):
                here = slice(j * D, (j + 1) * D)
                grad = block_grad(b, j, first, count)
                g[b, here] = ((g[b, here].astype(F32) + grad) if add else grad).astype(BF)

        def forward(i):
            cp_b(i, sendB).wait_recv()
            x = xin[i].astype(F32)
            xhat, _ = unit(x)
            a = (xhat * gain + shift).astype(BF)
            A[rows(i, LAT)] = a
            return ffn_fwd(i, x, a, W, Fd, X, 4).astype(BF)

        def backward(i):
            db = dBin[i]
            return latent_back(xin, i, ffn_bwd(i, db, W, Fd, X, True), db).astype(BF)

        @pl.when(s == 1)
        def _():
            @pl.loop(0, 3)
            def _(i):
                sendB[i] = forward(i)
                cp_b(i, sendB).start()
                for blk in range(2):
                    cp_gu(i, blk).start()

            def send_back(i):
                cp_d(i).wait_recv()
                sendD[i] = backward(i)
                cp_d(i).start()

            @pl.loop(0, 2)
            def _(i):
                send_back(i)
            for b in ORDER:
                apart(store_grads, b, 0, 2, False)
            pl.loop(2, 2 + once)(send_back)
            for t, b in enumerate(ORDER):
                apart(store_grads, b, 2, 1, True)
                cp_a(b).start()
                if t > 0:
                    apart(stage_b, ORDER[t - 1])

        @pl.when(s == 3)
        def _():
            @pl.loop(0, 3)
            def _(i):
                forward(i)
                backward(i)
            for t, b in enumerate(ORDER):
                apart(store_grads, b, 0, 3, False)
                cp_a(b).start()
                if t > 0:
                    apart(stage_b, ORDER[t - 1])
        apart(stage_b, ORDER[2])

    def sum_far(b):
        for j in (0, 1):
            cp_rb(b, j).wait_recv()
            mine = half_of(1 + 2 * j, j)
            arrived = rB[b, 2, j * SIDE:(j + 1) * SIDE].astype(F32)
            g[b, mine] = (g[b, mine].astype(F32) + arrived).astype(BF)
            cp_rb(b, 4 + j).start()

    def sum_quarter(b):
        for j in (2, 3, 4, 5):
            cp_rb(b, j).wait_recv()
        part = at(own_quarter, QUARTER, QUARTER)
        total = g[b, part].astype(F32) + rB[b, 0].astype(F32) + rB[b, 1].astype(F32)
        g[b, part] = total.astype(BF)
        for k in ring:
            cp_rc(b, k).start()

    def sum_piece(b):
        cp_a(b).wait_send()
        pl.semaphore_signal(free_a.at[b], inc=1, device_id=(mate, s), device_id_type=MESH)
        for j in range(6):
            cp_rb(b, j).wait_send()
        for k in (1, 3):
            pl.semaphore_signal(free_b.at[b], inc=1, device_id=(peer1(k), s), device_id_type=MESH)
        for k in ring:
            cp_rc(b, k).wait_recv()
        total = g[b, at(own_piece, PIECE, PIECE)].astype(F32)
        for k in ring:
            total = total + rC[b, k - 1].astype(F32)
        q[b, at(r2 * PIECE, PIECE, PIECE)] = total.astype(BF)
        for k in ring:
            gather_g(b).d(k).start()

    def spread_quarter(b):
        for k in ring:
            cp_rc(b, k).wait_send()
        pl.semaphore_wait(free_b.at[b], 2)
        for k in ring:
            gather_g(b).d_in(k).wait_recv()
        gather_g(b).e1()
        g[b, at(own_quarter, QUARTER, QUARTER)] = q[b]

    def spread_far(b):
        gather_g(b).e2()

    def leave(b, h):
        src = g.at[b, at(h * HALF, HALF, HALF)]
        if b == 2:
            return pltpu.make_async_copy(src, down_ref.at[0, at(h * HALF, HALF, HALF)], g_sem.at[b, h])
        return pltpu.make_async_copy(
            src, entry_ref.at[0, :, at((2 * b + h) * D, D, D)], g_sem.at[b, h]
        )

    def spread_half(b):
        gather_g(b).e_done()
        pl.semaphore_wait(free_a.at[b], 1)
        gather_g(b).f().start()
        leave(b, c).start()

    def finish(b):
        gather_g(b).f_in().wait_recv()
        leave(b, 1 - c).start()

    def small(step, buf, ss, rs, k, dp_to, sec_to):
        return remote(tsrc.at[step], buf.at[k], ss.at[k], rs.at[k], dp_to, sec_to)

    def own_rows():
        @pl.when((s == 1) | (s == 3))
        def _():
            for k in (1, 2, 3):
                cp_in(k).wait_recv()
        local_raw().wait()
        in_gain = 1.0 + inb[0:1] + inr[0, 0:1] + inr[1, 0:1] + inr[2, 0:1]

        @pl.loop(0, 3)
        def _(i):
            @pl.when(s != 2)
            def _():
                cp_o(i, 0).wait_recv()

            @pl.when(s != 0)
            def _():
                cp_lg(i, 1).wait_recv()
                cp_du(i, 1).wait_recv()
            dx, dg, dbias = ln_back(rawv[i].astype(F32), dUb[i].astype(F32), in_gain)
            igrad_ref[i] = dx
            nacc[2:3] = nacc[2:3] + dg
            nacc[3:4] = nacc[3:4] + dbias
            out_ref[i] = outb[i]
            lgrad_ref[i] = lgb[i]
        tsrc[0] = nacc[...]
        for k in (1, 2, 3):
            small(0, tX, tx_s, tx_r, k - 1, dp, sec_of(k)).start()

    def small_mate():
        for k in (1, 2, 3):
            small(0, tX, tx_s, tx_r, k - 1, dp, sec_of(k)).wait_recv()
        row = lax.broadcasted_iota(jnp.int32, (8, D), 0)
        own = tsrc[0]
        tsrc[1] = jnp.where(row < 2, own, own + tX[0] + tX[1] + tX[2])
        small(1, tC, tc_s, tc_r, 0, mate, s).start()

    def small_ring1():
        small(1, tC, tc_s, tc_r, 0, mate, s).wait_recv()
        tsrc[2] = tsrc[1] + tC[0]
        for k in ring:
            small(2, t1, t1_s, t1_r, k - 1, peer1(k), s).start()

    def small_ring2():
        for k in ring:
            small(2, t1, t1_s, t1_r, k - 1, peer1(k), s).wait_recv()
        tsrc[3] = tsrc[2] + t1[0] + t1[1] + t1[2]
        for k in ring:
            small(3, t2, t2_s, t2_r, k - 1, peer2(k), s).start()

    def small_done():
        for k in ring:
            small(3, t2, t2_s, t2_r, k - 1, peer2(k), s).wait_recv()
        tiny_ref[...] = tsrc[3] + t2[0] + t2[1] + t2[2]

    stages = (sum_far, sum_quarter, sum_piece, spread_quarter, spread_far, spread_half, finish)
    beside = {5: own_rows, 6: small_mate, 7: small_ring1, 8: small_ring2}
    for turn in range(len(stages) + 2):
        for t in range(3):
            if 0 <= turn - t < len(stages):
                apart(stages[turn - t], ORDER[t])
        if turn in beside:
            apart(beside[turn])
    small_done()
    for b in range(3):
        for h in range(2):
            leave(b, h).wait()

    for k in (1, 2, 3):
        cp_in(k).wait_send()
        small(0, tX, tx_s, tx_r, k - 1, dp, sec_of(k)).wait_send()
    small(1, tC, tc_s, tc_r, 0, mate, s).wait_send()
    for k in ring:
        small(2, t1, t1_s, t1_r, k - 1, peer1(k), s).wait_send()
        small(3, t2, t2_s, t2_r, k - 1, peer2(k), s).wait_send()
    for b in range(3):
        gather_g(b).drain()
    for to in (2, 3):
        @pl.when(s != to)
        def _():
            cp_cot(s, to).wait_send()

    for sec in range(4):
        @pl.when(s == sec)
        def _():
            if sec != 1:
                cp_fx().wait_send()
            if sec == 3:
                cp_wx().wait_send()
            if sec == 2:
                gather_w().drain()
                gather_f(1).drain()
            if sec in (1, 3):
                gather_f(0).drain()
            for i in range(3):
                if sec > 0:
                    cp_lat(i, sec).wait_send()
                    cp_u(i, sec).wait_send()
                if sec < 3:
                    cp_b(i, sendB).wait_send()
                if sec in (1, 2):
                    cp_via(i).wait_send()
                    cp_d(i).wait_send()
                if sec == 0:
                    for t in (1, 2, 3):
                        cp_lg(i, t).wait_send()
                        cp_du(i, t).wait_send()
                if sec == 1:
                    for blk in range(2):
                        cp_gu(i, blk).wait_send()
                if sec == 2:
                    cp_e(i).wait_send()
                    for t in (0, 1, 3):
                        cp_o(i, t).wait_send()


def widen(
    out_in, lgrad_in, igrad_in, entry_in, down_in, tiny_in,
    out_ref, lgrad_ref, igrad_ref, entry_ref, down_ref, norm_ref, in_norm_ref,
):
    igrad_ref[...] = igrad_in[...]
    entry_ref[...] = entry_in[...].astype(F32)
    down_ref[...] = down_in[...].astype(F32)

    @pl.when(pl.program_id(0) == 0)
    def _():
        out_ref[...] = out_in[...]
        lgrad_ref[...] = lgrad_in[...].astype(F32)
        norm_ref[...] = tiny_in[0:2]
        s = lax.axis_index("section")
        mine = jnp.zeros((2, 192), F32)
        for k in range(4):
            mine = jnp.where(s == k, tiny_in[2:4, k * 192:(k + 1) * 192], mine)
        in_norm_ref[...] = mine


def on_device(lat, raw, cot, lengths, clip, w, f, snorm, inorm):
    def low(*shape):
        return pltpu.VMEM(shape, BF)

    def full(*shape):
        return pltpu.VMEM(shape, F32)

    def sem(*shape):
        return pltpu.SemaphoreType.DMA(shape)

    def pair(*shape):
        return [sem(*shape), sem(*shape)]

    one = pltpu.SemaphoreType.DMA
    ring = N - 1
    scratch = [
        low(D, 4 * D), low(D, 4 * D), low(2, 2 * D, D), low(3, 2 * D, D), low(6, 2 * D, D),
        low(3, 6, SEQ, 256), low(3, HALF, D), low(3, 3, QUARTER, D), low(3, ring, PIECE, D), low(3, QUARTER, D),
        *[low(3, LAT, D)] * 6,
        *[low(3 * LAT, D)] * 4, low(LAT, D),
        low(3, LAT, D), low(3, VIA, D), low(3, LAT, D), low(3, 32, D), low(3, 32, D),
        full(8, D), full(3, 8, D), full(8, D), full(4, 8, D),
        full(3, 8, D), full(1, 8, D), full(ring, 8, D), full(ring, 8, D),
        sem(8), *pair(3), sem(3), sem(3, 3), sem(2), sem(4), sem(3), sem(3, 4), *pair(3), one, one, one, one,
        *pair(3), *pair(3), *pair(3), *pair(3, 2), sem(3, 4), sem(3), sem(3, 3), sem(3), sem(3, 3), sem(3),
        *pair(3), *pair(3, 6), *pair(3, ring), *pair(3, ring), *pair(3, 4), *pair(3),
        *pair(ring), *pair(4), one, one, *pair(ring), *pair(4), one, one,
        *pair(3), *pair(1), *pair(ring), *pair(ring), sem(3, 2),
        pltpu.SemaphoreType.REGULAR((3,)), pltpu.SemaphoreType.REGULAR((3,)),
    ]
    hbm = pl.BlockSpec(memory_space=pl.ANY)
    vmem = pl.BlockSpec(memory_space=pltpu.VMEM)
    inner = pl.pallas_call(
        kernel,
        name="layers",
        out_shape=(
            jax.ShapeDtypeStruct(lat.shape, BF),
            jax.ShapeDtypeStruct(lat.shape, BF),
            jax.ShapeDtypeStruct(raw.shape, F32),
            jax.ShapeDtypeStruct(w.shape, BF),
            jax.ShapeDtypeStruct(f.shape, BF),
            jax.ShapeDtypeStruct((8, D), F32),
        ),
        in_specs=[hbm, hbm, hbm, pl.BlockSpec(memory_space=pltpu.SMEM), vmem, hbm, hbm, vmem, vmem],
        out_specs=(vmem, vmem, vmem, hbm, hbm, vmem),
        scratch_shapes=scratch,
        compiler_params=pltpu.CompilerParams(
            collective_id=0, has_side_effects=True, vmem_limit_bytes=60 * 2**20
        ),
    )(lat, raw, cot, lengths, clip, w, f, snorm, inorm)
    steps = 6

    def by_rows(array):
        rest = array.shape[1:]
        return pl.BlockSpec((array.shape[0] // steps, *rest), lambda t: (t,) + (0,) * len(rest))

    def whole(*shape):
        return pl.BlockSpec(shape, lambda t: (0,) * len(shape))

    out, lgrad, igrad, entry, down, tiny = inner
    igrad = igrad.reshape(3 * LAT, D)
    entry, down = entry[0], down[0]
    final = pl.pallas_call(
        widen,
        name="widen",
        grid=(steps,),
        out_shape=(
            jax.ShapeDtypeStruct(lat.shape, BF),
            jax.ShapeDtypeStruct(lat.shape, F32),
            jax.ShapeDtypeStruct(igrad.shape, F32),
            jax.ShapeDtypeStruct(entry.shape, F32),
            jax.ShapeDtypeStruct(down.shape, F32),
            jax.ShapeDtypeStruct((2, D), F32),
            jax.ShapeDtypeStruct((2, 192), F32),
        ),
        in_specs=[
            whole(*lat.shape), whole(*lat.shape), by_rows(igrad), by_rows(entry), by_rows(down), whole(8, D)
        ],
        out_specs=(
            whole(*lat.shape), whole(*lat.shape), by_rows(igrad), by_rows(entry), by_rows(down),
            whole(2, D), whole(2, 192),
        ),
        compiler_params=pltpu.CompilerParams(vmem_limit_bytes=60 * 2**20),
    )(out, lgrad, igrad, entry, down, tiny)
    out, lgrad, igrad, entry, down, norm, in_norm = final
    return out, lgrad, igrad.reshape(raw.shape), entry[None], down[None], norm[None], in_norm


def solution(mesh):
    rows_split = P("dp", "section", None)
    weight = P("section", None, None)
    return jax.shard_map(
        on_device,
        mesh=mesh,
        in_specs=(
            rows_split, rows_split, rows_split, P("dp", None), P("dp", None),
            weight, weight, weight, P(None, "section"),
        ),
        out_specs=(rows_split, rows_split, rows_split, weight, weight, weight, P(None, "section")),
        check_vma=False,
    )
```

```python
import functools

import jax
import jax.numpy as jnp
from jax import lax
from jax.experimental import pallas as pl
from jax.experimental.pallas import tpu as pltpu
from jax.sharding import PartitionSpec as P


D = 768
LAT = 128
SEQ = 512
EPS = 1e-5
NEG = -1e9
F32 = jnp.float32
BF = jnp.bfloat16


def nn(a, b):
    return jnp.dot(a, b, preferred_element_type=F32)


def nt(a, b):
    return lax.dot_general(a, b, (((1,), (1,)), ((), ())), preferred_element_type=F32)


def tn(a, b):
    return lax.dot_general(a, b, (((0,), (0,)), ((), ())), preferred_element_type=F32)


def unit(x):
    mean = jnp.mean(x, -1, keepdims=True)
    cen = x - mean
    var = jnp.mean(cen * cen, -1, keepdims=True)
    rstd = lax.rsqrt(var + EPS)
    return cen * rstd, rstd


def ln_back(x, da, gain):
    xhat, rstd = unit(x)
    dx = da * gain
    m1 = jnp.mean(dx, -1, keepdims=True)
    m2 = jnp.mean(dx * xhat, -1, keepdims=True)
    grad = rstd * (dx - m1 - xhat * m2)
    return grad, jnp.sum(da * xhat, 0, keepdims=True), jnp.sum(da, 0, keepdims=True)


def gelu_pair(z):
    a = jnp.abs(z)
    t = 1.0 / (1.0 + (0.3275911 * 0.7071067811865476) * a)
    e = jnp.exp(-0.5 * (z * z))
    p = t * (0.254829592 + t * (-0.284496736 + t * (1.421413741 + t * (-1.453152027 + t * 1.061405429))))
    half = (0.5 * p) * e
    cdf = jnp.where(z >= 0, 1.0 - half, half)
    return z * cdf, cdf + z * (0.3989422804014327 * e)


def rows(i, n):
    return pl.ds(pl.multiple_of(i * n, n), n)


def ffn_fwd(i, x, a, W, Fd, X, kept):
    total = x
    for c in range(4):
        gate, slope = gelu_pair(nn(a, W[:, c * D:(c + 1) * D]))
        gate = gate.astype(BF)
        where_ = pl.ds(pl.multiple_of(c * 384 + i * LAT, LAT), LAT)
        if c < kept:
            X[0, where_] = gate
        X[5, where_] = slope.astype(BF)
        total = total + nn(gate, Fd[c // 2, (c % 2) * D:(c % 2 + 1) * D])
    return total


def ffn_bwd(i, db, W, Fd, X, kept):
    da = None
    for c in range(4):
        dg = nt(db, Fd[c // 2, (c % 2) * D:(c % 2 + 1) * D])
        where_ = pl.ds(pl.multiple_of(c * 384 + i * LAT, LAT), LAT)
        dz = (X[5, where_].astype(F32) * dg).astype(BF)
        if kept:
            X[1, where_] = dz
        part = nt(dz, W[:, c * D:(c + 1) * D])
        da = part if da is None else da + part
    return da


def halves(m):
    lane = lax.broadcasted_iota(jnp.int32, m.shape, 1)
    zero = jnp.zeros_like(m)
    return jnp.concatenate([jnp.where(lane < 64, m, zero), jnp.where(lane >= 64, m, zero)], 0)


def unhalves(mt):
    q = mt.shape[1] // 2
    return jnp.concatenate([mt[0:64, 0:q], mt[64:128, q:2 * q]], 0).T


def attn_fwd(q, k, v, maskf, PT, O):
    for p in range(6):
        cols = slice(p * 128, (p + 1) * 128)
        qs = halves(q[:, cols])
        s = nt(k[:, cols], qs) * 0.125
        s = jnp.where(maskf, s, NEG)
        m = jnp.max(s, 0, keepdims=True)
        e = jnp.exp(s - m)
        l = jnp.sum(e, 0, keepdims=True)
        pt = (e * (1.0 / l)).astype(BF)
        PT[p] = pt
        ot = tn(v[:, cols], pt)
        O[:, cols] = unhalves(ot).astype(BF)


def attn_bwd(q, k, v, PT, do, dq, dk, dv):
    for p in range(6):
        cols = slice(p * 128, (p + 1) * 128)
        dos = halves(do[:, cols])
        qs = halves(q[:, cols])
        pt = PT[p]
        dp = nt(v[:, cols], dos)
        ptf = pt.astype(F32)
        w = dp * ptf
        delta = jnp.sum(w, 0, keepdims=True)
        ds = (w - ptf * delta).astype(BF)
        dk[:, cols] = (nn(ds, qs) * 0.125).astype(BF)
        dv[:, cols] = nn(pt, dos).astype(BF)
        dqt = tn(k[:, cols], ds)
        dq[:, cols] = (unhalves(dqt) * 0.125).astype(BF)


HALF = 768
QUARTER = 192
PIECE = 48
SIDE = 96
VIA = 80
N = 4
MESH = pl.DeviceIdType.MESH


ORDER = (2, 0, 1)


def kernel(
    lat_ref, raw_ref, cot_ref, len_ref, clip_ref, w_ref, f_ref, snorm_ref, inorm_ref,
    out_ref, lgrad_ref, igrad_ref, entry_ref, down_ref, tiny_ref,
    W, Wb, Fd, g, X, PT, rA, rB, rC, q, xin, yin, dBin, dBm, sendB, sendD,
    A, Q, O, dQ, dO, relay, dUb, outb, lgb, inb, inr, nacc, tsrc, tX, tC, t1, t2,
    loc, in_s, in_r, lat_s, lat_r, cot_s, cot_r, u_s, u_r, via_s, via_r, fx_s, fx_r, wx_s, wx_r,
    b_s, b_r, d_s, d_r, e_s, e_r, gu_s, gu_r, o_s, o_r, lg_s, lg_r, du_s, du_r,
    a_s, a_r, bb_s, bb_r, c_s, c_r, gd_s, gd_r, ge_s, ge_r, gf_s, gf_r,
    fd_s, fd_r, fe_s, fe_r, ff_s, ff_r, wd_s, wd_r, we_s, we_r, wf_s, wf_r,
    tx_s, tx_r, tc_s, tc_r, t1_s, t1_r, t2_s, t2_r, g_sem, free_a, free_b,
):
    s = lax.axis_index("section")
    dp = lax.axis_index("dp")
    c = lax.rem(dp, 2)
    z = lax.rem(dp // 2, N)
    y = dp // (2 * N)
    odd = lax.rem(s, 2) == 1
    r1 = y * (1 - c) + z * c
    r2 = z * (1 - c) + y * c
    mate = dp + 1 - 2 * c
    ring = range(1, N)
    once = jnp.minimum(s + 1, 1)

    def apart(work, *args):
        @pl.loop(0, once)
        def _(_):
            work(*args)

    def sec_of(k):
        return lax.rem(s + k, 4)

    def peer1(k):
        other = lax.rem(r1 + k, N)
        return ((other * (1 - c) + y * c) * N + z * (1 - c) + other * c) * 2 + c

    def peer2(k):
        other = lax.rem(r2 + k, N)
        return ((y * (1 - c) + other * c) * N + other * (1 - c) + z * c) * 2 + c

    def at(start, size, unit_size):
        return pl.ds(pl.multiple_of(start, unit_size), size)

    def remote(src, dst, send_sem, recv_sem, dp_to, sec_to):
        return pltpu.make_async_remote_copy(
            src_ref=src, dst_ref=dst, send_sem=send_sem, recv_sem=recv_sem,
            device_id=(dp_to, sec_to), device_id_type=MESH,
        )

    def local_w():
        return pltpu.make_async_copy(w_ref.at[0], W, loc.at[0])

    def local_f():
        return pltpu.make_async_copy(f_ref.at[0], Fd.at[jnp.where(odd, 1, 0)], loc.at[1])

    def local_lat():
        return pltpu.make_async_copy(lat_ref, xin.at[:, at(s * 32, 32, 32)], loc.at[3])

    def local_cot():
        return pltpu.make_async_copy(cot_ref, dBin.at[:, at(s * 32, 32, 32)], loc.at[4])

    def local_tokens(i):
        return pltpu.make_async_copy(raw_ref.at[i], X.at[5, at(i * SEQ, LAT, LAT)], loc.at[5 + i])

    def cp_in(k):
        return remote(inb, inr.at[k - 1], in_s.at[k - 1], in_r.at[k - 1], dp, sec_of(k))

    def cp_lat(i, src):
        return remote(
            lat_ref.at[i], xin.at[i, at(src * 32, 32, 32)],
            lat_s.at[i], lat_r.at[i, src - 1], dp, 0,
        )

    def cp_cot(src, to):
        return remote(
            cot_ref, dBin.at[:, at(src * 32, 32, 32)], cot_s.at[to - 2], cot_r.at[src], dp, to
        )

    def cp_u(i, src):
        count = LAT - VIA if src == 2 else LAT
        return remote(
            raw_ref.at[i, 0:count], X.at[5, at(i * SEQ + src * LAT, count, 16)],
            u_s.at[i], u_r.at[i, src - 1], dp, 0,
        )

    def cp_via(i):
        return remote(raw_ref.at[i, LAT - VIA:LAT], relay.at[i], via_s.at[i], via_r.at[i], dp, 1)

    def cp_on(i):
        return remote(
            relay.at[i], X.at[5, at(i * SEQ + 3 * LAT - VIA, VIA, 16)],
            via_s.at[i], u_r.at[i, 3], dp, 0,
        )

    own_quarter = c * HALF + r1 * QUARTER
    own_piece = own_quarter + r2 * PIECE

    def cp_fx():
        where_ = at(own_piece, PIECE, PIECE)
        to = jnp.where(s == 3, 2, jnp.minimum(s + 1, 3))
        return remote(
            f_ref.at[0, where_], Fd.at[jnp.where(s == 3, 1, 0), where_], fx_s, fx_r, dp, to
        )

    def cp_wx():
        rows_ = at(r1 * QUARTER + r2 * PIECE, PIECE, PIECE)
        cols = at(c * 2 * D, 2 * D, 2 * D)
        return remote(w_ref.at[0, rows_, cols], Wb.at[rows_, cols], wx_s, wx_r, dp, 2)

    def cp_b(i, src):
        return remote(src.at[i], xin.at[i], b_s.at[i], b_r.at[i], dp, jnp.minimum(s + 1, 3))

    def cp_d(i):
        return remote(sendD.at[i], dBin.at[i], d_s.at[i], d_r.at[i], dp, jnp.maximum(s - 1, 0))

    def cp_e(i):
        return remote(sendD.at[i], Fd.at[1, at(i * LAT, LAT, LAT)], e_s.at[i], e_r.at[i], dp, 0)

    def cp_gu(i, blk):
        where_ = at(blk * 384 + i * LAT, LAT, LAT)
        return remote(X.at[0, where_], Fd.at[0, where_], gu_s.at[i, blk], gu_r.at[i, blk], dp, 0)

    def cp_o(i, t):
        return remote(sendB.at[i, t * 32:(t + 1) * 32], outb.at[i], o_s.at[i, t], o_r.at[i], dp, t)

    def cp_lg(i, t):
        return remote(sendD.at[i, t * 32:(t + 1) * 32], lgb.at[i], lg_s.at[i, t - 1], lg_r.at[i], dp, t)

    def cp_du(i, t):
        return remote(
            X.at[5, at(i * SEQ + t * LAT, LAT, LAT)], dUb.at[i],
            du_s.at[i, t - 1], du_r.at[i], dp, t,
        )

    def cp_a(b):
        return remote(g.at[b, at((1 - c) * HALF, HALF, HALF)], rA.at[b], a_s.at[b], a_r.at[b], mate, s)

    def half_of(j, h):
        return at(c * HALF + lax.rem(r1 + j, N) * QUARTER + h * SIDE, SIDE, SIDE)

    def cp_rb(b, j):
        source, slot, lo, to = (
            (half_of(2, 0), 2, 0, 1), (half_of(2, 1), 2, 1, 3),
            (half_of(1, 1), 0, 1, 1), (half_of(3, 0), 1, 0, 3),
            (half_of(1, 0), 0, 0, 1), (half_of(3, 1), 1, 1, 3),
        )[j]
        return remote(
            g.at[b, source], rB.at[b, slot, lo * SIDE:(lo + 1) * SIDE],
            bb_s.at[b, j], bb_r.at[b, j], peer1(to), s,
        )

    def cp_rc(b, k):
        start = own_quarter + lax.rem(r2 + k, N) * PIECE
        return remote(
            g.at[b, at(start, PIECE, PIECE)], rC.at[b, k - 1],
            c_s.at[b, k - 1], c_r.at[b, k - 1], peer2(k), s,
        )

    class Gather:
        def __init__(self, view, own, sems):
            self.view, self.own, self.sems = view, own, sems

        def d(self, k):
            piece = self.own(r2 * PIECE, PIECE)
            return remote(piece, piece, self.sems[0].at[k - 1], self.sems[1].at[k - 1], peer2(k), s)

        def d_in(self, k):
            piece = self.own(lax.rem(r2 + N - k, N) * PIECE, PIECE)
            return remote(piece, piece, self.sems[0].at[k - 1], self.sems[1].at[k - 1], peer2(k), s)

        def e(self, j):
            if j < 2:
                src, dst = self.own(0, QUARTER), self.view(c, r1 * QUARTER, QUARTER)
            else:
                far = lax.rem(r1 + (3 if j == 2 else 1), N) * QUARTER + (j - 2) * SIDE
                src = dst = self.view(c, far, SIDE)
            return remote(
                src, dst, self.sems[2].at[j], self.sems[3].at[j], peer1(1 if j % 2 == 0 else 3), s
            )

        def e_in(self, j):
            if j < 2:
                dst = self.view(c, lax.rem(r1 + 3 - 2 * j, N) * QUARTER, QUARTER)
            else:
                dst = self.view(c, lax.rem(r1 + 2, N) * QUARTER + (j - 2) * SIDE, SIDE)
            return remote(dst, dst, self.sems[2].at[j], self.sems[3].at[j], peer1(1), s)

        def f(self):
            half = self.view(c, 0, HALF)
            return remote(half, half, self.sems[4], self.sems[5], mate, s)

        def f_in(self):
            half = self.view(1 - c, 0, HALF)
            return remote(half, half, self.sems[4], self.sems[5], mate, s)

        def e1(self):
            for j in (0, 1):
                self.e(j).start()

        def e2(self):
            for j in (0, 1):
                self.e_in(j).wait_recv()
                self.e(j + 2).start()

        def e_done(self):
            for j in (2, 3):
                self.e_in(j).wait_recv()

        def drain(self):
            for k in ring:
                self.d(k).wait_send()
            for j in range(4):
                self.e(j).wait_send()
            self.f().wait_send()

    def gather_f(half):
        def view(core, start, size):
            return Fd.at[half, at(core * HALF + start, size, 16)]
        return Gather(
            view, lambda start, size: view(c, r1 * QUARTER + start, size),
            (fd_s, fd_r, fe_s, fe_r, ff_s, ff_r),
        )

    def gather_w():
        def view(core, start, size):
            return Wb.at[at(start, size, 16), at(core * 2 * D, 2 * D, 2 * D)]
        return Gather(
            view, lambda start, size: view(c, r1 * QUARTER + start, size),
            (wd_s, wd_r, we_s, we_r, wf_s, wf_r),
        )

    def gather_g(b):
        def view(core, start, size):
            return g.at[b, at(core * HALF + start, size, 16)]
        return Gather(
            view, lambda start, size: q.at[b, at(start, size, 16)],
            (gd_s.at[b], gd_r.at[b], ge_s.at[b], ge_r.at[b], gf_s.at[b], gf_r.at[b]),
        )

    def stage_b(b):
        cp_a(b).wait_recv()
        for j in (2, 1, 3, 0):
            part = at(c * HALF + lax.rem(r1 + j, N) * QUARTER, QUARTER, QUARTER)
            other = at(lax.rem(r1 + j, N) * QUARTER, QUARTER, QUARTER)
            g[b, part] = (g[b, part].astype(F32) + rA[b, other].astype(F32)).astype(BF)
            if j == 2:
                cp_rb(b, 0).start()
                cp_rb(b, 1).start()
            elif j == 1:
                cp_rb(b, 2).start()
            elif j == 3:
                cp_rb(b, 3).start()

    def sum_far(b):
        for j in (0, 1):
            cp_rb(b, j).wait_recv()
            mine = half_of(1 + 2 * j, j)
            arrived = rB[b, 2, j * SIDE:(j + 1) * SIDE].astype(F32)
            g[b, mine] = (g[b, mine].astype(F32) + arrived).astype(BF)
            cp_rb(b, 4 + j).start()

    def sum_quarter(b):
        for j in (2, 3, 4, 5):
            cp_rb(b, j).wait_recv()
        part = at(own_quarter, QUARTER, QUARTER)
        total = g[b, part].astype(F32) + rB[b, 0].astype(F32) + rB[b, 1].astype(F32)
        g[b, part] = total.astype(BF)
        for k in ring:
            cp_rc(b, k).start()

    def sum_piece(b):
        cp_a(b).wait_send()
        pl.semaphore_signal(free_a.at[b], inc=1, device_id=(mate, s), device_id_type=MESH)
        for j in range(6):
            cp_rb(b, j).wait_send()
        for k in (1, 3):
            pl.semaphore_signal(free_b.at[b], inc=1, device_id=(peer1(k), s), device_id_type=MESH)
        for k in ring:
            cp_rc(b, k).wait_recv()
        total = g[b, at(own_piece, PIECE, PIECE)].astype(F32)
        for k in ring:
            total = total + rC[b, k - 1].astype(F32)
        q[b, at(r2 * PIECE, PIECE, PIECE)] = total.astype(BF)
        for k in ring:
            gather_g(b).d(k).start()

    local_w().start()

    @pl.when(s != 0)
    def _():
        local_f().start()

    barrier = pltpu.get_barrier_semaphore()
    partners = [(dp, sec_of(k)) for k in (1, 2, 3)] + [(mate, s)]
    partners += [(peer1(k), s) for k in ring] + [(peer2(k), s) for k in ring]
    for partner in partners:
        pl.semaphore_signal(barrier, inc=1, device_id=partner, device_id_type=MESH)
    select = lax.broadcasted_iota(jnp.int32, (192, D), 1) == lax.broadcasted_iota(jnp.int32, (192, D), 0) + s * 192
    snorm = snorm_ref[0].astype(F32)
    gain = 1.0 + snorm[0:1]
    shift = snorm[1:2]
    inb[...] = jnp.zeros_like(inb)
    inb[0:2] = nn(inorm_ref[...], select.astype(F32).astype(BF))
    inb[2:4] = snorm
    nacc[...] = jnp.zeros_like(nacc)
    pl.semaphore_wait(barrier, len(partners))

    for k in (1, 2, 3):
        cp_in(k).start()

    @pl.when(s == 0)
    def _():
        local_lat().start()
        for i in range(3):
            local_tokens(i).start()

    @pl.when(s != 1)
    def _():
        cp_fx().start()

    @pl.when(s == 3)
    def _():
        cp_wx().start()

    for sec in (1, 2, 3):
        @pl.when(s == sec)
        def _():
            for i in range(3):
                cp_lat(i, sec).start()
                if sec == 2:
                    cp_via(i).start()
                cp_u(i, sec).start()

    @pl.when(s >= 2)
    def _():
        local_cot().start()

    for to in (2, 3):
        @pl.when(s != to)
        def _():
            cp_cot(s, to).start()

    def project(a, lo, hi):
        return nn(a, W[:, lo:hi])

    def latent_back(x_ref, i, da, db):
        dx, dg, dbias = ln_back(x_ref[i].astype(F32), da, gain)
        nacc[0:1] = nacc[0:1] + dg
        nacc[1:2] = nacc[1:2] + dbias
        return db.astype(F32) + dx

    local_w().wait()

    def send_du(i):
        in_gain = 1.0 + inb[0:1] + inr[0, 0:1] + inr[1, 0:1] + inr[2, 0:1]
        at_rows = rows(i, SEQ)
        du = nt(X[3, at_rows], W[:, D:2 * D]) + nt(X[4, at_rows], W[:, 2 * D:3 * D])
        X[1, at_rows] = du.astype(BF)

        @pl.loop(0, 4)
        def _(j):
            part = at(i * SEQ + j * LAT, LAT, LAT)
            dx, dg, dbias = ln_back(X[5, part].astype(F32), X[1, part].astype(F32), in_gain)
            X[5, part] = dx.astype(BF)
            nacc[2:3] = nacc[2:3] + dg
            nacc[3:4] = nacc[3:4] + dbias
        dUb[i] = X[5, at(i * SEQ, LAT, LAT)]
        for t in (1, 2, 3):
            cp_du(i, t).start()

    @pl.when(s == 0)
    def _():
        local_lat().wait()
        for k in (1, 2, 3):
            cp_in(k).wait_recv()
        in_all = inb[...] + inr[0] + inr[1] + inr[2]

        @pl.loop(0, 3)
        def _(i):
            for src in (1, 2, 3):
                cp_lat(i, src).wait_recv()
            x = xin[i].astype(F32)
            xhat, _ = unit(x)
            a = (xhat * gain + shift).astype(BF)
            lat_rows = rows(i, LAT)
            A[lat_rows] = a
            Q[lat_rows] = project(a, 0, D).astype(BF)
            for src in (1, 2, 3):
                cp_u(i, src).wait_recv()
            cp_on(i).wait_recv()
            local_tokens(i).wait()

            @pl.loop(0, 4)
            def _(j):
                part = at(i * SEQ + j * LAT, LAT, LAT)
                xhat, _ = unit(X[5, part].astype(F32))
                X[0, part] = (xhat * (1.0 + in_all[0:1]) + in_all[1:2]).astype(BF)
            u = X[0, rows(i, SEQ)]
            kv = [X.at[j, rows(i, SEQ)] for j in (1, 2)]
            kv[0][...] = project(u, D, 2 * D).astype(BF)
            kv[1][...] = project(u, 2 * D, 3 * D).astype(BF)
            where_ = lax.broadcasted_iota(jnp.int32, (SEQ, 256), 0)
            clip = jnp.zeros((SEQ, 256), jnp.int32)
            end = jnp.int32(0)
            for j in range(4):
                end = end + len_ref[i, j]
                clip = clip + (where_ >= end).astype(jnp.int32)
            ids = clip_ref[pl.ds(i, 1)]
            ids = jnp.concatenate([ids, ids], 1)
            attn_fwd(Q.at[lat_rows], kv[0], kv[1], clip == ids, PT.at[i], O.at[lat_rows])
            b = x + project(O[lat_rows], 3 * D, 4 * D)
            sendB[i] = b.astype(BF)
            cp_b(i, sendB).start()

        def latent_out(i):
            db = dBin[i]
            grad = latent_back(xin, i, nt(dQ[rows(i, LAT)], W[:, :D]), db).astype(BF)
            sendD[i] = grad
            lgb[i] = grad[0:32]
            for t in (1, 2, 3):
                cp_lg(i, t).start()

        def block_grad(b, tokens, latents):
            count = latents.stop - latents.start
            db = dBin[latents.start // LAT:latents.stop // LAT].reshape(count, D)
            if b == 0:
                return tn(A[latents], dQ[latents]), tn(X[0, tokens], X[3, tokens])
            return tn(X[0, tokens], X[4, tokens]), tn(O[latents], db)

        def item_back(i):
            cp_d(i).wait_recv()
            dO[...] = nt(dBin[i], W[:, 3 * D:]).astype(BF)
            kv = [X.at[j, rows(i, SEQ)] for j in (1, 2, 3, 4)]
            lat_rows = rows(i, LAT)
            attn_bwd(Q.at[lat_rows], kv[0], kv[1], PT.at[i], dO, dQ.at[lat_rows], kv[2], kv[3])

        @pl.loop(0, 2)
        def _(i):
            item_back(i)
            latent_out(i)

            @pl.when(i == 0)
            def _():
                send_du(0)

        def first_grads(b):
            upper, lower = block_grad(b, slice(0, 2 * SEQ), slice(0, 2 * LAT))
            g[b, 0:D] = upper.astype(BF)
            g[b, D:] = lower.astype(BF)

        def last_grads(b):
            upper, lower = block_grad(b, slice(2 * SEQ, 3 * SEQ), slice(2 * LAT, 3 * LAT))
            g[b, 0:D] = (g[b, 0:D].astype(F32) + upper).astype(BF)
            g[b, D:] = (g[b, D:].astype(F32) + lower).astype(BF)

        def down_grads():
            for blk in range(2):
                g[2, blk * D:(blk + 1) * D] = tn(
                    Fd[0, blk * 384:(blk + 1) * 384], Fd[1, 0:384]
                ).astype(BF)

        for t in range(3):
            cp_e(t).wait_recv()
            for blk in range(2):
                cp_gu(t, blk).wait_recv()
        apart(down_grads)
        cp_a(2).start()
        apart(first_grads, 0)
        apart(first_grads, 1)
        apart(stage_b, 2)
        pl.loop(2, 2 + once)(item_back)
        apart(last_grads, 0)
        cp_a(0).start()
        apart(last_grads, 1)
        cp_a(1).start()
        pl.loop(2, 2 + once)(latent_out)

    @pl.when(s == 2)
    def _():
        for k in (1, 2, 3):
            cp_in(k).wait_recv()
        far_gain = 1.0 + inr[2, 2:3]
        far_shift = inr[2, 3:4]
        w3, f3 = gather_w(), gather_f(1)
        cp_fx().wait_recv()
        cp_wx().wait_recv()
        for k in ring:
            w3.d(k).start()
            f3.d(k).start()
        for one in (w3, f3):
            for k in ring:
                one.d_in(k).wait_recv()
            one.e1()
        for one in (w3, f3):
            one.e2()
        for one in (w3, f3):
            one.e_done()
            one.f().start()
        local_f().wait()
        local_cot().wait()
        for src in (0, 1, 3):
            cp_cot(src, 2).wait_recv()
        for one in (w3, f3):
            one.f_in().wait_recv()

        @pl.loop(0, 3)
        def _(i):
            lat_rows = rows(i, LAT)
            cp_b(i, yin).wait_recv()
            x = xin[i].astype(F32)
            xhat, _ = unit(x)
            a = (xhat * gain + shift).astype(BF)
            A[lat_rows] = a
            Q[lat_rows] = project(a, 0, D).astype(BF)
            X[1, lat_rows] = project(a, D, 2 * D).astype(BF)
            X[2, lat_rows] = project(a, 2 * D, 3 * D).astype(BF)
            ids = jnp.broadcast_to(clip_ref[pl.ds(i, 1)].astype(F32), (LAT, LAT))
            mask = jnp.concatenate([ids, ids], 1) == jnp.concatenate([ids.T, ids.T], 1)
            attn_fwd(
                Q.at[lat_rows], X.at[1, lat_rows], X.at[2, lat_rows], mask,
                PT.at[i, :, 0:LAT], O.at[lat_rows],
            )
            middle = (x + project(O[lat_rows], 3 * D, 4 * D)).astype(BF)
            yin[i] = middle
            cp_b(i, yin).start()
            x = middle.astype(F32)
            xhat, _ = unit(x)
            a = (xhat * far_gain + far_shift).astype(BF)
            b = ffn_fwd(i, x, a, Wb, Fd, X, 2).astype(BF)
            sendB[i] = b
            outb[i] = b[64:96]
            for t in (0, 1, 3):
                cp_o(i, t).start()
            db = dBin[i]
            dx, _, _ = ln_back(x, ffn_bwd(i, db, Wb, Fd, X, False), far_gain)
            db = (db.astype(F32) + dx).astype(BF)
            dBm[i] = db
            dO[...] = nt(db, W[:, 3 * D:]).astype(BF)
            attn_bwd(
                Q.at[lat_rows], X.at[1, lat_rows], X.at[2, lat_rows], PT.at[i, :, 0:LAT],
                dO, dQ.at[lat_rows], X.at[3, lat_rows], X.at[4, lat_rows],
            )
            da = nt(dQ[lat_rows], W[:, :D]) + nt(X[3, lat_rows], W[:, D:2 * D])
            da = da + nt(X[4, lat_rows], W[:, 2 * D:3 * D])
            sendD[i] = latent_back(xin, i, da, db).astype(BF)
            cp_d(i).start()
            cp_e(i).start()

        def all_grads(b):
            if b == 2:
                db = dBin[...].reshape(3 * LAT, D)
                pair = tn(X[0, 0:384], db), tn(X[0, 384:768], db)
            elif b == 0:
                pair = tn(A[...], dQ[...]), tn(A[...], X[3, 0:3 * LAT])
            else:
                pair = tn(A[...], X[4, 0:3 * LAT]), tn(O[...], dBm[...].reshape(3 * LAT, D))
            g[b, 0:D] = pair[0].astype(BF)
            g[b, D:] = pair[1].astype(BF)

        for b in ORDER:
            apart(all_grads, b)
            cp_a(b).start()

    @pl.when(odd)
    def _():
        def relay_on(i):
            @pl.when(s == 1)
            def _():
                cp_via(i).wait_recv()
                cp_on(i).start()

        prior = gather_f(0)
        relay_on(0)
        cp_fx().wait_recv()
        for k in ring:
            prior.d(k).start()
        relay_on(1)
        for k in ring:
            prior.d_in(k).wait_recv()
        prior.e1()
        relay_on(2)
        prior.e2()
        prior.e_done()
        prior.f().start()
        local_f().wait()
        prior.f_in().wait_recv()

        @pl.when(s == 3)
        def _():
            local_cot().wait()
            for src in (0, 1, 2):
                cp_cot(src, 3).wait_recv()

        def block_grad(b, j, first, count):
            start = (2 + j if b == 2 else 2 * b + j) * 384
            here = slice(start + first * LAT, start + (first + count) * LAT)
            own = slice(first * LAT, (first + count) * LAT)
            if b == 2:
                return tn(X[0, here], dBin[first:first + count].reshape(count * LAT, D))
            return tn(A[own], X[1, here])

        def store_grads(b, first, count, add):
            for j in range(2):
                here = slice(j * D, (j + 1) * D)
                grad = block_grad(b, j, first, count)
                g[b, here] = ((g[b, here].astype(F32) + grad) if add else grad).astype(BF)

        def forward(i):
            cp_b(i, sendB).wait_recv()
            x = xin[i].astype(F32)
            xhat, _ = unit(x)
            a = (xhat * gain + shift).astype(BF)
            A[rows(i, LAT)] = a
            return ffn_fwd(i, x, a, W, Fd, X, 4).astype(BF)

        def backward(i):
            db = dBin[i]
            return latent_back(xin, i, ffn_bwd(i, db, W, Fd, X, True), db).astype(BF)

        @pl.when(s == 1)
        def _():
            @pl.loop(0, 3)
            def _(i):
                sendB[i] = forward(i)
                cp_b(i, sendB).start()
                for blk in range(2):
                    cp_gu(i, blk).start()

            def send_back(i):
                cp_d(i).wait_recv()
                sendD[i] = backward(i)
                cp_d(i).start()

            @pl.loop(0, 2)
            def _(i):
                send_back(i)
            for b in ORDER:
                apart(store_grads, b, 0, 2, False)
            pl.loop(2, 2 + once)(send_back)
            for b in ORDER:
                apart(store_grads, b, 2, 1, True)
                cp_a(b).start()

        @pl.when(s == 3)
        def _():
            @pl.loop(0, 3)
            def _(i):
                forward(i)
                backward(i)
            for b in ORDER:
                apart(store_grads, b, 0, 3, False)
                cp_a(b).start()

    def spread_quarter(b):
        for k in ring:
            cp_rc(b, k).wait_send()
        pl.semaphore_wait(free_b.at[b], 2)
        for k in ring:
            gather_g(b).d_in(k).wait_recv()
        gather_g(b).e1()
        g[b, at(own_quarter, QUARTER, QUARTER)] = q[b]

    def spread_far(b):
        gather_g(b).e2()

    def leave(b, h, act):
        src = g.at[b, at(h * HALF, HALF, HALF)]

        @pl.when(b == 2)
        def _():
            act(pltpu.make_async_copy(src, down_ref.at[0, at(h * HALF, HALF, HALF)], g_sem.at[b, h]))

        @pl.when(b < 2)
        def _():
            block = at(jnp.minimum(2 * b + h, 3) * D, D, D)
            act(pltpu.make_async_copy(src, entry_ref.at[0, :, block], g_sem.at[b, h]))

    def spread_half(b):
        gather_g(b).e_done()
        pl.semaphore_wait(free_a.at[b], 1)
        gather_g(b).f().start()
        leave(b, c, lambda copy: copy.start())

    def finish(b):
        gather_g(b).f_in().wait_recv()
        leave(b, 1 - c, lambda copy: copy.start())

    def small(step, buf, ss, rs, k, dp_to, sec_to):
        return remote(tsrc.at[step], buf.at[k], ss.at[k], rs.at[k], dp_to, sec_to)

    def own_rows():
        @pl.when((s == 1) | (s == 3))
        def _():
            for k in (1, 2, 3):
                cp_in(k).wait_recv()

        @pl.loop(0, 3)
        def _(i):
            @pl.when(s != 2)
            def _():
                cp_o(i, 0).wait_recv()

            @pl.when(s != 0)
            def _():
                cp_lg(i, 1).wait_recv()
                cp_du(i, 1).wait_recv()
            igrad_ref[i] = dUb[i]
            out_ref[i] = outb[i]
            lgrad_ref[i] = lgb[i]

    def small_x(k):
        return remote(tsrc.at[0], tX.at[0], tx_s.at[k - 1], tx_r.at[0], dp, sec_of(k))

    def small_mate():
        tsrc[1] = nacc[...]
        small(1, tC, tc_s, tc_r, 0, mate, s).start()

    def small_ring1():
        small(1, tC, tc_s, tc_r, 0, mate, s).wait_recv()
        tsrc[2] = tsrc[1] + tC[0]
        for k in ring:
            small(2, t1, t1_s, t1_r, k - 1, peer1(k), s).start()

    def small_ring2():
        for k in ring:
            small(2, t1, t1_s, t1_r, k - 1, peer1(k), s).wait_recv()
        tsrc[3] = tsrc[2] + t1[0] + t1[1] + t1[2]
        for k in ring:
            small(3, t2, t2_s, t2_r, k - 1, peer2(k), s).start()

    def small_out():
        for k in ring:
            small(3, t2, t2_s, t2_r, k - 1, peer2(k), s).wait_recv()
        total = tsrc[3] + t2[0] + t2[1] + t2[2]
        tsrc[0] = total
        tiny_ref[...] = total

        @pl.when(s == 0)
        def _():
            for k in (1, 2, 3):
                small_x(k).start()

    def small_done():
        @pl.when(s != 0)
        def _():
            small_x(1).wait_recv()
            tiny_ref[2:4] = tX[0, 2:4]

    stages = (
        stage_b, sum_far, sum_quarter, sum_piece, spread_quarter, spread_far, spread_half, finish
    )

    @pl.loop(0, len(stages) + 2)
    def _(turn):
        for k, stage in enumerate(stages):
            t = turn - k
            due = (t >= 0) & (t < 3)
            if k == 0:
                due = due & ((s != 0) | (t > 0))
            pl.when(due)(functools.partial(stage, lax.rem(t + 2, 3)))

        @pl.when((s == 0) & (turn > 0) & (turn < 3))
        def _():
            send_du(turn)
        for k, step in ((4, small_mate), (5, small_ring1), (6, small_ring2), (8, small_out)):
            pl.when(turn == k)(step)
    apart(own_rows)
    small_done()

    @pl.loop(0, 3)
    def _(b):
        for h in range(2):
            leave(b, h, lambda copy: copy.wait())

    for k in (1, 2, 3):
        cp_in(k).wait_send()
    small(1, tC, tc_s, tc_r, 0, mate, s).wait_send()
    for k in ring:
        small(2, t1, t1_s, t1_r, k - 1, peer1(k), s).wait_send()
        small(3, t2, t2_s, t2_r, k - 1, peer2(k), s).wait_send()
    pl.loop(0, 3)(lambda b: gather_g(b).drain())
    for to in (2, 3):
        @pl.when(s != to)
        def _():
            cp_cot(s, to).wait_send()

    for sec in range(4):
        @pl.when(s == sec)
        def _():
            if sec != 1:
                cp_fx().wait_send()
            if sec == 3:
                cp_wx().wait_send()
            if sec == 2:
                gather_w().drain()
                gather_f(1).drain()
            if sec in (1, 3):
                gather_f(0).drain()
            for i in range(3):
                if sec > 0:
                    cp_lat(i, sec).wait_send()
                    cp_u(i, sec).wait_send()
                if sec < 3:
                    cp_b(i, sendB).wait_send()
                if sec in (1, 2):
                    cp_via(i).wait_send()
                    cp_d(i).wait_send()
                if sec == 0 and i == 0:
                    for k in (1, 2, 3):
                        small_x(k).wait_send()
                if sec == 0:
                    for t in (1, 2, 3):
                        cp_lg(i, t).wait_send()
                        cp_du(i, t).wait_send()
                if sec == 1:
                    for blk in range(2):
                        cp_gu(i, blk).wait_send()
                if sec == 2:
                    cp_e(i).wait_send()
                    for t in (0, 1, 3):
                        cp_o(i, t).wait_send()


def widen(
    out_in, lgrad_in, igrad_in, entry_in, down_in, tiny_in,
    out_ref, lgrad_ref, igrad_ref, entry_ref, down_ref, norm_ref, in_norm_ref,
):
    igrad_ref[...] = igrad_in[...].astype(F32)
    entry_ref[...] = entry_in[...].astype(F32)
    down_ref[...] = down_in[...].astype(F32)

    @pl.when(pl.program_id(0) == 0)
    def _():
        out_ref[...] = out_in[...]
        lgrad_ref[...] = lgrad_in[...].astype(F32)
        norm_ref[...] = tiny_in[0:2]
        s = lax.axis_index("section")
        mine = jnp.zeros((2, 192), F32)
        for k in range(4):
            mine = jnp.where(s == k, tiny_in[2:4, k * 192:(k + 1) * 192], mine)
        in_norm_ref[...] = mine


def on_device(lat, raw, cot, lengths, clip, w, f, snorm, inorm):
    def low(*shape):
        return pltpu.VMEM(shape, BF)

    def full(*shape):
        return pltpu.VMEM(shape, F32)

    def sem(*shape):
        return pltpu.SemaphoreType.DMA(shape)

    def pair(*shape):
        return [sem(*shape), sem(*shape)]

    one = pltpu.SemaphoreType.DMA
    ring = N - 1
    scratch = [
        low(D, 4 * D), low(D, 4 * D), low(2, 2 * D, D), low(3, 2 * D, D), low(6, 2 * D, D),
        low(3, 6, SEQ, 256), low(3, HALF, D), low(3, 3, QUARTER, D), low(3, ring, PIECE, D), low(3, QUARTER, D),
        *[low(3, LAT, D)] * 6,
        *[low(3 * LAT, D)] * 4, low(LAT, D),
        low(3, VIA, D), low(3, LAT, D), low(3, 32, D), low(3, 32, D),
        full(8, D), full(3, 8, D), full(8, D), full(4, 8, D),
        full(3, 8, D), full(1, 8, D), full(ring, 8, D), full(ring, 8, D),
        sem(8), *pair(3), sem(3), sem(3, 3), sem(2), sem(4), sem(3), sem(3, 4), *pair(3), one, one, one, one,
        *pair(3), *pair(3), *pair(3), *pair(3, 2), sem(3, 4), sem(3), sem(3, 3), sem(3), sem(3, 3), sem(3),
        *pair(3), *pair(3, 6), *pair(3, ring), *pair(3, ring), *pair(3, 4), *pair(3),
        *pair(ring), *pair(4), one, one, *pair(ring), *pair(4), one, one,
        *pair(3), *pair(1), *pair(ring), *pair(ring), sem(3, 2),
        pltpu.SemaphoreType.REGULAR((3,)), pltpu.SemaphoreType.REGULAR((3,)),
    ]
    hbm = pl.BlockSpec(memory_space=pl.ANY)
    vmem = pl.BlockSpec(memory_space=pltpu.VMEM)
    inner = pl.pallas_call(
        kernel,
        name="layers",
        out_shape=(
            jax.ShapeDtypeStruct(lat.shape, BF),
            jax.ShapeDtypeStruct(lat.shape, BF),
            jax.ShapeDtypeStruct(raw.shape, BF),
            jax.ShapeDtypeStruct(w.shape, BF),
            jax.ShapeDtypeStruct(f.shape, BF),
            jax.ShapeDtypeStruct((8, D), F32),
        ),
        in_specs=[hbm, hbm, hbm, pl.BlockSpec(memory_space=pltpu.SMEM), vmem, hbm, hbm, vmem, vmem],
        out_specs=(vmem, vmem, vmem, hbm, hbm, vmem),
        scratch_shapes=scratch,
        compiler_params=pltpu.CompilerParams(
            collective_id=0, has_side_effects=True, vmem_limit_bytes=60 * 2**20
        ),
    )(lat, raw, cot, lengths, clip, w, f, snorm, inorm)
    steps = 4

    def by_rows(array):
        rest = array.shape[1:]
        return pl.BlockSpec((array.shape[0] // steps, *rest), lambda t: (t,) + (0,) * len(rest))

    def whole(*shape):
        return pl.BlockSpec(shape, lambda t: (0,) * len(shape))

    out, lgrad, igrad, entry, down, tiny = inner
    igrad = igrad.reshape(3 * LAT, D)
    entry, down = entry[0], down[0]
    final = pl.pallas_call(
        widen,
        name="widen",
        grid=(steps,),
        out_shape=(
            jax.ShapeDtypeStruct(lat.shape, BF),
            jax.ShapeDtypeStruct(lat.shape, F32),
            jax.ShapeDtypeStruct(igrad.shape, F32),
            jax.ShapeDtypeStruct(entry.shape, F32),
            jax.ShapeDtypeStruct(down.shape, F32),
            jax.ShapeDtypeStruct((2, D), F32),
            jax.ShapeDtypeStruct((2, 192), F32),
        ),
        in_specs=[
            whole(*lat.shape), whole(*lat.shape), by_rows(igrad), by_rows(entry), by_rows(down), whole(8, D)
        ],
        out_specs=(
            whole(*lat.shape), whole(*lat.shape), by_rows(igrad), by_rows(entry), by_rows(down),
            whole(2, D), whole(2, 192),
        ),
        compiler_params=pltpu.CompilerParams(vmem_limit_bytes=60 * 2**20),
    )(out, lgrad, igrad, entry, down, tiny)
    out, lgrad, igrad, entry, down, norm, in_norm = final
    return out, lgrad, igrad.reshape(raw.shape), entry[None], down[None], norm[None], in_norm


def solution(mesh):
    rows_split = P("dp", "section", None)
    weight = P("section", None, None)
    return jax.shard_map(
        on_device,
        mesh=mesh,
        in_specs=(
            rows_split, rows_split, rows_split, P("dp", None), P("dp", None),
            weight, weight, weight, P(None, "section"),
        ),
        out_specs=(rows_split, rows_split, rows_split, weight, weight, weight, P(None, "section")),
        check_vma=False,
    )
```

```python
import functools

import jax
import jax.numpy as jnp
from jax import lax
from jax.experimental import pallas as pl
from jax.experimental.pallas import tpu as pltpu
from jax.sharding import PartitionSpec as P


D = 768
LAT = 128
SEQ = 512
EPS = 1e-5
NEG = -1e9
F32 = jnp.float32
BF = jnp.bfloat16


def nn(a, b):
    return jnp.dot(a, b, preferred_element_type=F32)


def nt(a, b):
    return lax.dot_general(a, b, (((1,), (1,)), ((), ())), preferred_element_type=F32)


def tn(a, b):
    return lax.dot_general(a, b, (((0,), (0,)), ((), ())), preferred_element_type=F32)


def unit(x):
    mean = jnp.mean(x, -1, keepdims=True)
    cen = x - mean
    var = jnp.mean(cen * cen, -1, keepdims=True)
    rstd = lax.rsqrt(var + EPS)
    return cen * rstd, rstd


def ln_back(x, da, gain):
    xhat, rstd = unit(x)
    dx = da * gain
    m1 = jnp.mean(dx, -1, keepdims=True)
    m2 = jnp.mean(dx * xhat, -1, keepdims=True)
    grad = rstd * (dx - m1 - xhat * m2)
    return grad, jnp.sum(da * xhat, 0, keepdims=True), jnp.sum(da, 0, keepdims=True)


def gelu_pair(z):
    a = jnp.abs(z)
    t = 1.0 / (1.0 + (0.3275911 * 0.7071067811865476) * a)
    e = jnp.exp(-0.5 * (z * z))
    p = t * (0.254829592 + t * (-0.284496736 + t * (1.421413741 + t * (-1.453152027 + t * 1.061405429))))
    half = (0.5 * p) * e
    cdf = jnp.where(z >= 0, 1.0 - half, half)
    return z * cdf, cdf + z * (0.3989422804014327 * e)


def rows(i, n):
    return pl.ds(pl.multiple_of(i * n, n), n)


def ffn_fwd(i, x, a, W, Fd, X, kept):
    total = x
    for c in range(4):
        gate, slope = gelu_pair(nn(a, W[:, c * D:(c + 1) * D]))
        gate = gate.astype(BF)
        where_ = pl.ds(pl.multiple_of(c * 384 + i * LAT, LAT), LAT)
        if c < kept:
            X[0, where_] = gate
        X[5, where_] = slope.astype(BF)
        total = total + nn(gate, Fd[c // 2, (c % 2) * D:(c % 2 + 1) * D])
    return total


def ffn_bwd(i, db, W, Fd, X, kept):
    da = None
    for c in range(4):
        dg = nt(db, Fd[c // 2, (c % 2) * D:(c % 2 + 1) * D])
        where_ = pl.ds(pl.multiple_of(c * 384 + i * LAT, LAT), LAT)
        dz = (X[5, where_].astype(F32) * dg).astype(BF)
        if kept:
            X[1, where_] = dz
        part = nt(dz, W[:, c * D:(c + 1) * D])
        da = part if da is None else da + part
    return da


def halves(m):
    lane = lax.broadcasted_iota(jnp.int32, m.shape, 1)
    zero = jnp.zeros_like(m)
    return jnp.concatenate([jnp.where(lane < 64, m, zero), jnp.where(lane >= 64, m, zero)], 0)


def unhalves(mt):
    q = mt.shape[1] // 2
    return jnp.concatenate([mt[0:64, 0:q], mt[64:128, q:2 * q]], 0).T


def attn_fwd(q, k, v, maskf, PT, O):
    for p in range(6):
        cols = slice(p * 128, (p + 1) * 128)
        qs = halves(q[:, cols])
        s = nt(k[:, cols], qs) * 0.125
        s = jnp.where(maskf, s, NEG)
        m = jnp.max(s, 0, keepdims=True)
        e = jnp.exp(s - m)
        l = jnp.sum(e, 0, keepdims=True)
        pt = (e * (1.0 / l)).astype(BF)
        PT[p] = pt
        ot = tn(v[:, cols], pt)
        O[:, cols] = unhalves(ot).astype(BF)


def attn_bwd(q, k, v, PT, do, dq, dk, dv):
    for p in range(6):
        cols = slice(p * 128, (p + 1) * 128)
        dos = halves(do[:, cols])
        qs = halves(q[:, cols])
        pt = PT[p]
        dp = nt(v[:, cols], dos)
        ptf = pt.astype(F32)
        w = dp * ptf
        delta = jnp.sum(w, 0, keepdims=True)
        ds = (w - ptf * delta).astype(BF)
        dk[:, cols] = (nn(ds, qs) * 0.125).astype(BF)
        dv[:, cols] = nn(pt, dos).astype(BF)
        dqt = tn(k[:, cols], ds)
        dq[:, cols] = (unhalves(dqt) * 0.125).astype(BF)


HALF = 768
QUARTER = 192
PIECE = 48
SIDE = 96
VIA = 80
N = 4
MESH = pl.DeviceIdType.MESH


ORDER = (2, 0, 1)


def kernel(
    lat_ref, raw_ref, cot_ref, len_ref, clip_ref, w_ref, f_ref, snorm_ref, inorm_ref,
    out_ref, lgrad_ref, igrad_ref, entry_ref, down_ref, tiny_ref,
    W, Wb, Fd, g, X, PT, rA, rB, rC, q, xin, yin, dBin, dBm, sendB, sendD,
    A, Q, O, dQ, dO, relay, dUb, outb, lgb, inb, inr, nacc, tsrc, tX, tC, t1, t2,
    loc, in_s, in_r, lat_s, lat_r, cot_s, cot_r, u_s, u_r, via_s, via_r, fx_s, fx_r, wx_s, wx_r,
    b_s, b_r, d_s, d_r, e_s, e_r, gu_s, gu_r, o_s, o_r, lg_s, lg_r, du_s, du_r,
    a_s, a_r, bb_s, bb_r, c_s, c_r, gd_s, gd_r, ge_s, ge_r, gf_s, gf_r,
    fd_s, fd_r, fe_s, fe_r, ff_s, ff_r, wd_s, wd_r, we_s, we_r, wf_s, wf_r,
    tx_s, tx_r, tc_s, tc_r, t1_s, t1_r, t2_s, t2_r, g_sem, free_a, free_b,
):
    s = lax.axis_index("section")
    dp = lax.axis_index("dp")
    c = lax.rem(dp, 2)
    z = lax.rem(dp // 2, N)
    y = dp // (2 * N)
    odd = lax.rem(s, 2) == 1
    r1 = y * (1 - c) + z * c
    r2 = z * (1 - c) + y * c
    mate = dp + 1 - 2 * c
    ring = range(1, N)
    once = jnp.minimum(s + 1, 1)

    def apart(work, *args):
        @pl.loop(0, once)
        def _(_):
            work(*args)

    def sec_of(k):
        return lax.rem(s + k, 4)

    def peer1(k):
        other = lax.rem(r1 + k, N)
        return ((other * (1 - c) + y * c) * N + z * (1 - c) + other * c) * 2 + c

    def peer2(k):
        other = lax.rem(r2 + k, N)
        return ((y * (1 - c) + other * c) * N + other * (1 - c) + z * c) * 2 + c

    def at(start, size, unit_size):
        return pl.ds(pl.multiple_of(start, unit_size), size)

    def remote(src, dst, send_sem, recv_sem, dp_to, sec_to):
        return pltpu.make_async_remote_copy(
            src_ref=src, dst_ref=dst, send_sem=send_sem, recv_sem=recv_sem,
            device_id=(dp_to, sec_to), device_id_type=MESH,
        )

    def local_w():
        return pltpu.make_async_copy(w_ref.at[0], W, loc.at[0])

    def local_f():
        return pltpu.make_async_copy(f_ref.at[0], Fd.at[jnp.where(odd, 1, 0)], loc.at[1])

    def local_lat():
        return pltpu.make_async_copy(lat_ref, xin.at[:, at(s * 32, 32, 32)], loc.at[3])

    def local_cot():
        return pltpu.make_async_copy(cot_ref, dBin.at[:, at(s * 32, 32, 32)], loc.at[4])

    def local_tokens(i):
        return pltpu.make_async_copy(raw_ref.at[i], X.at[5, at(i * SEQ, LAT, LAT)], loc.at[5 + i])

    def cp_in(k):
        return remote(inb, inr.at[k - 1], in_s.at[k - 1], in_r.at[k - 1], dp, sec_of(k))

    def cp_lat(i, src):
        return remote(
            lat_ref.at[i], xin.at[i, at(src * 32, 32, 32)],
            lat_s.at[i], lat_r.at[i, src - 1], dp, 0,
        )

    def cp_cot(src, to):
        return remote(
            cot_ref, dBin.at[:, at(src * 32, 32, 32)], cot_s.at[to - 2], cot_r.at[src], dp, to
        )

    def cp_u(i, src):
        count = LAT - VIA if src == 2 else LAT
        return remote(
            raw_ref.at[i, 0:count], X.at[5, at(i * SEQ + src * LAT, count, 16)],
            u_s.at[i], u_r.at[i, src - 1], dp, 0,
        )

    def cp_via(i):
        return remote(raw_ref.at[i, LAT - VIA:LAT], relay.at[i], via_s.at[i], via_r.at[i], dp, 1)

    def cp_on(i):
        return remote(
            relay.at[i], X.at[5, at(i * SEQ + 3 * LAT - VIA, VIA, 16)],
            via_s.at[i], u_r.at[i, 3], dp, 0,
        )

    own_quarter = c * HALF + r1 * QUARTER
    own_piece = own_quarter + r2 * PIECE

    def cp_fx():
        where_ = at(own_piece, PIECE, PIECE)
        to = jnp.where(s == 3, 2, jnp.minimum(s + 1, 3))
        return remote(
            f_ref.at[0, where_], Fd.at[jnp.where(s == 3, 1, 0), where_], fx_s, fx_r, dp, to
        )

    def cp_wx():
        rows_ = at(r1 * QUARTER + r2 * PIECE, PIECE, PIECE)
        cols = at(c * 2 * D, 2 * D, 2 * D)
        return remote(w_ref.at[0, rows_, cols], Wb.at[rows_, cols], wx_s, wx_r, dp, 2)

    def cp_b(i, src):
        return remote(src.at[i], xin.at[i], b_s.at[i], b_r.at[i], dp, jnp.minimum(s + 1, 3))

    def cp_d(i):
        return remote(sendD.at[i], dBin.at[i], d_s.at[i], d_r.at[i], dp, jnp.maximum(s - 1, 0))

    def cp_e(i):
        return remote(sendD.at[i], Fd.at[1, at(i * LAT, LAT, LAT)], e_s.at[i], e_r.at[i], dp, 0)

    def cp_gu(i, blk):
        where_ = at(blk * 384 + i * LAT, LAT, LAT)
        return remote(X.at[0, where_], Fd.at[0, where_], gu_s.at[i, blk], gu_r.at[i, blk], dp, 0)

    def cp_o(i, t):
        return remote(sendB.at[i, t * 32:(t + 1) * 32], outb.at[i], o_s.at[i, t], o_r.at[i], dp, t)

    def cp_lg(i, t):
        return remote(sendD.at[i, t * 32:(t + 1) * 32], lgb.at[i], lg_s.at[i, t - 1], lg_r.at[i], dp, t)

    def cp_du(i, t):
        return remote(
            X.at[5, at(i * SEQ + t * LAT, LAT, LAT)], dUb.at[i],
            du_s.at[i, t - 1], du_r.at[i], dp, t,
        )

    def cp_a(b):
        return remote(g.at[b, at((1 - c) * HALF, HALF, HALF)], rA.at[b], a_s.at[b], a_r.at[b], mate, s)

    def half_of(j, h):
        return at(c * HALF + lax.rem(r1 + j, N) * QUARTER + h * SIDE, SIDE, SIDE)

    def cp_rb(b, j):
        source, slot, lo, to = (
            (half_of(2, 0), 2, 0, 1), (half_of(2, 1), 2, 1, 3),
            (half_of(1, 1), 0, 1, 1), (half_of(3, 0), 1, 0, 3),
            (half_of(1, 0), 0, 0, 1), (half_of(3, 1), 1, 1, 3),
        )[j]
        return remote(
            g.at[b, source], rB.at[b, slot, lo * SIDE:(lo + 1) * SIDE],
            bb_s.at[b, j], bb_r.at[b, j], peer1(to), s,
        )

    def cp_rc(b, k):
        start = own_quarter + lax.rem(r2 + k, N) * PIECE
        return remote(
            g.at[b, at(start, PIECE, PIECE)], rC.at[b, k - 1],
            c_s.at[b, k - 1], c_r.at[b, k - 1], peer2(k), s,
        )

    class Gather:
        def __init__(self, view, own, sems):
            self.view, self.own, self.sems = view, own, sems

        def d(self, k):
            piece = self.own(r2 * PIECE, PIECE)
            return remote(piece, piece, self.sems[0].at[k - 1], self.sems[1].at[k - 1], peer2(k), s)

        def d_in(self, k):
            piece = self.own(lax.rem(r2 + N - k, N) * PIECE, PIECE)
            return remote(piece, piece, self.sems[0].at[k - 1], self.sems[1].at[k - 1], peer2(k), s)

        def e(self, j):
            if j < 2:
                src, dst = self.own(0, QUARTER), self.view(c, r1 * QUARTER, QUARTER)
            else:
                far = lax.rem(r1 + (3 if j == 2 else 1), N) * QUARTER + (j - 2) * SIDE
                src = dst = self.view(c, far, SIDE)
            return remote(
                src, dst, self.sems[2].at[j], self.sems[3].at[j], peer1(1 if j % 2 == 0 else 3), s
            )

        def e_in(self, j):
            if j < 2:
                dst = self.view(c, lax.rem(r1 + 3 - 2 * j, N) * QUARTER, QUARTER)
            else:
                dst = self.view(c, lax.rem(r1 + 2, N) * QUARTER + (j - 2) * SIDE, SIDE)
            return remote(dst, dst, self.sems[2].at[j], self.sems[3].at[j], peer1(1), s)

        def f(self):
            half = self.view(c, 0, HALF)
            return remote(half, half, self.sems[4], self.sems[5], mate, s)

        def f_in(self):
            half = self.view(1 - c, 0, HALF)
            return remote(half, half, self.sems[4], self.sems[5], mate, s)

        def e1(self):
            for j in (0, 1):
                self.e(j).start()

        def e2(self):
            for j in (0, 1):
                self.e_in(j).wait_recv()
                self.e(j + 2).start()

        def e_done(self):
            for j in (2, 3):
                self.e_in(j).wait_recv()

        def drain(self):
            for k in ring:
                self.d(k).wait_send()
            for j in range(4):
                self.e(j).wait_send()
            self.f().wait_send()

    def gather_f(half):
        def view(core, start, size):
            return Fd.at[half, at(core * HALF + start, size, 16)]
        return Gather(
            view, lambda start, size: view(c, r1 * QUARTER + start, size),
            (fd_s, fd_r, fe_s, fe_r, ff_s, ff_r),
        )

    def gather_w():
        def view(core, start, size):
            return Wb.at[at(start, size, 16), at(core * 2 * D, 2 * D, 2 * D)]
        return Gather(
            view, lambda start, size: view(c, r1 * QUARTER + start, size),
            (wd_s, wd_r, we_s, we_r, wf_s, wf_r),
        )

    def gather_g(b):
        def view(core, start, size):
            return g.at[b, at(core * HALF + start, size, 16)]
        return Gather(
            view, lambda start, size: q.at[b, at(start, size, 16)],
            (gd_s.at[b], gd_r.at[b], ge_s.at[b], ge_r.at[b], gf_s.at[b], gf_r.at[b]),
        )

    def stage_b(b):
        cp_a(b).wait_recv()
        for j in (2, 1, 3, 0):
            part = at(c * HALF + lax.rem(r1 + j, N) * QUARTER, QUARTER, QUARTER)
            other = at(lax.rem(r1 + j, N) * QUARTER, QUARTER, QUARTER)
            g[b, part] = (g[b, part].astype(F32) + rA[b, other].astype(F32)).astype(BF)
            if j == 2:
                cp_rb(b, 0).start()
                cp_rb(b, 1).start()
            elif j == 1:
                cp_rb(b, 2).start()
            elif j == 3:
                cp_rb(b, 3).start()

    def sum_far(b):
        for j in (0, 1):
            cp_rb(b, j).wait_recv()
            mine = half_of(1 + 2 * j, j)
            arrived = rB[b, 2, j * SIDE:(j + 1) * SIDE].astype(F32)
            g[b, mine] = (g[b, mine].astype(F32) + arrived).astype(BF)
            cp_rb(b, 4 + j).start()

    def sum_quarter(b):
        for j in (2, 3, 4, 5):
            cp_rb(b, j).wait_recv()
        part = at(own_quarter, QUARTER, QUARTER)
        total = g[b, part].astype(F32) + rB[b, 0].astype(F32) + rB[b, 1].astype(F32)
        g[b, part] = total.astype(BF)
        for k in ring:
            cp_rc(b, k).start()

    def sum_piece(b):
        cp_a(b).wait_send()
        pl.semaphore_signal(free_a.at[b], inc=1, device_id=(mate, s), device_id_type=MESH)
        for j in range(6):
            cp_rb(b, j).wait_send()
        for k in (1, 3):
            pl.semaphore_signal(free_b.at[b], inc=1, device_id=(peer1(k), s), device_id_type=MESH)
        for k in ring:
            cp_rc(b, k).wait_recv()
        total = g[b, at(own_piece, PIECE, PIECE)].astype(F32)
        for k in ring:
            total = total + rC[b, k - 1].astype(F32)
        q[b, at(r2 * PIECE, PIECE, PIECE)] = total.astype(BF)
        for k in ring:
            gather_g(b).d(k).start()

    local_w().start()

    @pl.when(s != 0)
    def _():
        local_f().start()

    barrier = pltpu.get_barrier_semaphore()
    partners = [(dp, sec_of(k)) for k in (1, 2, 3)] + [(mate, s)]
    partners += [(peer1(k), s) for k in ring] + [(peer2(k), s) for k in ring]
    for partner in partners:
        pl.semaphore_signal(barrier, inc=1, device_id=partner, device_id_type=MESH)
    select = lax.broadcasted_iota(jnp.int32, (192, D), 1) == lax.broadcasted_iota(jnp.int32, (192, D), 0) + s * 192
    snorm = snorm_ref[0].astype(F32)
    gain = 1.0 + snorm[0:1]
    shift = snorm[1:2]
    inb[...] = jnp.zeros_like(inb)
    inb[0:2] = nn(inorm_ref[...], select.astype(F32).astype(BF))
    inb[2:4] = snorm
    nacc[...] = jnp.zeros_like(nacc)
    pl.semaphore_wait(barrier, len(partners))

    for k in (1, 2, 3):
        cp_in(k).start()

    @pl.when(s == 0)
    def _():
        local_lat().start()
        for i in range(3):
            local_tokens(i).start()

    @pl.when(s != 1)
    def _():
        cp_fx().start()

    @pl.when(s == 3)
    def _():
        cp_wx().start()

    for sec in (1, 2, 3):
        @pl.when(s == sec)
        def _():
            for i in range(3):
                cp_lat(i, sec).start()
                if sec == 2:
                    cp_via(i).start()
                cp_u(i, sec).start()

    @pl.when(s >= 2)
    def _():
        local_cot().start()

    for to in (2, 3):
        @pl.when(s != to)
        def _():
            cp_cot(s, to).start()

    def project(a, lo, hi):
        return nn(a, W[:, lo:hi])

    def latent_back(x_ref, i, da, db):
        dx, dg, dbias = ln_back(x_ref[i].astype(F32), da, gain)
        nacc[0:1] = nacc[0:1] + dg
        nacc[1:2] = nacc[1:2] + dbias
        return db.astype(F32) + dx

    local_w().wait()

    def send_du(i):
        in_gain = 1.0 + inb[0:1] + inr[0, 0:1] + inr[1, 0:1] + inr[2, 0:1]
        at_rows = rows(i, SEQ)
        du = nt(X[3, at_rows], W[:, D:2 * D]) + nt(X[4, at_rows], W[:, 2 * D:3 * D])
        X[1, at_rows] = du.astype(BF)

        @pl.loop(0, 4)
        def _(j):
            part = at(i * SEQ + j * LAT, LAT, LAT)
            dx, dg, dbias = ln_back(X[5, part].astype(F32), X[1, part].astype(F32), in_gain)
            X[5, part] = dx.astype(BF)
            nacc[2:3] = nacc[2:3] + dg
            nacc[3:4] = nacc[3:4] + dbias
        dUb[i] = X[5, at(i * SEQ, LAT, LAT)]
        for t in (1, 2, 3):
            cp_du(i, t).start()

    def plane_0():
        local_lat().wait()
        for k in (1, 2, 3):
            cp_in(k).wait_recv()
        in_all = inb[...] + inr[0] + inr[1] + inr[2]

        @pl.loop(0, 3)
        def _(i):
            for src in (1, 2, 3):
                cp_lat(i, src).wait_recv()
            x = xin[i].astype(F32)
            xhat, _ = unit(x)
            a = (xhat * gain + shift).astype(BF)
            lat_rows = rows(i, LAT)
            A[lat_rows] = a
            Q[lat_rows] = project(a, 0, D).astype(BF)
            for src in (1, 2, 3):
                cp_u(i, src).wait_recv()
            cp_on(i).wait_recv()
            local_tokens(i).wait()

            @pl.loop(0, 4)
            def _(j):
                part = at(i * SEQ + j * LAT, LAT, LAT)
                xhat, _ = unit(X[5, part].astype(F32))
                X[0, part] = (xhat * (1.0 + in_all[0:1]) + in_all[1:2]).astype(BF)
            u = X[0, rows(i, SEQ)]
            kv = [X.at[j, rows(i, SEQ)] for j in (1, 2)]
            kv[0][...] = project(u, D, 2 * D).astype(BF)
            kv[1][...] = project(u, 2 * D, 3 * D).astype(BF)
            where_ = lax.broadcasted_iota(jnp.int32, (SEQ, 256), 0)
            clip = jnp.zeros((SEQ, 256), jnp.int32)
            end = jnp.int32(0)
            for j in range(4):
                end = end + len_ref[i, j]
                clip = clip + (where_ >= end).astype(jnp.int32)
            ids = clip_ref[pl.ds(i, 1)]
            ids = jnp.concatenate([ids, ids], 1)
            attn_fwd(Q.at[lat_rows], kv[0], kv[1], clip == ids, PT.at[i], O.at[lat_rows])
            b = x + project(O[lat_rows], 3 * D, 4 * D)
            sendB[i] = b.astype(BF)
            cp_b(i, sendB).start()

        def latent_out(i):
            db = dBin[i]
            grad = latent_back(xin, i, nt(dQ[rows(i, LAT)], W[:, :D]), db).astype(BF)
            sendD[i] = grad
            lgb[i] = grad[0:32]
            for t in (1, 2, 3):
                cp_lg(i, t).start()

        def item_back(i):
            cp_d(i).wait_recv()
            dO[...] = nt(dBin[i], W[:, 3 * D:]).astype(BF)
            kv = [X.at[j, rows(i, SEQ)] for j in (1, 2, 3, 4)]
            lat_rows = rows(i, LAT)
            attn_bwd(Q.at[lat_rows], kv[0], kv[1], PT.at[i], dO, dQ.at[lat_rows], kv[2], kv[3])

        def weight_grads(tokens, latents, add):
            def put(b, rows_, grad):
                g[b, rows_] = ((g[b, rows_].astype(F32) + grad) if add else grad).astype(BF)
            count = latents.stop - latents.start
            db = dBin[latents.start // LAT:latents.stop // LAT].reshape(count, D)
            put(0, slice(0, D), tn(A[latents], dQ[latents]))
            put(1, slice(D, 2 * D), tn(O[latents], db))

            @pl.loop(0, 2)
            def _(b):
                put(b, at((1 - b) * D, D, D), tn(X[0, tokens], X[3 + b, tokens]))

        @pl.loop(0, 3)
        def _(i):
            @pl.when(i == 2)
            def _():
                for t in range(3):
                    cp_e(t).wait_recv()
                    for blk in range(2):
                        cp_gu(t, blk).wait_recv()

                @pl.loop(0, 2)
                def _(blk):
                    g[2, at(blk * D, D, D)] = tn(Fd[0, at(blk * 384, 384, 384)], Fd[1, 0:384]).astype(BF)
                cp_a(2).start()
                weight_grads(slice(0, 2 * SEQ), slice(0, 2 * LAT), False)
                apart(stage_b, 2)
            item_back(i)

            @pl.when(i < 2)
            def _():
                latent_out(i)
        weight_grads(slice(2 * SEQ, 3 * SEQ), slice(2 * LAT, 3 * LAT), True)
        cp_a(0).start()
        cp_a(1).start()
        pl.loop(2, 2 + once)(latent_out)

    def plane_2():
        for k in (1, 2, 3):
            cp_in(k).wait_recv()
        far_gain = 1.0 + inr[2, 2:3]
        far_shift = inr[2, 3:4]
        w3, f3 = gather_w(), gather_f(1)
        cp_fx().wait_recv()
        cp_wx().wait_recv()
        for k in ring:
            w3.d(k).start()
            f3.d(k).start()
        for one in (w3, f3):
            for k in ring:
                one.d_in(k).wait_recv()
            one.e1()
        for one in (w3, f3):
            one.e2()
        for one in (w3, f3):
            one.e_done()
            one.f().start()
        local_f().wait()
        local_cot().wait()
        for src in (0, 1, 3):
            cp_cot(src, 2).wait_recv()
        for one in (w3, f3):
            one.f_in().wait_recv()

        @pl.loop(0, 3)
        def _(i):
            lat_rows = rows(i, LAT)
            cp_b(i, yin).wait_recv()
            x = xin[i].astype(F32)
            xhat, _ = unit(x)
            a = (xhat * gain + shift).astype(BF)
            A[lat_rows] = a
            Q[lat_rows] = project(a, 0, D).astype(BF)
            X[1, lat_rows] = project(a, D, 2 * D).astype(BF)
            X[2, lat_rows] = project(a, 2 * D, 3 * D).astype(BF)
            ids = jnp.broadcast_to(clip_ref[pl.ds(i, 1)].astype(F32), (LAT, LAT))
            mask = jnp.concatenate([ids, ids], 1) == jnp.concatenate([ids.T, ids.T], 1)
            attn_fwd(
                Q.at[lat_rows], X.at[1, lat_rows], X.at[2, lat_rows], mask,
                PT.at[i, :, 0:LAT], O.at[lat_rows],
            )
            middle = (x + project(O[lat_rows], 3 * D, 4 * D)).astype(BF)
            yin[i] = middle
            cp_b(i, yin).start()
            x = middle.astype(F32)
            xhat, _ = unit(x)
            a = (xhat * far_gain + far_shift).astype(BF)
            b = ffn_fwd(i, x, a, Wb, Fd, X, 2).astype(BF)
            sendB[i] = b
            outb[i] = b[64:96]
            for t in (0, 1, 3):
                cp_o(i, t).start()
            db = dBin[i]
            dx, _, _ = ln_back(x, ffn_bwd(i, db, Wb, Fd, X, False), far_gain)
            db = (db.astype(F32) + dx).astype(BF)
            dBm[i] = db
            dO[...] = nt(db, W[:, 3 * D:]).astype(BF)
            attn_bwd(
                Q.at[lat_rows], X.at[1, lat_rows], X.at[2, lat_rows], PT.at[i, :, 0:LAT],
                dO, dQ.at[lat_rows], X.at[3, lat_rows], X.at[4, lat_rows],
            )
            da = nt(dQ[lat_rows], W[:, :D]) + nt(X[3, lat_rows], W[:, D:2 * D])
            da = da + nt(X[4, lat_rows], W[:, 2 * D:3 * D])
            sendD[i] = latent_back(xin, i, da, db).astype(BF)
            cp_d(i).start()
            cp_e(i).start()

        def all_grads(b):
            if b == 2:
                db = dBin[...].reshape(3 * LAT, D)
                pair = tn(X[0, 0:384], db), tn(X[0, 384:768], db)
            elif b == 0:
                pair = tn(A[...], dQ[...]), tn(A[...], X[3, 0:3 * LAT])
            else:
                pair = tn(A[...], X[4, 0:3 * LAT]), tn(O[...], dBm[...].reshape(3 * LAT, D))
            g[b, 0:D] = pair[0].astype(BF)
            g[b, D:] = pair[1].astype(BF)

        for b in ORDER:
            apart(all_grads, b)
            cp_a(b).start()

    def plane_odd(sec):
        def relay_on(i):
            if sec == 1:
                cp_via(i).wait_recv()
                cp_on(i).start()

        prior = gather_f(0)
        relay_on(0)
        cp_fx().wait_recv()
        for k in ring:
            prior.d(k).start()
        relay_on(1)
        for k in ring:
            prior.d_in(k).wait_recv()
        prior.e1()
        relay_on(2)
        prior.e2()
        prior.e_done()
        prior.f().start()
        local_f().wait()
        prior.f_in().wait_recv()

        if sec == 3:
            local_cot().wait()
            for src in (0, 1, 2):
                cp_cot(src, 3).wait_recv()

        def store_grads(b, first, count, add):
            own = slice(first * LAT, (first + count) * LAT)

            @pl.loop(0, 2)
            def _(j):
                block = (2 if b == 2 else 2 * b) + j
                units = at(block * 384 + first * LAT, count * LAT, LAT)
                if b == 2:
                    grad = tn(X[0, units], dBin[first:first + count].reshape(count * LAT, D))
                else:
                    grad = tn(A[own], X[1, units])
                here = at(j * D, D, D)
                g[b, here] = ((g[b, here].astype(F32) + grad) if add else grad).astype(BF)

        def forward(i):
            cp_b(i, sendB).wait_recv()
            x = xin[i].astype(F32)
            xhat, _ = unit(x)
            a = (xhat * gain + shift).astype(BF)
            A[rows(i, LAT)] = a
            return ffn_fwd(i, x, a, W, Fd, X, 4).astype(BF)

        def backward(i):
            db = dBin[i]
            return latent_back(xin, i, ffn_bwd(i, db, W, Fd, X, True), db).astype(BF)

        if sec == 1:
            @pl.loop(0, 3)
            def _(i):
                sendB[i] = forward(i)
                cp_b(i, sendB).start()
                for blk in range(2):
                    cp_gu(i, blk).start()

            @pl.loop(0, 3)
            def _(i):
                @pl.when(i == 2)
                def _():
                    for b in ORDER:
                        store_grads(b, 0, 2, False)
                cp_d(i).wait_recv()
                sendD[i] = backward(i)
                cp_d(i).start()
            for b in ORDER:
                apart(store_grads, b, 2, 1, True)
                cp_a(b).start()

        else:
            @pl.loop(0, 3)
            def _(i):
                forward(i)
                backward(i)
            for b in ORDER:
                apart(store_grads, b, 0, 3, False)
                cp_a(b).start()

    def spread_quarter(b):
        for k in ring:
            cp_rc(b, k).wait_send()
        pl.semaphore_wait(free_b.at[b], 2)
        for k in ring:
            gather_g(b).d_in(k).wait_recv()
        gather_g(b).e1()
        g[b, at(own_quarter, QUARTER, QUARTER)] = q[b]

    def spread_far(b):
        gather_g(b).e2()

    def leave(b, h, act):
        src = g.at[b, at(h * HALF, HALF, HALF)]

        @pl.when(b == 2)
        def _():
            act(pltpu.make_async_copy(src, down_ref.at[0, at(h * HALF, HALF, HALF)], g_sem.at[b, h]))

        @pl.when(b < 2)
        def _():
            block = at(jnp.minimum(2 * b + h, 3) * D, D, D)
            act(pltpu.make_async_copy(src, entry_ref.at[0, :, block], g_sem.at[b, h]))

    def spread_half(b):
        gather_g(b).e_done()
        pl.semaphore_wait(free_a.at[b], 1)
        gather_g(b).f().start()
        leave(b, c, lambda copy: copy.start())

    def finish(b):
        gather_g(b).f_in().wait_recv()
        leave(b, 1 - c, lambda copy: copy.start())

    def small(step, buf, ss, rs, k, dp_to, sec_to):
        return remote(tsrc.at[step], buf.at[k], ss.at[k], rs.at[k], dp_to, sec_to)

    def own_rows():
        @pl.when(odd)
        def _():
            for k in (1, 2, 3):
                cp_in(k).wait_recv()

        @pl.loop(0, 3)
        def _(i):
            @pl.when(s != 2)
            def _():
                cp_o(i, 0).wait_recv()

            @pl.when(s != 0)
            def _():
                cp_lg(i, 1).wait_recv()
                cp_du(i, 1).wait_recv()
            igrad_ref[i] = dUb[i]
            out_ref[i] = outb[i]
            lgrad_ref[i] = lgb[i]

    def small_x(k):
        return remote(tsrc.at[0], tX.at[0], tx_s.at[k - 1], tx_r.at[0], dp, sec_of(k))

    def small_mate():
        tsrc[1] = nacc[...]
        small(1, tC, tc_s, tc_r, 0, mate, s).start()

    def small_ring1():
        small(1, tC, tc_s, tc_r, 0, mate, s).wait_recv()
        tsrc[2] = tsrc[1] + tC[0]
        for k in ring:
            small(2, t1, t1_s, t1_r, k - 1, peer1(k), s).start()

    def small_ring2():
        for k in ring:
            small(2, t1, t1_s, t1_r, k - 1, peer1(k), s).wait_recv()
        tsrc[3] = tsrc[2] + t1[0] + t1[1] + t1[2]
        for k in ring:
            small(3, t2, t2_s, t2_r, k - 1, peer2(k), s).start()

    def small_out(sec):
        for k in ring:
            small(3, t2, t2_s, t2_r, k - 1, peer2(k), s).wait_recv()
        total = tsrc[3] + t2[0] + t2[1] + t2[2]
        tsrc[0] = total
        tiny_ref[...] = total

        if sec == 0:
            for k in (1, 2, 3):
                small_x(k).start()

    def small_done():
        @pl.when(s != 0)
        def _():
            small_x(1).wait_recv()
            tiny_ref[2:4] = tX[0, 2:4]

    def tail(sec):
        stages = (
            stage_b, sum_far, sum_quarter, sum_piece, spread_quarter, spread_far, spread_half, finish
        )

        @pl.loop(0, len(stages) + 2)
        def _(turn):
            for k, stage in enumerate(stages):
                t = turn - k
                due = (t >= 0) & (t < 3)
                if k == 0 and sec == 0:
                    due = due & (t > 0)
                pl.when(due)(functools.partial(stage, lax.rem(t + 2, 3)))

            if sec == 0:
                pl.when((turn > 0) & (turn < 4))(functools.partial(send_du, turn - 1))
            for k, step in ((4, small_mate), (5, small_ring1), (6, small_ring2), (8, functools.partial(small_out, sec))):
                pl.when(turn == k)(step)

        @pl.loop(0, 3)
        def _(b):
            for h in range(2):
                leave(b, h, lambda copy: copy.wait())

        for k in (1, 2, 3):
            cp_in(k).wait_send()
        small(1, tC, tc_s, tc_r, 0, mate, s).wait_send()
        for k in ring:
            small(2, t1, t1_s, t1_r, k - 1, peer1(k), s).wait_send()
            small(3, t2, t2_s, t2_r, k - 1, peer2(k), s).wait_send()
        pl.loop(0, 3)(lambda b: gather_g(b).drain())
        for to in (2, 3):
            if sec != to:
                cp_cot(sec, to).wait_send()
        if sec != 1:
            cp_fx().wait_send()
        if sec == 3:
            cp_wx().wait_send()
        if sec == 2:
            gather_w().drain()
            gather_f(1).drain()
        if sec in (1, 3):
            gather_f(0).drain()
        for i in range(3):
            if sec > 0:
                cp_lat(i, sec).wait_send()
                cp_u(i, sec).wait_send()
            if sec < 3:
                cp_b(i, sendB).wait_send()
            if sec in (1, 2):
                cp_via(i).wait_send()
                cp_d(i).wait_send()
            if sec == 0 and i == 0:
                for k in (1, 2, 3):
                    small_x(k).wait_send()
            if sec == 0:
                for t in (1, 2, 3):
                    cp_lg(i, t).wait_send()
                    cp_du(i, t).wait_send()
            if sec == 1:
                for blk in range(2):
                    cp_gu(i, blk).wait_send()
            if sec == 2:
                cp_e(i).wait_send()
                for t in (0, 1, 3):
                    cp_o(i, t).wait_send()

    work = {0: plane_0, 1: functools.partial(plane_odd, 1), 2: plane_2, 3: functools.partial(plane_odd, 3)}
    for sec in (3, 2, 1, 0):
        @pl.when(s == sec)
        def _():
            work[sec]()
            tail(sec)
    own_rows()
    small_done()


def widen(
    out_in, lgrad_in, igrad_in, entry_in, down_in, tiny_in,
    out_ref, lgrad_ref, igrad_ref, entry_ref, down_ref, norm_ref, in_norm_ref,
):
    igrad_ref[...] = igrad_in[...].astype(F32)
    entry_ref[...] = entry_in[...].astype(F32)
    down_ref[...] = down_in[...].astype(F32)

    @pl.when(pl.program_id(0) == 0)
    def _():
        out_ref[...] = out_in[...]
        lgrad_ref[...] = lgrad_in[...].astype(F32)
        norm_ref[...] = tiny_in[0:2]
        s = lax.axis_index("section")
        mine = jnp.zeros((2, 192), F32)
        for k in range(4):
            mine = jnp.where(s == k, tiny_in[2:4, k * 192:(k + 1) * 192], mine)
        in_norm_ref[...] = mine


def on_device(lat, raw, cot, lengths, clip, w, f, snorm, inorm):
    def low(*shape):
        return pltpu.VMEM(shape, BF)

    def full(*shape):
        return pltpu.VMEM(shape, F32)

    def sem(*shape):
        return pltpu.SemaphoreType.DMA(shape)

    def pair(*shape):
        return [sem(*shape), sem(*shape)]

    one = pltpu.SemaphoreType.DMA
    ring = N - 1
    scratch = [
        low(D, 4 * D), low(D, 4 * D), low(2, 2 * D, D), low(3, 2 * D, D), low(6, 2 * D, D),
        low(3, 6, SEQ, 256), low(3, HALF, D), low(3, 3, QUARTER, D), low(3, ring, PIECE, D), low(3, QUARTER, D),
        *[low(3, LAT, D)] * 6,
        *[low(3 * LAT, D)] * 4, low(LAT, D),
        low(3, VIA, D), low(3, LAT, D), low(3, 32, D), low(3, 32, D),
        full(8, D), full(3, 8, D), full(8, D), full(4, 8, D),
        full(3, 8, D), full(1, 8, D), full(ring, 8, D), full(ring, 8, D),
        sem(8), *pair(3), sem(3), sem(3, 3), sem(2), sem(4), sem(3), sem(3, 4), *pair(3), one, one, one, one,
        *pair(3), *pair(3), *pair(3), *pair(3, 2), sem(3, 4), sem(3), sem(3, 3), sem(3), sem(3, 3), sem(3),
        *pair(3), *pair(3, 6), *pair(3, ring), *pair(3, ring), *pair(3, 4), *pair(3),
        *pair(ring), *pair(4), one, one, *pair(ring), *pair(4), one, one,
        *pair(3), *pair(1), *pair(ring), *pair(ring), sem(3, 2),
        pltpu.SemaphoreType.REGULAR((3,)), pltpu.SemaphoreType.REGULAR((3,)),
    ]
    hbm = pl.BlockSpec(memory_space=pl.ANY)
    vmem = pl.BlockSpec(memory_space=pltpu.VMEM)
    inner = pl.pallas_call(
        kernel,
        name="layers",
        out_shape=(
            jax.ShapeDtypeStruct(lat.shape, BF),
            jax.ShapeDtypeStruct(lat.shape, BF),
            jax.ShapeDtypeStruct(raw.shape, BF),
            jax.ShapeDtypeStruct(w.shape, BF),
            jax.ShapeDtypeStruct(f.shape, BF),
            jax.ShapeDtypeStruct((8, D), F32),
        ),
        in_specs=[hbm, hbm, hbm, pl.BlockSpec(memory_space=pltpu.SMEM), vmem, hbm, hbm, vmem, vmem],
        out_specs=(vmem, vmem, vmem, hbm, hbm, vmem),
        scratch_shapes=scratch,
        compiler_params=pltpu.CompilerParams(
            collective_id=0, has_side_effects=True, vmem_limit_bytes=60 * 2**20
        ),
    )(lat, raw, cot, lengths, clip, w, f, snorm, inorm)
    steps = 4

    def by_rows(array):
        rest = array.shape[1:]
        return pl.BlockSpec((array.shape[0] // steps, *rest), lambda t: (t,) + (0,) * len(rest))

    def whole(*shape):
        return pl.BlockSpec(shape, lambda t: (0,) * len(shape))

    out, lgrad, igrad, entry, down, tiny = inner
    igrad = igrad.reshape(3 * LAT, D)
    entry, down = entry[0], down[0]
    final = pl.pallas_call(
        widen,
        name="widen",
        grid=(steps,),
        out_shape=(
            jax.ShapeDtypeStruct(lat.shape, BF),
            jax.ShapeDtypeStruct(lat.shape, F32),
            jax.ShapeDtypeStruct(igrad.shape, F32),
            jax.ShapeDtypeStruct(entry.shape, F32),
            jax.ShapeDtypeStruct(down.shape, F32),
            jax.ShapeDtypeStruct((2, D), F32),
            jax.ShapeDtypeStruct((2, 192), F32),
        ),
        in_specs=[
            whole(*lat.shape), whole(*lat.shape), by_rows(igrad), by_rows(entry), by_rows(down), whole(8, D)
        ],
        out_specs=(
            whole(*lat.shape), whole(*lat.shape), by_rows(igrad), by_rows(entry), by_rows(down),
            whole(2, D), whole(2, 192),
        ),
        compiler_params=pltpu.CompilerParams(vmem_limit_bytes=60 * 2**20),
    )(out, lgrad, igrad, entry, down, tiny)
    out, lgrad, igrad, entry, down, norm, in_norm = final
    return out, lgrad, igrad.reshape(raw.shape), entry[None], down[None], norm[None], in_norm


def solution(mesh):
    rows_split = P("dp", "section", None)
    weight = P("section", None, None)
    return jax.shard_map(
        on_device,
        mesh=mesh,
        in_specs=(
            rows_split, rows_split, rows_split, P("dp", None), P("dp", None),
            weight, weight, weight, P(None, "section"),
        ),
        out_specs=(rows_split, rows_split, rows_split, weight, weight, weight, P(None, "section")),
        check_vma=False,
    )
```

```python
import functools

import jax
import jax.numpy as jnp
from jax import lax
from jax.experimental import pallas as pl
from jax.experimental.pallas import tpu as pltpu
from jax.sharding import PartitionSpec as P


D = 768
LAT = 128
SEQ = 512
EPS = 1e-5
NEG = -1e9
F32 = jnp.float32
BF = jnp.bfloat16


def nn(a, b):
    return jnp.dot(a, b, preferred_element_type=F32)


def nt(a, b):
    return lax.dot_general(a, b, (((1,), (1,)), ((), ())), preferred_element_type=F32)


def tn(a, b):
    return lax.dot_general(a, b, (((0,), (0,)), ((), ())), preferred_element_type=F32)


def unit(x):
    mean = jnp.mean(x, -1, keepdims=True)
    cen = x - mean
    var = jnp.mean(cen * cen, -1, keepdims=True)
    rstd = lax.rsqrt(var + EPS)
    return cen * rstd, rstd


def ln_back(x, da, gain):
    xhat, rstd = unit(x)
    dx = da * gain
    m1 = jnp.mean(dx, -1, keepdims=True)
    m2 = jnp.mean(dx * xhat, -1, keepdims=True)
    grad = rstd * (dx - m1 - xhat * m2)
    return grad, jnp.sum(da * xhat, 0, keepdims=True), jnp.sum(da, 0, keepdims=True)


def gelu_pair(z):
    a = jnp.abs(z)
    t = 1.0 / (1.0 + (0.3275911 * 0.7071067811865476) * a)
    e = jnp.exp(-0.5 * (z * z))
    p = t * (0.254829592 + t * (-0.284496736 + t * (1.421413741 + t * (-1.453152027 + t * 1.061405429))))
    half = (0.5 * p) * e
    cdf = jnp.where(z >= 0, 1.0 - half, half)
    return z * cdf, cdf + z * (0.3989422804014327 * e)


def rows(i, n):
    return pl.ds(pl.multiple_of(i * n, n), n)


def ffn_fwd(i, x, a, W, Fd, X, kept):
    total = x
    for c in range(4):
        gate, slope = gelu_pair(nn(a, W[:, c * D:(c + 1) * D]))
        gate = gate.astype(BF)
        where_ = pl.ds(pl.multiple_of(c * 384 + i * LAT, LAT), LAT)
        if c < kept:
            X[0, where_] = gate
        X[5, where_] = slope.astype(BF)
        total = total + nn(gate, Fd[c // 2, (c % 2) * D:(c % 2 + 1) * D])
    return total


def ffn_bwd(i, db, W, Fd, X, kept):
    da = None
    for c in range(4):
        dg = nt(db, Fd[c // 2, (c % 2) * D:(c % 2 + 1) * D])
        where_ = pl.ds(pl.multiple_of(c * 384 + i * LAT, LAT), LAT)
        dz = (X[5, where_].astype(F32) * dg).astype(BF)
        if kept:
            X[1, where_] = dz
        part = nt(dz, W[:, c * D:(c + 1) * D])
        da = part if da is None else da + part
    return da


def halves(m):
    lane = lax.broadcasted_iota(jnp.int32, m.shape, 1)
    zero = jnp.zeros_like(m)
    return jnp.concatenate([jnp.where(lane < 64, m, zero), jnp.where(lane >= 64, m, zero)], 0)


def unhalves(mt):
    q = mt.shape[1] // 2
    return jnp.concatenate([mt[0:64, 0:q], mt[64:128, q:2 * q]], 0).T


def attn_fwd(q, k, v, maskf, PT, O):
    for p in range(6):
        cols = slice(p * 128, (p + 1) * 128)
        qs = halves(q[:, cols])
        s = nt(k[:, cols], qs) * 0.125
        s = jnp.where(maskf, s, NEG)
        m = jnp.max(s, 0, keepdims=True)
        e = jnp.exp(s - m)
        l = jnp.sum(e, 0, keepdims=True)
        pt = (e * (1.0 / l)).astype(BF)
        PT[p] = pt
        ot = tn(v[:, cols], pt)
        O[:, cols] = unhalves(ot).astype(BF)


def attn_bwd(q, k, v, PT, do, dq, dk, dv):
    for p in range(6):
        cols = slice(p * 128, (p + 1) * 128)
        dos = halves(do[:, cols])
        qs = halves(q[:, cols])
        pt = PT[p]
        dp = nt(v[:, cols], dos)
        ptf = pt.astype(F32)
        w = dp * ptf
        delta = jnp.sum(w, 0, keepdims=True)
        ds = (w - ptf * delta).astype(BF)
        dk[:, cols] = (nn(ds, qs) * 0.125).astype(BF)
        dv[:, cols] = nn(pt, dos).astype(BF)
        dqt = tn(k[:, cols], ds)
        dq[:, cols] = (unhalves(dqt) * 0.125).astype(BF)


HALF = 768
QUARTER = 192
PIECE = 48
SIDE = 96
VIA = 80
N = 4
MESH = pl.DeviceIdType.MESH


ORDER = (2, 0, 1)


def kernel(
    lat_ref, raw_ref, cot_ref, len_ref, clip_ref, w_ref, f_ref, snorm_ref, inorm_ref,
    out_ref, lgrad_ref, igrad_ref, entry_ref, down_ref, tiny_ref,
    W, Wb, Fd, g, X, PT, rA, rB, rC, q, xin, yin, dBin, dBm, sendB, sendD,
    A, Q, O, dQ, dO, relay, dUb, outb, lgb, inb, inr, nacc, tsrc, tX, tC, t1, t2,
    loc, in_s, in_r, lat_s, lat_r, cot_s, cot_r, u_s, u_r, via_s, via_r, fx_s, fx_r, wx_s, wx_r,
    b_s, b_r, d_s, d_r, e_s, e_r, gu_s, gu_r, o_s, o_r, lg_s, lg_r, du_s, du_r,
    a_s, a_r, bb_s, bb_r, c_s, c_r, gd_s, gd_r, ge_s, ge_r, gf_s, gf_r,
    fd_s, fd_r, fe_s, fe_r, ff_s, ff_r, wd_s, wd_r, we_s, we_r, wf_s, wf_r,
    tx_s, tx_r, tc_s, tc_r, t1_s, t1_r, t2_s, t2_r, g_sem, free_a, free_b,
):
    s = lax.axis_index("section")
    dp = lax.axis_index("dp")
    c = lax.rem(dp, 2)
    z = lax.rem(dp // 2, N)
    y = dp // (2 * N)
    odd = lax.rem(s, 2) == 1
    r1 = y * (1 - c) + z * c
    r2 = z * (1 - c) + y * c
    mate = dp + 1 - 2 * c
    ring = range(1, N)
    once = jnp.minimum(s + 1, 1)

    def apart(work, *args):
        @pl.loop(0, once)
        def _(_):
            work(*args)

    def sec_of(k):
        return lax.rem(s + k, 4)

    def peer1(k):
        other = lax.rem(r1 + k, N)
        return ((other * (1 - c) + y * c) * N + z * (1 - c) + other * c) * 2 + c

    def peer2(k):
        other = lax.rem(r2 + k, N)
        return ((y * (1 - c) + other * c) * N + other * (1 - c) + z * c) * 2 + c

    def at(start, size, unit_size):
        return pl.ds(pl.multiple_of(start, unit_size), size)

    def remote(src, dst, send_sem, recv_sem, dp_to, sec_to):
        return pltpu.make_async_remote_copy(
            src_ref=src, dst_ref=dst, send_sem=send_sem, recv_sem=recv_sem,
            device_id=(dp_to, sec_to), device_id_type=MESH,
        )

    def local_w():
        return pltpu.make_async_copy(w_ref.at[0], W, loc.at[0])

    def local_f():
        return pltpu.make_async_copy(f_ref.at[0], Fd.at[jnp.where(odd, 1, 0)], loc.at[1])

    def local_lat():
        return pltpu.make_async_copy(lat_ref, xin.at[:, at(s * 32, 32, 32)], loc.at[3])

    def local_cot():
        return pltpu.make_async_copy(cot_ref, dBin.at[:, at(s * 32, 32, 32)], loc.at[4])

    def local_tokens(i):
        return pltpu.make_async_copy(raw_ref.at[i], X.at[5, at(i * SEQ, LAT, LAT)], loc.at[5 + i])

    def cp_in(k):
        return remote(inb, inr.at[k - 1], in_s.at[k - 1], in_r.at[k - 1], dp, sec_of(k))

    def cp_lat(i, src):
        return remote(
            lat_ref.at[i], xin.at[i, at(src * 32, 32, 32)],
            lat_s.at[i], lat_r.at[i, src - 1], dp, 0,
        )

    def cp_cot(src, to):
        return remote(
            cot_ref, dBin.at[:, at(src * 32, 32, 32)], cot_s.at[to - 2], cot_r.at[src], dp, to
        )

    def cp_u(i, src):
        count = LAT - VIA if src == 2 else LAT
        return remote(
            raw_ref.at[i, 0:count], X.at[5, at(i * SEQ + src * LAT, count, 16)],
            u_s.at[i], u_r.at[i, src - 1], dp, 0,
        )

    def cp_via(i):
        return remote(raw_ref.at[i, LAT - VIA:LAT], relay.at[i], via_s.at[i], via_r.at[i], dp, 1)

    def cp_on(i):
        return remote(
            relay.at[i], X.at[5, at(i * SEQ + 3 * LAT - VIA, VIA, 16)],
            via_s.at[i], u_r.at[i, 3], dp, 0,
        )

    own_quarter = c * HALF + r1 * QUARTER
    own_piece = own_quarter + r2 * PIECE

    def cp_fx():
        where_ = at(own_piece, PIECE, PIECE)
        to = jnp.where(s == 3, 2, jnp.minimum(s + 1, 3))
        return remote(
            f_ref.at[0, where_], Fd.at[jnp.where(s == 3, 1, 0), where_], fx_s, fx_r, dp, to
        )

    def cp_wx():
        rows_ = at(r1 * QUARTER + r2 * PIECE, PIECE, PIECE)
        cols = at(c * 2 * D, 2 * D, 2 * D)
        return remote(w_ref.at[0, rows_, cols], Wb.at[rows_, cols], wx_s, wx_r, dp, 2)

    def cp_b(i, src):
        return remote(src.at[i], xin.at[i], b_s.at[i], b_r.at[i], dp, jnp.minimum(s + 1, 3))

    def cp_d(i):
        return remote(sendD.at[i], dBin.at[i], d_s.at[i], d_r.at[i], dp, jnp.maximum(s - 1, 0))

    def cp_e(i):
        return remote(sendD.at[i], Fd.at[1, at(i * LAT, LAT, LAT)], e_s.at[i], e_r.at[i], dp, 0)

    def cp_gu(i, blk):
        where_ = at(blk * 384 + i * LAT, LAT, LAT)
        return remote(X.at[0, where_], Fd.at[0, where_], gu_s.at[i, blk], gu_r.at[i, blk], dp, 0)

    def cp_o(i, t):
        return remote(sendB.at[i, t * 32:(t + 1) * 32], outb.at[i], o_s.at[i, t], o_r.at[i], dp, t)

    def cp_lg(i, t):
        return remote(sendD.at[i, t * 32:(t + 1) * 32], lgb.at[i], lg_s.at[i, t - 1], lg_r.at[i], dp, t)

    def cp_du(i, t):
        return remote(
            X.at[5, at(i * SEQ + t * LAT, LAT, LAT)], dUb.at[i],
            du_s.at[i, t - 1], du_r.at[i], dp, t,
        )

    def cp_a(b):
        return remote(g.at[b, at((1 - c) * HALF, HALF, HALF)], rA.at[b], a_s.at[b], a_r.at[b], mate, s)

    def half_of(j, h):
        return at(c * HALF + lax.rem(r1 + j, N) * QUARTER + h * SIDE, SIDE, SIDE)

    def cp_rb(b, j):
        source, slot, lo, to = (
            (half_of(2, 0), 2, 0, 1), (half_of(2, 1), 2, 1, 3),
            (half_of(1, 1), 0, 1, 1), (half_of(3, 0), 1, 0, 3),
            (half_of(1, 0), 0, 0, 1), (half_of(3, 1), 1, 1, 3),
        )[j]
        return remote(
            g.at[b, source], rB.at[b, slot, lo * SIDE:(lo + 1) * SIDE],
            bb_s.at[b, j], bb_r.at[b, j], peer1(to), s,
        )

    def cp_rc(b, k):
        start = own_quarter + lax.rem(r2 + k, N) * PIECE
        return remote(
            g.at[b, at(start, PIECE, PIECE)], rC.at[b, k - 1],
            c_s.at[b, k - 1], c_r.at[b, k - 1], peer2(k), s,
        )

    class Gather:
        def __init__(self, view, own, sems):
            self.view, self.own, self.sems = view, own, sems

        def d(self, k):
            piece = self.own(r2 * PIECE, PIECE)
            return remote(piece, piece, self.sems[0].at[k - 1], self.sems[1].at[k - 1], peer2(k), s)

        def d_in(self, k):
            piece = self.own(lax.rem(r2 + N - k, N) * PIECE, PIECE)
            return remote(piece, piece, self.sems[0].at[k - 1], self.sems[1].at[k - 1], peer2(k), s)

        def e(self, j):
            if j < 2:
                src, dst = self.own(0, QUARTER), self.view(c, r1 * QUARTER, QUARTER)
            else:
                far = lax.rem(r1 + (3 if j == 2 else 1), N) * QUARTER + (j - 2) * SIDE
                src = dst = self.view(c, far, SIDE)
            return remote(
                src, dst, self.sems[2].at[j], self.sems[3].at[j], peer1(1 if j % 2 == 0 else 3), s
            )

        def e_in(self, j):
            if j < 2:
                dst = self.view(c, lax.rem(r1 + 3 - 2 * j, N) * QUARTER, QUARTER)
            else:
                dst = self.view(c, lax.rem(r1 + 2, N) * QUARTER + (j - 2) * SIDE, SIDE)
            return remote(dst, dst, self.sems[2].at[j], self.sems[3].at[j], peer1(1), s)

        def f(self):
            half = self.view(c, 0, HALF)
            return remote(half, half, self.sems[4], self.sems[5], mate, s)

        def f_in(self):
            half = self.view(1 - c, 0, HALF)
            return remote(half, half, self.sems[4], self.sems[5], mate, s)

        def e1(self):
            for j in (0, 1):
                self.e(j).start()

        def e2(self):
            for j in (0, 1):
                self.e_in(j).wait_recv()
                self.e(j + 2).start()

        def e_done(self):
            for j in (2, 3):
                self.e_in(j).wait_recv()

        def drain(self):
            for k in ring:
                self.d(k).wait_send()
            for j in range(4):
                self.e(j).wait_send()
            self.f().wait_send()

    def gather_f(half):
        def view(core, start, size):
            return Fd.at[half, at(core * HALF + start, size, 16)]
        return Gather(
            view, lambda start, size: view(c, r1 * QUARTER + start, size),
            (fd_s, fd_r, fe_s, fe_r, ff_s, ff_r),
        )

    def gather_w():
        def view(core, start, size):
            return Wb.at[at(start, size, 16), at(core * 2 * D, 2 * D, 2 * D)]
        return Gather(
            view, lambda start, size: view(c, r1 * QUARTER + start, size),
            (wd_s, wd_r, we_s, we_r, wf_s, wf_r),
        )

    def gather_g(b):
        def view(core, start, size):
            return g.at[b, at(core * HALF + start, size, 16)]
        return Gather(
            view, lambda start, size: q.at[b, at(start, size, 16)],
            (gd_s.at[b], gd_r.at[b], ge_s.at[b], ge_r.at[b], gf_s.at[b], gf_r.at[b]),
        )

    def stage_b(b):
        cp_a(b).wait_recv()
        for j in (2, 1, 3, 0):
            part = at(c * HALF + lax.rem(r1 + j, N) * QUARTER, QUARTER, QUARTER)
            other = at(lax.rem(r1 + j, N) * QUARTER, QUARTER, QUARTER)
            g[b, part] = (g[b, part].astype(F32) + rA[b, other].astype(F32)).astype(BF)
            if j == 2:
                cp_rb(b, 0).start()
                cp_rb(b, 1).start()
            elif j == 1:
                cp_rb(b, 2).start()
            elif j == 3:
                cp_rb(b, 3).start()

    def sum_far(b):
        for j in (0, 1):
            cp_rb(b, j).wait_recv()
            mine = half_of(1 + 2 * j, j)
            arrived = rB[b, 2, j * SIDE:(j + 1) * SIDE].astype(F32)
            g[b, mine] = (g[b, mine].astype(F32) + arrived).astype(BF)
            cp_rb(b, 4 + j).start()

    def sum_quarter(b):
        for j in (2, 3, 4, 5):
            cp_rb(b, j).wait_recv()
        part = at(own_quarter, QUARTER, QUARTER)
        total = g[b, part].astype(F32) + rB[b, 0].astype(F32) + rB[b, 1].astype(F32)
        g[b, part] = total.astype(BF)
        for k in ring:
            cp_rc(b, k).start()

    def sum_piece(b):
        cp_a(b).wait_send()
        pl.semaphore_signal(free_a.at[b], inc=1, device_id=(mate, s), device_id_type=MESH)
        for j in range(6):
            cp_rb(b, j).wait_send()
        for k in (1, 3):
            pl.semaphore_signal(free_b.at[b], inc=1, device_id=(peer1(k), s), device_id_type=MESH)
        for k in ring:
            cp_rc(b, k).wait_recv()
        total = g[b, at(own_piece, PIECE, PIECE)].astype(F32)
        for k in ring:
            total = total + rC[b, k - 1].astype(F32)
        q[b, at(r2 * PIECE, PIECE, PIECE)] = total.astype(BF)
        for k in ring:
            gather_g(b).d(k).start()

    local_w().start()

    @pl.when(s != 0)
    def _():
        local_f().start()

    barrier = pltpu.get_barrier_semaphore()
    partners = [(dp, sec_of(k)) for k in (1, 2, 3)] + [(mate, s)]
    partners += [(peer1(k), s) for k in ring] + [(peer2(k), s) for k in ring]
    for partner in partners:
        pl.semaphore_signal(barrier, inc=1, device_id=partner, device_id_type=MESH)
    select = lax.broadcasted_iota(jnp.int32, (192, D), 1) == lax.broadcasted_iota(jnp.int32, (192, D), 0) + s * 192
    snorm = snorm_ref[0].astype(F32)
    gain = 1.0 + snorm[0:1]
    shift = snorm[1:2]
    inb[...] = jnp.zeros_like(inb)
    inb[0:2] = nn(inorm_ref[...], select.astype(F32).astype(BF))
    inb[2:4] = snorm
    nacc[...] = jnp.zeros_like(nacc)
    pl.semaphore_wait(barrier, len(partners))

    for k in (1, 2, 3):
        cp_in(k).start()

    @pl.when(s == 0)
    def _():
        local_lat().start()
        for i in range(3):
            local_tokens(i).start()

    @pl.when(s != 1)
    def _():
        cp_fx().start()

    @pl.when(s == 3)
    def _():
        cp_wx().start()

    for sec in (1, 2, 3):
        @pl.when(s == sec)
        def _():
            for i in range(3):
                cp_lat(i, sec).start()
                if sec == 2:
                    cp_via(i).start()
                cp_u(i, sec).start()

    @pl.when(s >= 2)
    def _():
        local_cot().start()

    for to in (2, 3):
        @pl.when(s != to)
        def _():
            cp_cot(s, to).start()

    def project(a, lo, hi):
        return nn(a, W[:, lo:hi])

    def latent_back(x_ref, i, da, db):
        dx, dg, dbias = ln_back(x_ref[i].astype(F32), da, gain)
        nacc[0:1] = nacc[0:1] + dg
        nacc[1:2] = nacc[1:2] + dbias
        return db.astype(F32) + dx

    local_w().wait()

    def send_du(i):
        in_gain = 1.0 + inb[0:1] + inr[0, 0:1] + inr[1, 0:1] + inr[2, 0:1]
        at_rows = rows(i, SEQ)
        du = nt(X[3, at_rows], W[:, D:2 * D]) + nt(X[4, at_rows], W[:, 2 * D:3 * D])
        X[1, at_rows] = du.astype(BF)

        @pl.loop(0, 4)
        def _(j):
            part = at(i * SEQ + j * LAT, LAT, LAT)
            dx, dg, dbias = ln_back(X[5, part].astype(F32), X[1, part].astype(F32), in_gain)
            X[5, part] = dx.astype(BF)
            nacc[2:3] = nacc[2:3] + dg
            nacc[3:4] = nacc[3:4] + dbias
        dUb[i] = X[5, at(i * SEQ, LAT, LAT)]
        for t in (1, 2, 3):
            cp_du(i, t).start()

    def plane_0():
        local_lat().wait()
        for k in (1, 2, 3):
            cp_in(k).wait_recv()
        in_all = inb[...] + inr[0] + inr[1] + inr[2]

        @pl.loop(0, 3)
        def _(i):
            for src in (1, 2, 3):
                cp_lat(i, src).wait_recv()
            x = xin[i].astype(F32)
            xhat, _ = unit(x)
            a = (xhat * gain + shift).astype(BF)
            lat_rows = rows(i, LAT)
            A[lat_rows] = a
            Q[lat_rows] = project(a, 0, D).astype(BF)
            for src in (1, 2, 3):
                cp_u(i, src).wait_recv()
            cp_on(i).wait_recv()
            local_tokens(i).wait()

            @pl.loop(0, 4)
            def _(j):
                part = at(i * SEQ + j * LAT, LAT, LAT)
                xhat, _ = unit(X[5, part].astype(F32))
                X[0, part] = (xhat * (1.0 + in_all[0:1]) + in_all[1:2]).astype(BF)
            u = X[0, rows(i, SEQ)]
            kv = [X.at[j, rows(i, SEQ)] for j in (1, 2)]
            kv[0][...] = project(u, D, 2 * D).astype(BF)
            kv[1][...] = project(u, 2 * D, 3 * D).astype(BF)
            where_ = lax.broadcasted_iota(jnp.int32, (SEQ, 256), 0)
            clip = jnp.zeros((SEQ, 256), jnp.int32)
            end = jnp.int32(0)
            for j in range(4):
                end = end + len_ref[i, j]
                clip = clip + (where_ >= end).astype(jnp.int32)
            ids = clip_ref[pl.ds(i, 1)]
            ids = jnp.concatenate([ids, ids], 1)
            attn_fwd(Q.at[lat_rows], kv[0], kv[1], clip == ids, PT.at[i], O.at[lat_rows])
            b = x + project(O[lat_rows], 3 * D, 4 * D)
            sendB[i] = b.astype(BF)
            cp_b(i, sendB).start()

        def latent_out(i):
            db = dBin[i]
            grad = latent_back(xin, i, nt(dQ[rows(i, LAT)], W[:, :D]), db).astype(BF)
            sendD[i] = grad
            lgb[i] = grad[0:32]
            for t in (1, 2, 3):
                cp_lg(i, t).start()

        def item_back(i):
            cp_d(i).wait_recv()
            dO[...] = nt(dBin[i], W[:, 3 * D:]).astype(BF)
            kv = [X.at[j, rows(i, SEQ)] for j in (1, 2, 3, 4)]
            lat_rows = rows(i, LAT)
            attn_bwd(Q.at[lat_rows], kv[0], kv[1], PT.at[i], dO, dQ.at[lat_rows], kv[2], kv[3])

        def weight_grads(tokens, latents, add):
            def put(b, rows_, grad):
                g[b, rows_] = ((g[b, rows_].astype(F32) + grad) if add else grad).astype(BF)
            count = latents.stop - latents.start
            db = dBin[latents.start // LAT:latents.stop // LAT].reshape(count, D)
            put(0, slice(0, D), tn(A[latents], dQ[latents]))
            put(1, slice(D, 2 * D), tn(O[latents], db))

            @pl.loop(0, 2)
            def _(b):
                put(b, at((1 - b) * D, D, D), tn(X[0, tokens], X[3 + b, tokens]))

        @pl.loop(0, 3)
        def _(i):
            @pl.when(i == 2)
            def _():
                for t in range(3):
                    cp_e(t).wait_recv()
                    for blk in range(2):
                        cp_gu(t, blk).wait_recv()

                @pl.loop(0, 2)
                def _(blk):
                    g[2, at(blk * D, D, D)] = tn(Fd[0, at(blk * 384, 384, 384)], Fd[1, 0:384]).astype(BF)
                cp_a(2).start()
                weight_grads(slice(0, 2 * SEQ), slice(0, 2 * LAT), False)
                apart(stage_b, 2)
            item_back(i)

            @pl.when(i < 2)
            def _():
                latent_out(i)
        weight_grads(slice(2 * SEQ, 3 * SEQ), slice(2 * LAT, 3 * LAT), True)
        cp_a(0).start()
        cp_a(1).start()
        pl.loop(2, 2 + once)(latent_out)

    def plane_2():
        for k in (1, 2, 3):
            cp_in(k).wait_recv()
        far_gain = 1.0 + inr[2, 2:3]
        far_shift = inr[2, 3:4]
        w3, f3 = gather_w(), gather_f(1)
        cp_fx().wait_recv()
        cp_wx().wait_recv()
        for k in ring:
            w3.d(k).start()
            f3.d(k).start()
        for one in (w3, f3):
            for k in ring:
                one.d_in(k).wait_recv()
            one.e1()
        for one in (w3, f3):
            one.e2()
        for one in (w3, f3):
            one.e_done()
            one.f().start()
        local_f().wait()
        local_cot().wait()
        for src in (0, 1, 3):
            cp_cot(src, 2).wait_recv()
        for one in (w3, f3):
            one.f_in().wait_recv()

        @pl.loop(0, 3)
        def _(i):
            lat_rows = rows(i, LAT)
            cp_b(i, yin).wait_recv()
            x = xin[i].astype(F32)
            xhat, _ = unit(x)
            a = (xhat * gain + shift).astype(BF)
            A[lat_rows] = a
            Q[lat_rows] = project(a, 0, D).astype(BF)
            X[1, lat_rows] = project(a, D, 2 * D).astype(BF)
            X[2, lat_rows] = project(a, 2 * D, 3 * D).astype(BF)
            ids = jnp.broadcast_to(clip_ref[pl.ds(i, 1)].astype(F32), (LAT, LAT))
            mask = jnp.concatenate([ids, ids], 1) == jnp.concatenate([ids.T, ids.T], 1)
            attn_fwd(
                Q.at[lat_rows], X.at[1, lat_rows], X.at[2, lat_rows], mask,
                PT.at[i, :, 0:LAT], O.at[lat_rows],
            )
            middle = (x + project(O[lat_rows], 3 * D, 4 * D)).astype(BF)
            yin[i] = middle
            cp_b(i, yin).start()
            x = middle.astype(F32)
            xhat, _ = unit(x)
            a = (xhat * far_gain + far_shift).astype(BF)
            b = ffn_fwd(i, x, a, Wb, Fd, X, 2).astype(BF)
            sendB[i] = b
            outb[i] = b[64:96]
            for t in (0, 1, 3):
                cp_o(i, t).start()
            db = dBin[i]
            dx, _, _ = ln_back(x, ffn_bwd(i, db, Wb, Fd, X, False), far_gain)
            db = (db.astype(F32) + dx).astype(BF)
            dBm[i] = db
            dO[...] = nt(db, W[:, 3 * D:]).astype(BF)
            attn_bwd(
                Q.at[lat_rows], X.at[1, lat_rows], X.at[2, lat_rows], PT.at[i, :, 0:LAT],
                dO, dQ.at[lat_rows], X.at[3, lat_rows], X.at[4, lat_rows],
            )
            da = nt(dQ[lat_rows], W[:, :D]) + nt(X[3, lat_rows], W[:, D:2 * D])
            da = da + nt(X[4, lat_rows], W[:, 2 * D:3 * D])
            sendD[i] = latent_back(xin, i, da, db).astype(BF)
            cp_d(i).start()
            cp_e(i).start()

        def all_grads(b):
            if b == 2:
                db = dBin[...].reshape(3 * LAT, D)
                pair = tn(X[0, 0:384], db), tn(X[0, 384:768], db)
            elif b == 0:
                pair = tn(A[...], dQ[...]), tn(A[...], X[3, 0:3 * LAT])
            else:
                pair = tn(A[...], X[4, 0:3 * LAT]), tn(O[...], dBm[...].reshape(3 * LAT, D))
            g[b, 0:D] = pair[0].astype(BF)
            g[b, D:] = pair[1].astype(BF)

        for b in ORDER:
            apart(all_grads, b)
            cp_a(b).start()

    def plane_odd():
        def relay_on(i):
            @pl.when(s == 1)
            def _():
                cp_via(i).wait_recv()
                cp_on(i).start()

        prior = gather_f(0)
        relay_on(0)
        cp_fx().wait_recv()
        for k in ring:
            prior.d(k).start()
        relay_on(1)
        for k in ring:
            prior.d_in(k).wait_recv()
        prior.e1()
        relay_on(2)
        prior.e2()
        prior.e_done()
        prior.f().start()
        local_f().wait()
        prior.f_in().wait_recv()

        @pl.when(s == 3)
        def _():
            local_cot().wait()
            for src in (0, 1, 2):
                cp_cot(src, 3).wait_recv()

        def store_grads(b, first, count, add):
            own = slice(first * LAT, (first + count) * LAT)

            @pl.loop(0, 2)
            def _(j):
                block = (2 if b == 2 else 2 * b) + j
                units = at(block * 384 + first * LAT, count * LAT, LAT)
                if b == 2:
                    grad = tn(X[0, units], dBin[first:first + count].reshape(count * LAT, D))
                else:
                    grad = tn(A[own], X[1, units])
                here = at(j * D, D, D)
                g[b, here] = ((g[b, here].astype(F32) + grad) if add else grad).astype(BF)

        def forward(i):
            cp_b(i, sendB).wait_recv()
            x = xin[i].astype(F32)
            xhat, _ = unit(x)
            a = (xhat * gain + shift).astype(BF)
            A[rows(i, LAT)] = a
            return ffn_fwd(i, x, a, W, Fd, X, 4).astype(BF)

        def backward(i):
            db = dBin[i]
            return latent_back(xin, i, ffn_bwd(i, db, W, Fd, X, True), db).astype(BF)

        @pl.loop(0, 6)
        def _(step):
            last = s == 3
            ahead = jnp.where(last, lax.rem(step, 2) == 0, step < 3)
            i = jnp.where(last, step // 2, lax.rem(step, 3))

            @pl.when(ahead)
            def _():
                sendB[i] = forward(i)

                @pl.when(s == 1)
                def _():
                    cp_b(i, sendB).start()
                    for blk in range(2):
                        cp_gu(i, blk).start()

            @pl.when(jnp.logical_not(ahead))
            def _():
                @pl.when((s == 1) & (i == 2))
                def _():
                    for b in ORDER:
                        store_grads(b, 0, 2, False)

                @pl.when(s == 1)
                def _():
                    cp_d(i).wait_recv()
                sendD[i] = backward(i)

                @pl.when(s == 1)
                def _():
                    cp_d(i).start()

        for b in ORDER:
            @pl.when(s == 1)
            def _():
                store_grads(b, 2, 1, True)

            @pl.when(s == 3)
            def _():
                store_grads(b, 0, 3, False)
            cp_a(b).start()

    def spread_quarter(b):
        for k in ring:
            cp_rc(b, k).wait_send()
        pl.semaphore_wait(free_b.at[b], 2)
        for k in ring:
            gather_g(b).d_in(k).wait_recv()
        gather_g(b).e1()
        g[b, at(own_quarter, QUARTER, QUARTER)] = q[b]

    def spread_far(b):
        gather_g(b).e2()

    def leave(b, h, act):
        src = g.at[b, at(h * HALF, HALF, HALF)]

        @pl.when(b == 2)
        def _():
            act(pltpu.make_async_copy(src, down_ref.at[0, at(h * HALF, HALF, HALF)], g_sem.at[b, h]))

        @pl.when(b < 2)
        def _():
            block = at(jnp.minimum(2 * b + h, 3) * D, D, D)
            act(pltpu.make_async_copy(src, entry_ref.at[0, :, block], g_sem.at[b, h]))

    def spread_half(b):
        gather_g(b).e_done()
        pl.semaphore_wait(free_a.at[b], 1)
        gather_g(b).f().start()
        leave(b, c, lambda copy: copy.start())

    def finish(b):
        gather_g(b).f_in().wait_recv()
        leave(b, 1 - c, lambda copy: copy.start())

    def small(step, buf, ss, rs, k, dp_to, sec_to):
        return remote(tsrc.at[step], buf.at[k], ss.at[k], rs.at[k], dp_to, sec_to)

    def own_rows():
        @pl.when(odd)
        def _():
            for k in (1, 2, 3):
                cp_in(k).wait_recv()

        @pl.loop(0, 3)
        def _(i):
            @pl.when(s != 2)
            def _():
                cp_o(i, 0).wait_recv()

            @pl.when(s != 0)
            def _():
                cp_lg(i, 1).wait_recv()
                cp_du(i, 1).wait_recv()
            igrad_ref[i] = dUb[i]
            out_ref[i] = outb[i]
            lgrad_ref[i] = lgb[i]

    def small_x(k):
        return remote(tsrc.at[0], tX.at[0], tx_s.at[k - 1], tx_r.at[0], dp, sec_of(k))

    def small_mate():
        tsrc[1] = nacc[...]
        small(1, tC, tc_s, tc_r, 0, mate, s).start()

    def small_ring1():
        small(1, tC, tc_s, tc_r, 0, mate, s).wait_recv()
        tsrc[2] = tsrc[1] + tC[0]
        for k in ring:
            small(2, t1, t1_s, t1_r, k - 1, peer1(k), s).start()

    def small_ring2():
        for k in ring:
            small(2, t1, t1_s, t1_r, k - 1, peer1(k), s).wait_recv()
        tsrc[3] = tsrc[2] + t1[0] + t1[1] + t1[2]
        for k in ring:
            small(3, t2, t2_s, t2_r, k - 1, peer2(k), s).start()

    def small_out(sec):
        for k in ring:
            small(3, t2, t2_s, t2_r, k - 1, peer2(k), s).wait_recv()
        total = tsrc[3] + t2[0] + t2[1] + t2[2]
        tsrc[0] = total
        tiny_ref[...] = total

        if sec == 0:
            for k in (1, 2, 3):
                small_x(k).start()

    def small_done():
        @pl.when(s != 0)
        def _():
            small_x(1).wait_recv()
            tiny_ref[2:4] = tX[0, 2:4]

    def sums(sec):
        stages = (
            stage_b, sum_far, sum_quarter, sum_piece, spread_quarter, spread_far, spread_half, finish
        )

        @pl.loop(0, len(stages) + 2)
        def _(turn):
            for k, stage in enumerate(stages):
                t = turn - k
                due = (t >= 0) & (t < 3)
                if k == 0 and sec == 0:
                    due = due & (t > 0)
                pl.when(due)(functools.partial(stage, lax.rem(t + 2, 3)))

            if sec == 0:
                pl.when((turn > 0) & (turn < 4))(functools.partial(send_du, turn - 1))
            for k, step in ((4, small_mate), (5, small_ring1), (6, small_ring2), (8, functools.partial(small_out, sec))):
                pl.when(turn == k)(step)

        @pl.loop(0, 3)
        def _(b):
            for h in range(2):
                leave(b, h, lambda copy: copy.wait())

    def drain(sec):
        for k in (1, 2, 3):
            cp_in(k).wait_send()
        small(1, tC, tc_s, tc_r, 0, mate, s).wait_send()
        for k in ring:
            small(2, t1, t1_s, t1_r, k - 1, peer1(k), s).wait_send()
            small(3, t2, t2_s, t2_r, k - 1, peer2(k), s).wait_send()
        pl.loop(0, 3)(lambda b: gather_g(b).drain())
        for to in (2, 3):
            if sec != to:
                cp_cot(sec, to).wait_send()
        if sec != 1:
            cp_fx().wait_send()
        if sec == 3:
            cp_wx().wait_send()
        if sec == 2:
            gather_w().drain()
            gather_f(1).drain()
        if sec in (1, 3):
            gather_f(0).drain()
        for i in range(3):
            if sec > 0:
                cp_lat(i, sec).wait_send()
                cp_u(i, sec).wait_send()
            if sec < 3:
                cp_b(i, sendB).wait_send()
            if sec in (1, 2):
                cp_via(i).wait_send()
                cp_d(i).wait_send()
            if sec == 0 and i == 0:
                for k in (1, 2, 3):
                    small_x(k).wait_send()
            if sec == 0:
                for t in (1, 2, 3):
                    cp_lg(i, t).wait_send()
                    cp_du(i, t).wait_send()
            if sec == 1:
                for blk in range(2):
                    cp_gu(i, blk).wait_send()
            if sec == 2:
                cp_e(i).wait_send()
                for t in (0, 1, 3):
                    cp_o(i, t).wait_send()

    @pl.when(s == 2)
    def _():
        plane_2()
        sums(2)
        drain(2)

    @pl.when(odd)
    def _():
        plane_odd()
        sums(1)
        for sec in (1, 3):
            pl.when(s == sec)(functools.partial(drain, sec))

    @pl.when(s == 0)
    def _():
        plane_0()
        sums(0)
        drain(0)

    own_rows()
    small_done()


def widen(
    out_in, lgrad_in, igrad_in, entry_in, down_in, tiny_in,
    out_ref, lgrad_ref, igrad_ref, entry_ref, down_ref, norm_ref, in_norm_ref,
):
    igrad_ref[...] = igrad_in[...].astype(F32)
    entry_ref[...] = entry_in[...].astype(F32)
    down_ref[...] = down_in[...].astype(F32)

    @pl.when(pl.program_id(0) == 0)
    def _():
        out_ref[...] = out_in[...]
        lgrad_ref[...] = lgrad_in[...].astype(F32)
        norm_ref[...] = tiny_in[0:2]
        s = lax.axis_index("section")
        mine = jnp.zeros((2, 192), F32)
        for k in range(4):
            mine = jnp.where(s == k, tiny_in[2:4, k * 192:(k + 1) * 192], mine)
        in_norm_ref[...] = mine


def on_device(lat, raw, cot, lengths, clip, w, f, snorm, inorm):
    def low(*shape):
        return pltpu.VMEM(shape, BF)

    def full(*shape):
        return pltpu.VMEM(shape, F32)

    def sem(*shape):
        return pltpu.SemaphoreType.DMA(shape)

    def pair(*shape):
        return [sem(*shape), sem(*shape)]

    one = pltpu.SemaphoreType.DMA
    ring = N - 1
    scratch = [
        low(D, 4 * D), low(D, 4 * D), low(2, 2 * D, D), low(3, 2 * D, D), low(6, 2 * D, D),
        low(3, 6, SEQ, 256), low(3, HALF, D), low(3, 3, QUARTER, D), low(3, ring, PIECE, D), low(3, QUARTER, D),
        *[low(3, LAT, D)] * 6,
        *[low(3 * LAT, D)] * 4, low(LAT, D),
        low(3, VIA, D), low(3, LAT, D), low(3, 32, D), low(3, 32, D),
        full(8, D), full(3, 8, D), full(8, D), full(4, 8, D),
        full(3, 8, D), full(1, 8, D), full(ring, 8, D), full(ring, 8, D),
        sem(8), *pair(3), sem(3), sem(3, 3), sem(2), sem(4), sem(3), sem(3, 4), *pair(3), one, one, one, one,
        *pair(3), *pair(3), *pair(3), *pair(3, 2), sem(3, 4), sem(3), sem(3, 3), sem(3), sem(3, 3), sem(3),
        *pair(3), *pair(3, 6), *pair(3, ring), *pair(3, ring), *pair(3, 4), *pair(3),
        *pair(ring), *pair(4), one, one, *pair(ring), *pair(4), one, one,
        *pair(3), *pair(1), *pair(ring), *pair(ring), sem(3, 2),
        pltpu.SemaphoreType.REGULAR((3,)), pltpu.SemaphoreType.REGULAR((3,)),
    ]
    hbm = pl.BlockSpec(memory_space=pl.ANY)
    vmem = pl.BlockSpec(memory_space=pltpu.VMEM)
    inner = pl.pallas_call(
        kernel,
        name="layers",
        out_shape=(
            jax.ShapeDtypeStruct(lat.shape, BF),
            jax.ShapeDtypeStruct(lat.shape, BF),
            jax.ShapeDtypeStruct(raw.shape, BF),
            jax.ShapeDtypeStruct(w.shape, BF),
            jax.ShapeDtypeStruct(f.shape, BF),
            jax.ShapeDtypeStruct((8, D), F32),
        ),
        in_specs=[hbm, hbm, hbm, pl.BlockSpec(memory_space=pltpu.SMEM), vmem, hbm, hbm, vmem, vmem],
        out_specs=(vmem, vmem, vmem, hbm, hbm, vmem),
        scratch_shapes=scratch,
        compiler_params=pltpu.CompilerParams(
            collective_id=0, has_side_effects=True, vmem_limit_bytes=60 * 2**20
        ),
    )(lat, raw, cot, lengths, clip, w, f, snorm, inorm)
    steps = 4

    def by_rows(array):
        rest = array.shape[1:]
        return pl.BlockSpec((array.shape[0] // steps, *rest), lambda t: (t,) + (0,) * len(rest))

    def whole(*shape):
        return pl.BlockSpec(shape, lambda t: (0,) * len(shape))

    out, lgrad, igrad, entry, down, tiny = inner
    igrad = igrad.reshape(3 * LAT, D)
    entry, down = entry[0], down[0]
    final = pl.pallas_call(
        widen,
        name="widen",
        grid=(steps,),
        out_shape=(
            jax.ShapeDtypeStruct(lat.shape, BF),
            jax.ShapeDtypeStruct(lat.shape, F32),
            jax.ShapeDtypeStruct(igrad.shape, F32),
            jax.ShapeDtypeStruct(entry.shape, F32),
            jax.ShapeDtypeStruct(down.shape, F32),
            jax.ShapeDtypeStruct((2, D), F32),
            jax.ShapeDtypeStruct((2, 192), F32),
        ),
        in_specs=[
            whole(*lat.shape), whole(*lat.shape), by_rows(igrad), by_rows(entry), by_rows(down), whole(8, D)
        ],
        out_specs=(
            whole(*lat.shape), whole(*lat.shape), by_rows(igrad), by_rows(entry), by_rows(down),
            whole(2, D), whole(2, 192),
        ),
        compiler_params=pltpu.CompilerParams(vmem_limit_bytes=60 * 2**20),
    )(out, lgrad, igrad, entry, down, tiny)
    out, lgrad, igrad, entry, down, norm, in_norm = final
    return out, lgrad, igrad.reshape(raw.shape), entry[None], down[None], norm[None], in_norm


def solution(mesh):
    rows_split = P("dp", "section", None)
    weight = P("section", None, None)
    return jax.shard_map(
        on_device,
        mesh=mesh,
        in_specs=(
            rows_split, rows_split, rows_split, P("dp", None), P("dp", None),
            weight, weight, weight, P(None, "section"),
        ),
        out_specs=(rows_split, rows_split, rows_split, weight, weight, weight, P(None, "section")),
        check_vma=False,
    )
```

```python
import functools

import jax
import jax.numpy as jnp
from jax import lax
from jax.experimental import pallas as pl
from jax.experimental.pallas import tpu as pltpu
from jax.sharding import PartitionSpec as P


D = 768
LAT = 128
SEQ = 512
EPS = 1e-5
NEG = -1e9
F32 = jnp.float32
BF = jnp.bfloat16


def nn(a, b):
    return jnp.dot(a, b, preferred_element_type=F32)


def nt(a, b):
    return lax.dot_general(a, b, (((1,), (1,)), ((), ())), preferred_element_type=F32)


def tn(a, b):
    return lax.dot_general(a, b, (((0,), (0,)), ((), ())), preferred_element_type=F32)


def unit(x):
    mean = jnp.mean(x, -1, keepdims=True)
    cen = x - mean
    var = jnp.mean(cen * cen, -1, keepdims=True)
    rstd = lax.rsqrt(var + EPS)
    return cen * rstd, rstd


def ln_back(x, da, gain):
    xhat, rstd = unit(x)
    dx = da * gain
    m1 = jnp.mean(dx, -1, keepdims=True)
    m2 = jnp.mean(dx * xhat, -1, keepdims=True)
    grad = rstd * (dx - m1 - xhat * m2)
    return grad, jnp.sum(da * xhat, 0, keepdims=True), jnp.sum(da, 0, keepdims=True)


def gelu_pair(z):
    a = jnp.abs(z)
    t = 1.0 / (1.0 + (0.3275911 * 0.7071067811865476) * a)
    e = jnp.exp(-0.5 * (z * z))
    p = t * (0.254829592 + t * (-0.284496736 + t * (1.421413741 + t * (-1.453152027 + t * 1.061405429))))
    half = (0.5 * p) * e
    cdf = jnp.where(z >= 0, 1.0 - half, half)
    return z * cdf, cdf + z * (0.3989422804014327 * e)


def rows(i, n):
    return pl.ds(pl.multiple_of(i * n, n), n)


def ffn_fwd(i, x, a, W, Fd, X, kept):
    total = x
    for c in range(4):
        gate, slope = gelu_pair(nn(a, W[:, c * D:(c + 1) * D]))
        gate = gate.astype(BF)
        where_ = pl.ds(pl.multiple_of(c * 384 + i * LAT, LAT), LAT)
        if c < kept:
            X[0, where_] = gate
        X[5, where_] = slope.astype(BF)
        total = total + nn(gate, Fd[c // 2, (c % 2) * D:(c % 2 + 1) * D])
    return total


def ffn_bwd(i, db, W, Fd, X, kept):
    da = None
    for c in range(4):
        dg = nt(db, Fd[c // 2, (c % 2) * D:(c % 2 + 1) * D])
        where_ = pl.ds(pl.multiple_of(c * 384 + i * LAT, LAT), LAT)
        dz = (X[5, where_].astype(F32) * dg).astype(BF)
        if kept:
            X[1, where_] = dz
        part = nt(dz, W[:, c * D:(c + 1) * D])
        da = part if da is None else da + part
    return da


def halves(m):
    lane = lax.broadcasted_iota(jnp.int32, m.shape, 1)
    zero = jnp.zeros_like(m)
    return jnp.concatenate([jnp.where(lane < 64, m, zero), jnp.where(lane >= 64, m, zero)], 0)


def unhalves(mt):
    q = mt.shape[1] // 2
    return jnp.concatenate([mt[0:64, 0:q], mt[64:128, q:2 * q]], 0).T


def attn_fwd(q, k, v, maskf, PT, O):
    for p in range(6):
        cols = slice(p * 128, (p + 1) * 128)
        qs = halves(q[:, cols])
        s = nt(k[:, cols], qs) * 0.125
        s = jnp.where(maskf, s, NEG)
        m = jnp.max(s, 0, keepdims=True)
        e = jnp.exp(s - m)
        l = jnp.sum(e, 0, keepdims=True)
        pt = (e * (1.0 / l)).astype(BF)
        PT[p] = pt
        ot = tn(v[:, cols], pt)
        O[:, cols] = unhalves(ot).astype(BF)


def attn_bwd(q, k, v, PT, do, dq, dk, dv):
    for p in range(6):
        cols = slice(p * 128, (p + 1) * 128)
        dos = halves(do[:, cols])
        qs = halves(q[:, cols])
        pt = PT[p]
        dp = nt(v[:, cols], dos)
        ptf = pt.astype(F32)
        w = dp * ptf
        delta = jnp.sum(w, 0, keepdims=True)
        ds = (w - ptf * delta).astype(BF)
        dk[:, cols] = (nn(ds, qs) * 0.125).astype(BF)
        dv[:, cols] = nn(pt, dos).astype(BF)
        dqt = tn(k[:, cols], ds)
        dq[:, cols] = (unhalves(dqt) * 0.125).astype(BF)


HALF = 768
QUARTER = 192
PIECE = 48
SIDE = 96
VIA = 80
N = 4
MESH = pl.DeviceIdType.MESH


ORDER = (2, 0, 1)


def kernel(
    lat_ref, raw_ref, cot_ref, len_ref, clip_ref, w_ref, f_ref, snorm_ref, inorm_ref,
    out_ref, lgrad_ref, igrad_ref, entry_ref, down_ref, tiny_ref,
    W, Wb, Fd, g, X, PT, rA, rB, rC, q, xin, yin, dBin, dBm, sendB, sendD,
    A, Q, O, dQ, dO, relay, dUb, outb, lgb, inb, inr, nacc, tsrc, tX, tC, t1, t2,
    loc, in_s, in_r, lat_s, lat_r, cot_s, cot_r, u_s, u_r, via_s, via_r, fx_s, fx_r, wx_s, wx_r,
    b_s, b_r, d_s, d_r, e_s, e_r, gu_s, gu_r, o_s, o_r, lg_s, lg_r, du_s, du_r,
    a_s, a_r, bb_s, bb_r, c_s, c_r, gd_s, gd_r, ge_s, ge_r, gf_s, gf_r,
    fd_s, fd_r, fe_s, fe_r, ff_s, ff_r, wd_s, wd_r, we_s, we_r, wf_s, wf_r,
    tx_s, tx_r, tc_s, tc_r, t1_s, t1_r, t2_s, t2_r, g_sem, free_a, free_b,
):
    s = lax.axis_index("section")
    dp = lax.axis_index("dp")
    c = lax.rem(dp, 2)
    z = lax.rem(dp // 2, N)
    y = dp // (2 * N)
    odd = lax.rem(s, 2) == 1
    r1 = y * (1 - c) + z * c
    r2 = z * (1 - c) + y * c
    mate = dp + 1 - 2 * c
    ring = range(1, N)
    once = jnp.minimum(s + 1, 1)

    def apart(work, *args):
        @pl.loop(0, once)
        def _(_):
            work(*args)

    def sec_of(k):
        return lax.rem(s + k, 4)

    def peer1(k):
        other = lax.rem(r1 + k, N)
        return ((other * (1 - c) + y * c) * N + z * (1 - c) + other * c) * 2 + c

    def peer2(k):
        other = lax.rem(r2 + k, N)
        return ((y * (1 - c) + other * c) * N + other * (1 - c) + z * c) * 2 + c

    def at(start, size, unit_size):
        return pl.ds(pl.multiple_of(start, unit_size), size)

    def remote(src, dst, send_sem, recv_sem, dp_to, sec_to):
        return pltpu.make_async_remote_copy(
            src_ref=src, dst_ref=dst, send_sem=send_sem, recv_sem=recv_sem,
            device_id=(dp_to, sec_to), device_id_type=MESH,
        )

    def local_w():
        return pltpu.make_async_copy(w_ref.at[0], W, loc.at[0])

    def local_f():
        return pltpu.make_async_copy(f_ref.at[0], Fd.at[jnp.where(odd, 1, 0)], loc.at[1])

    def local_lat():
        return pltpu.make_async_copy(lat_ref, xin.at[:, at(s * 32, 32, 32)], loc.at[3])

    def local_cot():
        return pltpu.make_async_copy(cot_ref, dBin.at[:, at(s * 32, 32, 32)], loc.at[4])

    def local_tokens(i):
        return pltpu.make_async_copy(raw_ref.at[i], X.at[5, at(i * SEQ, LAT, LAT)], loc.at[5 + i])

    def cp_in(k):
        return remote(inb, inr.at[k - 1], in_s.at[k - 1], in_r.at[k - 1], dp, sec_of(k))

    def cp_lat(i, src):
        return remote(
            lat_ref.at[i], xin.at[i, at(src * 32, 32, 32)],
            lat_s.at[i], lat_r.at[i, src - 1], dp, 0,
        )

    def cp_cot(src, to):
        return remote(
            cot_ref, dBin.at[:, at(src * 32, 32, 32)], cot_s.at[to - 2], cot_r.at[src], dp, to
        )

    def cp_u(i, src):
        count = LAT - VIA if src == 2 else LAT
        return remote(
            raw_ref.at[i, 0:count], X.at[5, at(i * SEQ + src * LAT, count, 16)],
            u_s.at[i], u_r.at[i, src - 1], dp, 0,
        )

    def cp_via(i):
        return remote(raw_ref.at[i, LAT - VIA:LAT], relay.at[i], via_s.at[i], via_r.at[i], dp, 1)

    def cp_on(i):
        return remote(
            relay.at[i], X.at[5, at(i * SEQ + 3 * LAT - VIA, VIA, 16)],
            via_s.at[i], u_r.at[i, 3], dp, 0,
        )

    own_quarter = c * HALF + r1 * QUARTER
    own_piece = own_quarter + r2 * PIECE

    def cp_fx():
        where_ = at(own_piece, PIECE, PIECE)
        to = jnp.where(s == 3, 2, jnp.minimum(s + 1, 3))
        return remote(
            f_ref.at[0, where_], Fd.at[jnp.where(s == 3, 1, 0), where_], fx_s, fx_r, dp, to
        )

    def cp_wx():
        rows_ = at(r1 * QUARTER + r2 * PIECE, PIECE, PIECE)
        cols = at(c * 2 * D, 2 * D, 2 * D)
        return remote(w_ref.at[0, rows_, cols], Wb.at[rows_, cols], wx_s, wx_r, dp, 2)

    def cp_b(i, src):
        return remote(src.at[i], xin.at[i], b_s.at[i], b_r.at[i], dp, jnp.minimum(s + 1, 3))

    def cp_d(i):
        return remote(sendD.at[i], dBin.at[i], d_s.at[i], d_r.at[i], dp, jnp.maximum(s - 1, 0))

    def cp_e(i):
        return remote(sendD.at[i], Fd.at[1, at(i * LAT, LAT, LAT)], e_s.at[i], e_r.at[i], dp, 0)

    def cp_gu(i, blk):
        where_ = at(blk * 384 + i * LAT, LAT, LAT)
        return remote(X.at[0, where_], Fd.at[0, where_], gu_s.at[i, blk], gu_r.at[i, blk], dp, 0)

    def cp_o(i, t):
        return remote(sendB.at[i, t * 32:(t + 1) * 32], outb.at[i], o_s.at[i, t], o_r.at[i], dp, t)

    def cp_lg(i, t):
        return remote(sendD.at[i, t * 32:(t + 1) * 32], lgb.at[i], lg_s.at[i, t - 1], lg_r.at[i], dp, t)

    def cp_du(i, t):
        return remote(
            X.at[5, at(i * SEQ + t * LAT, LAT, LAT)], dUb.at[i],
            du_s.at[i, t - 1], du_r.at[i], dp, t,
        )

    def cp_a(b):
        return remote(g.at[b, at((1 - c) * HALF, HALF, HALF)], rA.at[b], a_s.at[b], a_r.at[b], mate, s)

    def half_of(j, h):
        return at(c * HALF + lax.rem(r1 + j, N) * QUARTER + h * SIDE, SIDE, SIDE)

    def cp_rb(b, j):
        source, slot, lo, to = (
            (half_of(2, 0), 2, 0, 1), (half_of(2, 1), 2, 1, 3),
            (half_of(1, 1), 0, 1, 1), (half_of(3, 0), 1, 0, 3),
            (half_of(1, 0), 0, 0, 1), (half_of(3, 1), 1, 1, 3),
        )[j]
        return remote(
            g.at[b, source], rB.at[b, slot, lo * SIDE:(lo + 1) * SIDE],
            bb_s.at[b, j], bb_r.at[b, j], peer1(to), s,
        )

    def cp_rc(b, k):
        start = own_quarter + lax.rem(r2 + k, N) * PIECE
        return remote(
            g.at[b, at(start, PIECE, PIECE)], rC.at[b, k - 1],
            c_s.at[b, k - 1], c_r.at[b, k - 1], peer2(k), s,
        )

    class Gather:
        def __init__(self, view, own, sems):
            self.view, self.own, self.sems = view, own, sems

        def d(self, k):
            piece = self.own(r2 * PIECE, PIECE)
            return remote(piece, piece, self.sems[0].at[k - 1], self.sems[1].at[k - 1], peer2(k), s)

        def d_in(self, k):
            piece = self.own(lax.rem(r2 + N - k, N) * PIECE, PIECE)
            return remote(piece, piece, self.sems[0].at[k - 1], self.sems[1].at[k - 1], peer2(k), s)

        def e(self, j):
            if j < 2:
                src, dst = self.own(0, QUARTER), self.view(c, r1 * QUARTER, QUARTER)
            else:
                far = lax.rem(r1 + (3 if j == 2 else 1), N) * QUARTER + (j - 2) * SIDE
                src = dst = self.view(c, far, SIDE)
            return remote(
                src, dst, self.sems[2].at[j], self.sems[3].at[j], peer1(1 if j % 2 == 0 else 3), s
            )

        def e_in(self, j):
            if j < 2:
                dst = self.view(c, lax.rem(r1 + 3 - 2 * j, N) * QUARTER, QUARTER)
            else:
                dst = self.view(c, lax.rem(r1 + 2, N) * QUARTER + (j - 2) * SIDE, SIDE)
            return remote(dst, dst, self.sems[2].at[j], self.sems[3].at[j], peer1(1), s)

        def f(self):
            half = self.view(c, 0, HALF)
            return remote(half, half, self.sems[4], self.sems[5], mate, s)

        def f_in(self):
            half = self.view(1 - c, 0, HALF)
            return remote(half, half, self.sems[4], self.sems[5], mate, s)

        def e1(self):
            for j in (0, 1):
                self.e(j).start()

        def e2(self):
            for j in (0, 1):
                self.e_in(j).wait_recv()
                self.e(j + 2).start()

        def e_done(self):
            for j in (2, 3):
                self.e_in(j).wait_recv()

        def drain(self):
            for k in ring:
                self.d(k).wait_send()
            for j in range(4):
                self.e(j).wait_send()
            self.f().wait_send()

    def gather_f(half):
        def view(core, start, size):
            return Fd.at[half, at(core * HALF + start, size, 16)]
        return Gather(
            view, lambda start, size: view(c, r1 * QUARTER + start, size),
            (fd_s, fd_r, fe_s, fe_r, ff_s, ff_r),
        )

    def gather_w():
        def view(core, start, size):
            return Wb.at[at(start, size, 16), at(core * 2 * D, 2 * D, 2 * D)]
        return Gather(
            view, lambda start, size: view(c, r1 * QUARTER + start, size),
            (wd_s, wd_r, we_s, we_r, wf_s, wf_r),
        )

    def gather_g(b):
        def view(core, start, size):
            return g.at[b, at(core * HALF + start, size, 16)]
        return Gather(
            view, lambda start, size: q.at[b, at(start, size, 16)],
            (gd_s.at[b], gd_r.at[b], ge_s.at[b], ge_r.at[b], gf_s.at[b], gf_r.at[b]),
        )

    def stage_b(b):
        cp_a(b).wait_recv()
        for j in (2, 1, 3, 0):
            part = at(c * HALF + lax.rem(r1 + j, N) * QUARTER, QUARTER, QUARTER)
            other = at(lax.rem(r1 + j, N) * QUARTER, QUARTER, QUARTER)
            g[b, part] = (g[b, part].astype(F32) + rA[b, other].astype(F32)).astype(BF)
            if j == 2:
                cp_rb(b, 0).start()
                cp_rb(b, 1).start()
            elif j == 1:
                cp_rb(b, 2).start()
            elif j == 3:
                cp_rb(b, 3).start()

    def sum_far(b):
        for j in (0, 1):
            cp_rb(b, j).wait_recv()
            mine = half_of(1 + 2 * j, j)
            arrived = rB[b, 2, j * SIDE:(j + 1) * SIDE].astype(F32)
            g[b, mine] = (g[b, mine].astype(F32) + arrived).astype(BF)
            cp_rb(b, 4 + j).start()

    def sum_quarter(b):
        for j in (2, 3, 4, 5):
            cp_rb(b, j).wait_recv()
        part = at(own_quarter, QUARTER, QUARTER)
        total = g[b, part].astype(F32) + rB[b, 0].astype(F32) + rB[b, 1].astype(F32)
        g[b, part] = total.astype(BF)
        for k in ring:
            cp_rc(b, k).start()

    def sum_piece(b):
        cp_a(b).wait_send()
        pl.semaphore_signal(free_a.at[b], inc=1, device_id=(mate, s), device_id_type=MESH)
        for j in range(6):
            cp_rb(b, j).wait_send()
        for k in (1, 3):
            pl.semaphore_signal(free_b.at[b], inc=1, device_id=(peer1(k), s), device_id_type=MESH)
        for k in ring:
            cp_rc(b, k).wait_recv()
        total = g[b, at(own_piece, PIECE, PIECE)].astype(F32)
        for k in ring:
            total = total + rC[b, k - 1].astype(F32)
        q[b, at(r2 * PIECE, PIECE, PIECE)] = total.astype(BF)
        for k in ring:
            gather_g(b).d(k).start()

    local_w().start()

    @pl.when(s != 0)
    def _():
        local_f().start()

    barrier = pltpu.get_barrier_semaphore()
    partners = [(dp, sec_of(k)) for k in (1, 2, 3)] + [(mate, s)]
    partners += [(peer1(k), s) for k in ring] + [(peer2(k), s) for k in ring]
    for partner in partners:
        pl.semaphore_signal(barrier, inc=1, device_id=partner, device_id_type=MESH)
    select = lax.broadcasted_iota(jnp.int32, (192, D), 1) == lax.broadcasted_iota(jnp.int32, (192, D), 0) + s * 192
    snorm = snorm_ref[0].astype(F32)
    gain = 1.0 + snorm[0:1]
    shift = snorm[1:2]
    inb[...] = jnp.zeros_like(inb)
    inb[0:2] = nn(inorm_ref[...], select.astype(F32).astype(BF))
    inb[2:4] = snorm
    nacc[...] = jnp.zeros_like(nacc)
    pl.semaphore_wait(barrier, len(partners))

    for k in (1, 2, 3):
        cp_in(k).start()

    @pl.when(s == 0)
    def _():
        local_lat().start()
        for i in range(3):
            local_tokens(i).start()

    @pl.when(s != 1)
    def _():
        cp_fx().start()

    @pl.when(s == 3)
    def _():
        cp_wx().start()

    for sec in (1, 2, 3):
        @pl.when(s == sec)
        def _():
            for i in range(3):
                cp_lat(i, sec).start()
                if sec == 2:
                    cp_via(i).start()
                cp_u(i, sec).start()

    @pl.when(s >= 2)
    def _():
        local_cot().start()

    for to in (2, 3):
        @pl.when(s != to)
        def _():
            cp_cot(s, to).start()

    def project(a, lo, hi):
        return nn(a, W[:, lo:hi])

    def latent_back(x_ref, i, da, db):
        dx, dg, dbias = ln_back(x_ref[i].astype(F32), da, gain)
        nacc[0:1] = nacc[0:1] + dg
        nacc[1:2] = nacc[1:2] + dbias
        return db.astype(F32) + dx

    local_w().wait()

    def send_du(i):
        in_gain = 1.0 + inb[0:1] + inr[0, 0:1] + inr[1, 0:1] + inr[2, 0:1]
        at_rows = rows(i, SEQ)
        du = nt(X[3, at_rows], W[:, D:2 * D]) + nt(X[4, at_rows], W[:, 2 * D:3 * D])
        X[1, at_rows] = du.astype(BF)

        @pl.loop(0, 4)
        def _(j):
            part = at(i * SEQ + j * LAT, LAT, LAT)
            dx, dg, dbias = ln_back(X[5, part].astype(F32), X[1, part].astype(F32), in_gain)
            X[5, part] = dx.astype(BF)
            nacc[2:3] = nacc[2:3] + dg
            nacc[3:4] = nacc[3:4] + dbias
        dUb[i] = X[5, at(i * SEQ, LAT, LAT)]
        for t in (1, 2, 3):
            cp_du(i, t).start()

    def plane_0():
        local_lat().wait()
        for k in (1, 2, 3):
            cp_in(k).wait_recv()
        in_all = inb[...] + inr[0] + inr[1] + inr[2]

        @pl.loop(0, 3)
        def _(i):
            for src in (1, 2, 3):
                cp_lat(i, src).wait_recv()
            x = xin[i].astype(F32)
            xhat, _ = unit(x)
            a = (xhat * gain + shift).astype(BF)
            lat_rows = rows(i, LAT)
            A[lat_rows] = a
            Q[lat_rows] = project(a, 0, D).astype(BF)
            for src in (1, 2, 3):
                cp_u(i, src).wait_recv()
            cp_on(i).wait_recv()
            local_tokens(i).wait()

            @pl.loop(0, 4)
            def _(j):
                part = at(i * SEQ + j * LAT, LAT, LAT)
                xhat, _ = unit(X[5, part].astype(F32))
                X[0, part] = (xhat * (1.0 + in_all[0:1]) + in_all[1:2]).astype(BF)
            u = X[0, rows(i, SEQ)]
            kv = [X.at[j, rows(i, SEQ)] for j in (1, 2)]
            kv[0][...] = project(u, D, 2 * D).astype(BF)
            kv[1][...] = project(u, 2 * D, 3 * D).astype(BF)
            where_ = lax.broadcasted_iota(jnp.int32, (SEQ, 256), 0)
            clip = jnp.zeros((SEQ, 256), jnp.int32)
            end = jnp.int32(0)
            for j in range(4):
                end = end + len_ref[i, j]
                clip = clip + (where_ >= end).astype(jnp.int32)
            ids = clip_ref[pl.ds(i, 1)]
            ids = jnp.concatenate([ids, ids], 1)
            attn_fwd(Q.at[lat_rows], kv[0], kv[1], clip == ids, PT.at[i], O.at[lat_rows])
            b = x + project(O[lat_rows], 3 * D, 4 * D)
            sendB[i] = b.astype(BF)
            cp_b(i, sendB).start()

        def latent_out(i):
            db = dBin[i]
            grad = latent_back(xin, i, nt(dQ[rows(i, LAT)], W[:, :D]), db).astype(BF)
            sendD[i] = grad
            lgb[i] = grad[0:32]
            for t in (1, 2, 3):
                cp_lg(i, t).start()

        def item_back(i):
            cp_d(i).wait_recv()
            dO[...] = nt(dBin[i], W[:, 3 * D:]).astype(BF)
            kv = [X.at[j, rows(i, SEQ)] for j in (1, 2, 3, 4)]
            lat_rows = rows(i, LAT)
            attn_bwd(Q.at[lat_rows], kv[0], kv[1], PT.at[i], dO, dQ.at[lat_rows], kv[2], kv[3])

        def weight_grads(tokens, latents, add):
            def put(b, rows_, grad):
                g[b, rows_] = ((g[b, rows_].astype(F32) + grad) if add else grad).astype(BF)
            count = latents.stop - latents.start
            db = dBin[latents.start // LAT:latents.stop // LAT].reshape(count, D)
            put(0, slice(0, D), tn(A[latents], dQ[latents]))
            put(1, slice(D, 2 * D), tn(O[latents], db))

            @pl.loop(0, 2)
            def _(b):
                put(b, at((1 - b) * D, D, D), tn(X[0, tokens], X[3 + b, tokens]))
                if add:
                    cp_a(b).start()

        @pl.loop(0, 3)
        def _(i):
            @pl.when(i == 2)
            def _():
                for t in range(3):
                    cp_e(t).wait_recv()
                    for blk in range(2):
                        cp_gu(t, blk).wait_recv()

                @pl.loop(0, 2)
                def _(blk):
                    g[2, at(blk * D, D, D)] = tn(Fd[0, at(blk * 384, 384, 384)], Fd[1, 0:384]).astype(BF)
                cp_a(2).start()
                weight_grads(slice(0, 2 * SEQ), slice(0, 2 * LAT), False)
                apart(stage_b, 2)
            item_back(i)

            @pl.when(i < 2)
            def _():
                latent_out(i)
        weight_grads(slice(2 * SEQ, 3 * SEQ), slice(2 * LAT, 3 * LAT), True)
        pl.loop(2, 2 + once)(latent_out)

    def plane_2():
        for k in (1, 2, 3):
            cp_in(k).wait_recv()
        far_gain = 1.0 + inr[2, 2:3]
        far_shift = inr[2, 3:4]
        w3, f3 = gather_w(), gather_f(1)
        cp_fx().wait_recv()
        cp_wx().wait_recv()
        for k in ring:
            w3.d(k).start()
            f3.d(k).start()
        for one in (w3, f3):
            for k in ring:
                one.d_in(k).wait_recv()
            one.e1()
        for one in (w3, f3):
            one.e2()
        for one in (w3, f3):
            one.e_done()
            one.f().start()
        local_f().wait()
        local_cot().wait()
        for src in (0, 1, 3):
            cp_cot(src, 2).wait_recv()
        for one in (w3, f3):
            one.f_in().wait_recv()

        @pl.loop(0, 3)
        def _(i):
            lat_rows = rows(i, LAT)
            cp_b(i, yin).wait_recv()
            x = xin[i].astype(F32)
            xhat, _ = unit(x)
            a = (xhat * gain + shift).astype(BF)
            A[lat_rows] = a
            Q[lat_rows] = project(a, 0, D).astype(BF)
            X[1, lat_rows] = project(a, D, 2 * D).astype(BF)
            X[2, lat_rows] = project(a, 2 * D, 3 * D).astype(BF)
            ids = jnp.broadcast_to(clip_ref[pl.ds(i, 1)].astype(F32), (LAT, LAT))
            mask = jnp.concatenate([ids, ids], 1) == jnp.concatenate([ids.T, ids.T], 1)
            attn_fwd(
                Q.at[lat_rows], X.at[1, lat_rows], X.at[2, lat_rows], mask,
                PT.at[i, :, 0:LAT], O.at[lat_rows],
            )
            middle = (x + project(O[lat_rows], 3 * D, 4 * D)).astype(BF)
            yin[i] = middle
            cp_b(i, yin).start()
            x = middle.astype(F32)
            xhat, _ = unit(x)
            a = (xhat * far_gain + far_shift).astype(BF)
            b = ffn_fwd(i, x, a, Wb, Fd, X, 2).astype(BF)
            sendB[i] = b
            outb[i] = b[64:96]
            for t in (0, 1, 3):
                cp_o(i, t).start()
            db = dBin[i]
            dx, _, _ = ln_back(x, ffn_bwd(i, db, Wb, Fd, X, False), far_gain)
            db = (db.astype(F32) + dx).astype(BF)
            dBm[i] = db
            dO[...] = nt(db, W[:, 3 * D:]).astype(BF)
            attn_bwd(
                Q.at[lat_rows], X.at[1, lat_rows], X.at[2, lat_rows], PT.at[i, :, 0:LAT],
                dO, dQ.at[lat_rows], X.at[3, lat_rows], X.at[4, lat_rows],
            )
            da = nt(dQ[lat_rows], W[:, :D]) + nt(X[3, lat_rows], W[:, D:2 * D])
            da = da + nt(X[4, lat_rows], W[:, 2 * D:3 * D])
            sendD[i] = latent_back(xin, i, da, db).astype(BF)
            cp_d(i).start()
            cp_e(i).start()

        def all_grads(b):
            if b == 2:
                db = dBin[...].reshape(3 * LAT, D)
                pair = tn(X[0, 0:384], db), tn(X[0, 384:768], db)
            elif b == 0:
                pair = tn(A[...], dQ[...]), tn(A[...], X[3, 0:3 * LAT])
            else:
                pair = tn(A[...], X[4, 0:3 * LAT]), tn(O[...], dBm[...].reshape(3 * LAT, D))
            g[b, 0:D] = pair[0].astype(BF)
            g[b, D:] = pair[1].astype(BF)

        for b in ORDER:
            apart(all_grads, b)
            cp_a(b).start()

    def plane_odd():
        def relay_on(i):
            @pl.when(s == 1)
            def _():
                cp_via(i).wait_recv()
                cp_on(i).start()

        prior = gather_f(0)
        relay_on(0)
        cp_fx().wait_recv()
        for k in ring:
            prior.d(k).start()
        relay_on(1)
        for k in ring:
            prior.d_in(k).wait_recv()
        prior.e1()
        relay_on(2)
        prior.e2()
        prior.e_done()
        prior.f().start()
        local_f().wait()
        prior.f_in().wait_recv()

        @pl.when(s == 3)
        def _():
            local_cot().wait()
            for src in (0, 1, 2):
                cp_cot(src, 3).wait_recv()

        def store_grads(b, first, count, add):
            own = slice(first * LAT, (first + count) * LAT)

            @pl.loop(0, 2)
            def _(j):
                block = (2 if b == 2 else 2 * b) + j
                units = at(block * 384 + first * LAT, count * LAT, LAT)
                if b == 2:
                    grad = tn(X[0, units], dBin[first:first + count].reshape(count * LAT, D))
                else:
                    grad = tn(A[own], X[1, units])
                here = at(j * D, D, D)
                g[b, here] = ((g[b, here].astype(F32) + grad) if add else grad).astype(BF)

        def forward(i):
            cp_b(i, sendB).wait_recv()
            x = xin[i].astype(F32)
            xhat, _ = unit(x)
            a = (xhat * gain + shift).astype(BF)
            A[rows(i, LAT)] = a
            return ffn_fwd(i, x, a, W, Fd, X, 4).astype(BF)

        def backward(i):
            db = dBin[i]
            return latent_back(xin, i, ffn_bwd(i, db, W, Fd, X, True), db).astype(BF)

        @pl.loop(0, 6)
        def _(step):
            last = s == 3
            ahead = jnp.where(last, lax.rem(step, 2) == 0, step < 3)
            i = jnp.where(last, step // 2, lax.rem(step, 3))

            @pl.when(ahead)
            def _():
                sendB[i] = forward(i)

                @pl.when(s == 1)
                def _():
                    cp_b(i, sendB).start()
                    for blk in range(2):
                        cp_gu(i, blk).start()

            @pl.when(jnp.logical_not(ahead))
            def _():
                @pl.when((s == 1) & (i == 2))
                def _():
                    for b in ORDER:
                        store_grads(b, 0, 2, False)

                @pl.when(s == 1)
                def _():
                    cp_d(i).wait_recv()
                sendD[i] = backward(i)

                @pl.when(s == 1)
                def _():
                    cp_d(i).start()

        for b in ORDER:
            @pl.when(s == 1)
            def _():
                store_grads(b, 2, 1, True)

            @pl.when(s == 3)
            def _():
                store_grads(b, 0, 3, False)
            cp_a(b).start()

    def spread_quarter(b):
        for k in ring:
            cp_rc(b, k).wait_send()
        pl.semaphore_wait(free_b.at[b], 2)
        for k in ring:
            gather_g(b).d_in(k).wait_recv()
        gather_g(b).e1()
        g[b, at(own_quarter, QUARTER, QUARTER)] = q[b]

    def spread_far(b):
        gather_g(b).e2()

    def leave(b, h, act):
        src = g.at[b, at(h * HALF, HALF, HALF)]

        @pl.when(b == 2)
        def _():
            act(pltpu.make_async_copy(src, down_ref.at[0, at(h * HALF, HALF, HALF)], g_sem.at[b, h]))

        @pl.when(b < 2)
        def _():
            block = at(jnp.minimum(2 * b + h, 3) * D, D, D)
            act(pltpu.make_async_copy(src, entry_ref.at[0, :, block], g_sem.at[b, h]))

    def spread_half(b):
        gather_g(b).e_done()
        pl.semaphore_wait(free_a.at[b], 1)
        gather_g(b).f().start()
        leave(b, c, lambda copy: copy.start())

    def finish(b):
        gather_g(b).f_in().wait_recv()
        leave(b, 1 - c, lambda copy: copy.start())

    def small(step, buf, ss, rs, k, dp_to, sec_to):
        return remote(tsrc.at[step], buf.at[k], ss.at[k], rs.at[k], dp_to, sec_to)

    def own_rows():
        @pl.when(odd)
        def _():
            for k in (1, 2, 3):
                cp_in(k).wait_recv()

        @pl.loop(0, 3)
        def _(i):
            @pl.when(s != 2)
            def _():
                cp_o(i, 0).wait_recv()

            @pl.when(s != 0)
            def _():
                cp_lg(i, 1).wait_recv()
                cp_du(i, 1).wait_recv()
            igrad_ref[i] = dUb[i]
            out_ref[i] = outb[i]
            lgrad_ref[i] = lgb[i]

    def small_x(k):
        return remote(tsrc.at[0], tX.at[0], tx_s.at[k - 1], tx_r.at[0], dp, sec_of(k))

    def small_mate():
        tsrc[1] = nacc[...]
        small(1, tC, tc_s, tc_r, 0, mate, s).start()

    def small_ring1():
        small(1, tC, tc_s, tc_r, 0, mate, s).wait_recv()
        tsrc[2] = tsrc[1] + tC[0]
        for k in ring:
            small(2, t1, t1_s, t1_r, k - 1, peer1(k), s).start()

    def small_ring2():
        for k in ring:
            small(2, t1, t1_s, t1_r, k - 1, peer1(k), s).wait_recv()
        tsrc[3] = tsrc[2] + t1[0] + t1[1] + t1[2]
        for k in ring:
            small(3, t2, t2_s, t2_r, k - 1, peer2(k), s).start()

    def small_out(sec):
        for k in ring:
            small(3, t2, t2_s, t2_r, k - 1, peer2(k), s).wait_recv()
        total = tsrc[3] + t2[0] + t2[1] + t2[2]
        tsrc[0] = total
        tiny_ref[...] = total

        if sec == 0:
            for k in (1, 2, 3):
                small_x(k).start()

    def small_done():
        @pl.when(s != 0)
        def _():
            small_x(1).wait_recv()
            tiny_ref[2:4] = tX[0, 2:4]

    def sums(sec):
        stages = (
            stage_b, sum_far, sum_quarter, sum_piece, spread_quarter, spread_far, spread_half, finish
        )

        @pl.loop(0, len(stages) + 2)
        def _(turn):
            for k, stage in enumerate(stages):
                t = turn - k
                due = (t >= 0) & (t < 3)
                if k == 0 and sec == 0:
                    due = due & (t > 0)
                pl.when(due)(functools.partial(stage, lax.rem(t + 2, 3)))

            if sec == 0:
                pl.when((turn > 0) & (turn < 4))(functools.partial(send_du, turn - 1))
            for k, step in ((4, small_mate), (5, small_ring1), (6, small_ring2), (8, functools.partial(small_out, sec))):
                pl.when(turn == k)(step)

        @pl.loop(0, 3)
        def _(b):
            for h in range(2):
                leave(b, h, lambda copy: copy.wait())

    def drain(sec):
        for k in (1, 2, 3):
            cp_in(k).wait_send()
        small(1, tC, tc_s, tc_r, 0, mate, s).wait_send()
        for k in ring:
            small(2, t1, t1_s, t1_r, k - 1, peer1(k), s).wait_send()
            small(3, t2, t2_s, t2_r, k - 1, peer2(k), s).wait_send()
        pl.loop(0, 3)(lambda b: gather_g(b).drain())
        for to in (2, 3):
            if sec != to:
                cp_cot(sec, to).wait_send()
        if sec != 1:
            cp_fx().wait_send()
        if sec == 3:
            cp_wx().wait_send()
        if sec == 2:
            gather_w().drain()
            gather_f(1).drain()
        if sec in (1, 3):
            gather_f(0).drain()
        for i in range(3):
            if sec > 0:
                cp_lat(i, sec).wait_send()
                cp_u(i, sec).wait_send()
            if sec < 3:
                cp_b(i, sendB).wait_send()
            if sec in (1, 2):
                cp_via(i).wait_send()
                cp_d(i).wait_send()
            if sec == 0 and i == 0:
                for k in (1, 2, 3):
                    small_x(k).wait_send()
            if sec == 0:
                for t in (1, 2, 3):
                    cp_lg(i, t).wait_send()
                    cp_du(i, t).wait_send()
            if sec == 1:
                for blk in range(2):
                    cp_gu(i, blk).wait_send()
            if sec == 2:
                cp_e(i).wait_send()
                for t in (0, 1, 3):
                    cp_o(i, t).wait_send()

    @pl.when(s == 2)
    def _():
        plane_2()
        sums(2)
        drain(2)

    @pl.when(odd)
    def _():
        plane_odd()
        sums(1)
        for sec in (1, 3):
            pl.when(s == sec)(functools.partial(drain, sec))

    @pl.when(s == 0)
    def _():
        plane_0()
        sums(0)
        drain(0)

    own_rows()
    small_done()


def widen(
    out_in, lgrad_in, igrad_in, entry_in, down_in, tiny_in,
    out_ref, lgrad_ref, igrad_ref, entry_ref, down_ref, norm_ref, in_norm_ref,
):
    igrad_ref[...] = igrad_in[...].astype(F32)
    entry_ref[...] = entry_in[...].astype(F32)
    down_ref[...] = down_in[...].astype(F32)

    @pl.when(pl.program_id(0) == 0)
    def _():
        out_ref[...] = out_in[...]
        lgrad_ref[...] = lgrad_in[...].astype(F32)
        norm_ref[...] = tiny_in[0:2]
        s = lax.axis_index("section")
        mine = jnp.zeros((2, 192), F32)
        for k in range(4):
            mine = jnp.where(s == k, tiny_in[2:4, k * 192:(k + 1) * 192], mine)
        in_norm_ref[...] = mine


def on_device(lat, raw, cot, lengths, clip, w, f, snorm, inorm):
    def low(*shape):
        return pltpu.VMEM(shape, BF)

    def full(*shape):
        return pltpu.VMEM(shape, F32)

    def sem(*shape):
        return pltpu.SemaphoreType.DMA(shape)

    def pair(*shape):
        return [sem(*shape), sem(*shape)]

    one = pltpu.SemaphoreType.DMA
    ring = N - 1
    scratch = [
        low(D, 4 * D), low(D, 4 * D), low(2, 2 * D, D), low(3, 2 * D, D), low(6, 2 * D, D),
        low(3, 6, SEQ, 256), low(3, HALF, D), low(3, 3, QUARTER, D), low(3, ring, PIECE, D), low(3, QUARTER, D),
        *[low(3, LAT, D)] * 6,
        *[low(3 * LAT, D)] * 4, low(LAT, D),
        low(3, VIA, D), low(3, LAT, D), low(3, 32, D), low(3, 32, D),
        full(8, D), full(3, 8, D), full(8, D), full(4, 8, D),
        full(3, 8, D), full(1, 8, D), full(ring, 8, D), full(ring, 8, D),
        sem(8), *pair(3), sem(3), sem(3, 3), sem(2), sem(4), sem(3), sem(3, 4), *pair(3), one, one, one, one,
        *pair(3), *pair(3), *pair(3), *pair(3, 2), sem(3, 4), sem(3), sem(3, 3), sem(3), sem(3, 3), sem(3),
        *pair(3), *pair(3, 6), *pair(3, ring), *pair(3, ring), *pair(3, 4), *pair(3),
        *pair(ring), *pair(4), one, one, *pair(ring), *pair(4), one, one,
        *pair(3), *pair(1), *pair(ring), *pair(ring), sem(3, 2),
        pltpu.SemaphoreType.REGULAR((3,)), pltpu.SemaphoreType.REGULAR((3,)),
    ]
    hbm = pl.BlockSpec(memory_space=pl.ANY)
    vmem = pl.BlockSpec(memory_space=pltpu.VMEM)
    inner = pl.pallas_call(
        kernel,
        name="layers",
        out_shape=(
            jax.ShapeDtypeStruct(lat.shape, BF),
            jax.ShapeDtypeStruct(lat.shape, BF),
            jax.ShapeDtypeStruct(raw.shape, BF),
            jax.ShapeDtypeStruct(w.shape, BF),
            jax.ShapeDtypeStruct(f.shape, BF),
            jax.ShapeDtypeStruct((8, D), F32),
        ),
        in_specs=[hbm, hbm, hbm, pl.BlockSpec(memory_space=pltpu.SMEM), vmem, hbm, hbm, vmem, vmem],
        out_specs=(vmem, vmem, vmem, hbm, hbm, vmem),
        scratch_shapes=scratch,
        compiler_params=pltpu.CompilerParams(
            collective_id=0, has_side_effects=True, vmem_limit_bytes=60 * 2**20
        ),
    )(lat, raw, cot, lengths, clip, w, f, snorm, inorm)
    steps = 3

    def by_rows(array):
        rest = array.shape[1:]
        return pl.BlockSpec((array.shape[0] // steps, *rest), lambda t: (t,) + (0,) * len(rest))

    def whole(*shape):
        return pl.BlockSpec(shape, lambda t: (0,) * len(shape))

    out, lgrad, igrad, entry, down, tiny = inner
    igrad = igrad.reshape(3 * LAT, D)
    entry, down = entry[0], down[0]
    final = pl.pallas_call(
        widen,
        name="widen",
        grid=(steps,),
        out_shape=(
            jax.ShapeDtypeStruct(lat.shape, BF),
            jax.ShapeDtypeStruct(lat.shape, F32),
            jax.ShapeDtypeStruct(igrad.shape, F32),
            jax.ShapeDtypeStruct(entry.shape, F32),
            jax.ShapeDtypeStruct(down.shape, F32),
            jax.ShapeDtypeStruct((2, D), F32),
            jax.ShapeDtypeStruct((2, 192), F32),
        ),
        in_specs=[
            whole(*lat.shape), whole(*lat.shape), by_rows(igrad), by_rows(entry), by_rows(down), whole(8, D)
        ],
        out_specs=(
            whole(*lat.shape), whole(*lat.shape), by_rows(igrad), by_rows(entry), by_rows(down),
            whole(2, D), whole(2, 192),
        ),
        compiler_params=pltpu.CompilerParams(vmem_limit_bytes=60 * 2**20),
    )(out, lgrad, igrad, entry, down, tiny)
    out, lgrad, igrad, entry, down, norm, in_norm = final
    return out, lgrad, igrad.reshape(raw.shape), entry[None], down[None], norm[None], in_norm


def solution(mesh):
    rows_split = P("dp", "section", None)
    weight = P("section", None, None)
    return jax.shard_map(
        on_device,
        mesh=mesh,
        in_specs=(
            rows_split, rows_split, rows_split, P("dp", None), P("dp", None),
            weight, weight, weight, P(None, "section"),
        ),
        out_specs=(rows_split, rows_split, rows_split, weight, weight, weight, P(None, "section")),
        check_vma=False,
    )
```
